32 devices in a mesh: ctx: 8 (over y, x, core), fsdp: 4 (over z).
Axes of the slice: x: 2, y: 2, z: 4, core: 2. Of those that a mesh axis runs over, the one named last changes fastest.
Arguments:
- inputs: bfloat16 [4, 1024, 768], P('fsdp', 'ctx'), may hold values from -6 to 6
- segments: int32 [4, 1024], P('fsdp', 'ctx'), may hold values from 0 to 1, as said below
- query_weight: bfloat16 [768, 768], P('fsdp'), may hold values from -0.21875 to 0.21875
- query_bias: bfloat16 [768], P('fsdp'), may hold values from -1.75 to 1.75
- key_weight: bfloat16 [768, 768], P('fsdp'), may hold values from -0.21875 to 0.21875
- value_weight: bfloat16 [768, 768], P('fsdp'), may hold values from -0.21875 to 0.21875
- value_bias: bfloat16 [768], P('fsdp'), may hold values from -0.125 to 0.125
- output_weight: bfloat16 [768, 768], P('fsdp'), may hold values from -3.5 to 3.5
- output_bias: bfloat16 [768], P('fsdp'), may hold values from -1.75 to 1.75
- first_gain: bfloat16 [768], P('fsdp'), may hold values from 0.099609375 to 1.8984375
- first_shift: bfloat16 [768], P('fsdp'), may hold values from -1.75 to 1.75
- inner_weight: bfloat16 [768, 3072], P('fsdp'), may hold values from -0.21875 to 0.21875
- inner_bias: bfloat16 [3072], P('fsdp'), may hold values from -1.75 to 1.75
- outer_weight: bfloat16 [3072, 768], P('fsdp'), may hold values from -0.109375 to 0.109375
- outer_bias: bfloat16 [768], P('fsdp'), may hold values from -1.75 to 1.75
- second_gain: bfloat16 [768], P('fsdp'), may hold values from 0.099609375 to 1.8984375
- second_shift: bfloat16 [768], P('fsdp'), may hold values from -1.75 to 1.75
- cotangent: bfloat16 [4, 1024, 768], P('fsdp', 'ctx'), may hold values from -8 to 8
Outputs:
- output: bfloat16 [4, 1024, 768], P('fsdp', 'ctx')
- grad_input: bfloat16 [4, 1024, 768], P('fsdp', 'ctx')
- grad_query_weight: float32 [768, 768], P('fsdp')
- grad_query_bias: float32 [768], P('fsdp')
- grad_key_weight: float32 [768, 768], P('fsdp')
- grad_value_weight: float32 [768, 768], P('fsdp')
- grad_value_bias: float32 [768], P('fsdp')
- grad_output_weight: float32 [768, 768], P('fsdp')
- grad_output_bias: float32 [768], P('fsdp')
- grad_first_gain: float32 [768], P('fsdp')
- grad_first_shift: float32 [768], P('fsdp')
- grad_inner_weight: float32 [768, 3072], P('fsdp')
- grad_inner_bias: float32 [3072], P('fsdp')
- grad_outer_weight: float32 [3072, 768], P('fsdp')
- grad_outer_bias: float32 [768], P('fsdp')
- grad_second_gain: float32 [768], P('fsdp')
- grad_second_shift: float32 [768], P('fsdp')
The draws below stay inside these ranges and needn't reach their ends.
Inputs may be any that keep to these rules, and one draw needn't show every extreme that they name: `segments`: position p of a sequence is stored at entry (p mod R) * 128 + p div R, with R = 8. Taken in order of position, document numbers never fall and step by one; each document holds roughly a quarter to seven quarters of 512 positions.
All inputs are finite; a program needn't handle non-finite values.
Results may differ from the reference program's by a relative error of at most 0.02.
Values may be sent and summed in bfloat16 or wider, within the bound.
No kernel may reach another device: no remote copies, remote signals or barrier semaphores. Data moves between devices by JAX's collectives and lax.ppermute only.
A program may use at most 128 MiB of HBM per device.

```python
import jax
import jax.numpy as jnp
from jax import lax

D = 768
HEADS = 12
HEAD_DIM = 64
FF = 3072
TOK_DEV = 128
SEQ_LEN = 1024
DOCS = 2
SEQS = 4


def draw_segments(key, part):
    length = SEQ_LEN
    rank_count = SEQ_LEN // TOK_DEV
    spacing = SEQ_LEN // DOCS
    jitter_span = 3 * spacing // 8
    jitter = jax.random.randint(key, (SEQS, DOCS - 1), -jitter_span, jitter_span + 1, dtype=jnp.int32)
    cut_points = (jnp.arange(1, DOCS, dtype=jnp.int32) * spacing)[None, :] + jitter
    stored = jnp.arange(length, dtype=jnp.int32)
    position = stored % TOK_DEV * rank_count + stored // TOK_DEV
    return jnp.sum((position[None, :, None] >= cut_points[:, None, :]).astype(jnp.int32), -1)


def strengthened(values, own_key, source, target, blocks, factor):
    def block_of(axis_at):
        return (jnp.arange(values.shape[axis_at]) // (values.shape[axis_at] // blocks)).reshape((-1,) + (1,) * (values.ndim - 1 - axis_at))

    first = jax.random.permutation(own_key, blocks)[block_of(target)]
    far = (block_of(target) + blocks // 2) % blocks
    return jnp.where((block_of(source) == first) | (block_of(source) == far), factor * values, values)


def levels(stream_key, dims, cuts, low, largest):
    gain = 1.0
    for dim, shards_of in cuts:
        steps = jax.random.uniform(jax.random.fold_in(jax.random.fold_in(stream_key, 6), dim), (shards_of,), jnp.float32, low / len(cuts), largest / len(cuts))
        gain = gain * jnp.repeat(jnp.exp(steps), dims[dim] // shards_of).reshape((-1,) + (1,) * (len(dims) - 1 - dim))
    return gain


def normal_values(stream_key, dims, scale, reach, shards=(), held_as=jnp.bfloat16):
    loudness = levels(stream_key, dims, shards, -0.22, 0.18) if shards else 1.0
    array = jax.random.normal(stream_key, dims, jnp.float32) * scale * loudness
    return jnp.minimum(jnp.maximum(array, -reach), reach).astype(held_as)


def heavy_noise(rng, extent, scale, reach, cuts, heavy, kind=jnp.bfloat16):
    array = scale * jax.random.normal(rng, extent, jnp.float32)
    if cuts:
        array = array * levels(rng, extent, cuts, -0.22, 0.18)
    return jnp.clip(strengthened(array, jax.random.fold_in(rng, 3), *heavy), -reach, reach).astype(kind)


def setup_inputs(seed: int = 0) -> dict:
    keys = jax.random.split(jax.random.key(seed), 19)
    inputs = normal_values(keys[0], (SEQS, SEQ_LEN, D), 1.0, 6.0, ((0, 4), (1, 8)))
    segments = draw_segments(jax.random.fold_in(keys[18], 71), 0)
    query_weight = normal_values(keys[2], (D, D), D ** -0.5, 0.21875, ((0, 4),))
    query_bias = normal_values(keys[3], (D,), 0.3, 1.75, ((0, 4),))
    key_weight = normal_values(keys[4], (D, D), D ** -0.5, 0.21875, ((0, 4),))
    value_weight = normal_values(keys[5], (D, D), D ** -0.5, 0.21875, ((0, 4),))
    value_bias = normal_values(keys[6], (D,), 0.02, 0.125, ((0, 4),))
    output_weight = normal_values(keys[7], (D, D), (D // 256) ** -0.5, 3.5, ((0, 4),))
    output_bias = normal_values(keys[8], (D,), 0.3, 1.75, ((0, 4),))
    first_gain = jnp.clip(1.0 + 0.18 * jax.random.normal(keys[9], (D,), jnp.float32), 0.099609375, 1.8984375).astype(jnp.bfloat16)
    first_shift = normal_values(keys[10], (D,), 0.3, 1.75, ((0, 4),))
    inner_weight = normal_values(keys[11], (D, FF), D ** -0.5, 0.21875, ((0, 4),))
    inner_bias = normal_values(keys[12], (FF,), 0.3, 1.75, ((0, 4),))
    outer_weight = normal_values(keys[13], (FF, D), FF ** -0.5, 0.109375, ((0, 4),))
    outer_bias = normal_values(keys[14], (D,), 0.3, 1.75, ((0, 4),))
    second_gain = jnp.clip(1.0 + 0.18 * jax.random.normal(keys[15], (D,), jnp.float32), 0.099609375, 1.8984375).astype(jnp.bfloat16)
    second_shift = normal_values(keys[16], (D,), 0.3, 1.75, ((0, 4),))
    cotangent = heavy_noise(keys[17], (SEQS, SEQ_LEN, D), 1.0, 8.0, ((0, 4), (1, 8)), (1, 2, 8, 2.0))
    return dict(inputs=inputs, segments=segments, query_weight=query_weight, query_bias=query_bias, key_weight=key_weight, value_weight=value_weight, value_bias=value_bias, output_weight=output_weight, output_bias=output_bias, first_gain=first_gain, first_shift=first_shift, inner_weight=inner_weight, inner_bias=inner_bias, outer_weight=outer_weight, outer_bias=outer_bias, second_gain=second_gain, second_shift=second_shift, cotangent=cotangent)


NEGATIVE = -1000000000.0
EPSILON = 1e-12

@jax.custom_vjp
def low(v):
    return lax.optimization_barrier(v.astype(jnp.bfloat16)).astype(jnp.float32)

@jax.custom_vjp
def low_back(v):
    return v

def low_keep(v):
    return (low(v), None)

def low_pass(kept, grad):
    return (grad,)

def back_keep(v):
    return (v, None)

def back_low(kept, grad):
    return (low(grad),)
low.defvjp(low_keep, low_pass)
low_back.defvjp(back_keep, back_low)

def matmul(leading, trailing):
    return jnp.dot(leading, trailing, precision=lax.Precision.HIGHEST, preferred_element_type=jnp.float32)

def layer_norm(values, norm_gain, norm_shift):
    center = values - lax.optimization_barrier(jnp.mean(values, -1, keepdims=True))
    spread = lax.optimization_barrier(jnp.mean(center * center, -1, keepdims=True))
    return center * lax.rsqrt(spread + EPSILON) * norm_gain + norm_shift

def attend_sequence(queries, key_rows, values, segment_row):
    length = queries.shape[0]
    block_rows = min(512, length)
    head_scale = HEAD_DIM ** (-0.5)

    def one_block(block_index):
        offset = block_index * block_rows
        query_block = lax.dynamic_slice_in_dim(queries, offset, block_rows, 0)
        query_segment = lax.dynamic_slice_in_dim(segment_row, offset, block_rows, 0)
        scores = jnp.einsum('qhe,khe->hqk', query_block, key_rows, precision=lax.Precision.HIGHEST) * head_scale
        scores = low_back(scores)
        allowed = (query_segment[:, None] == segment_row[None, :])[None]
        scores = jnp.where(allowed, scores, NEGATIVE)
        soft_scores = low(jax.nn.softmax(scores, axis=-1))
        return jnp.einsum('hqk,khe->qhe', soft_scores, values, precision=lax.Precision.HIGHEST)
    blocks = lax.map(jax.checkpoint(one_block), jnp.arange(length // block_rows, dtype=jnp.int32))
    return blocks.reshape(length, HEADS * HEAD_DIM)

def forward(inputs, segments, query_weight, query_bias, key_weight, value_weight, value_bias, output_weight, output_bias, first_gain, first_shift, inner_weight, inner_bias, outer_weight, outer_bias, second_gain, second_shift):
    flat = inputs.reshape(-1, D)
    per_head = (SEQS, SEQ_LEN, HEADS, HEAD_DIM)
    queries = low(low_back(matmul(flat, query_weight) + query_bias)).reshape(per_head)
    key_rows = low(low_back(matmul(flat, key_weight))).reshape(per_head)
    values = low(low_back(matmul(flat, value_weight) + value_bias)).reshape(per_head)

    def per_sequence(members):
        return attend_sequence(members[0], members[1], members[2], members[3])
    context = lax.map(per_sequence, (queries, key_rows, values, segments)).reshape(-1, D)
    context = low(low_back(context))
    branch = low_back(matmul(context, output_weight) + output_bias)
    normed_one = layer_norm(flat + branch, first_gain, first_shift)
    inner_pre = low_back(matmul(low(normed_one), inner_weight) + inner_bias)
    activated = low(jax.nn.gelu(inner_pre, approximate=False))
    outer = low_back(matmul(activated, outer_weight) + outer_bias)
    return layer_norm(normed_one + outer, second_gain, second_shift).reshape(SEQS, SEQ_LEN, D)

def reference(inputs, segments, query_weight, query_bias, key_weight, value_weight, value_bias, output_weight, output_bias, first_gain, first_shift, inner_weight, inner_bias, outer_weight, outer_bias, second_gain, second_shift, cotangent):
    weights = (query_weight.astype(jnp.float32), query_bias.astype(jnp.float32), key_weight.astype(jnp.float32), value_weight.astype(jnp.float32), value_bias.astype(jnp.float32), output_weight.astype(jnp.float32), output_bias.astype(jnp.float32), first_gain.astype(jnp.float32), first_shift.astype(jnp.float32), inner_weight.astype(jnp.float32), inner_bias.astype(jnp.float32), outer_weight.astype(jnp.float32), outer_bias.astype(jnp.float32), second_gain.astype(jnp.float32), second_shift.astype(jnp.float32))

    def wrapped(tokens, *params):
        return forward(tokens, segments, *params)
    result, pullback = jax.vjp(wrapped, inputs.astype(jnp.float32), *weights)
    gradients = pullback(cotangent.astype(jnp.float32))
    return (result.astype(jnp.bfloat16), gradients[0].astype(jnp.bfloat16), gradients[1], gradients[2], gradients[3], gradients[4], gradients[5], gradients[6], gradients[7], gradients[8], gradients[9], gradients[10], gradients[11], gradients[12], gradients[13], gradients[14], gradients[15])
```

```python
import functools

import jax
import jax.numpy as jnp
from jax import lax
from jax.experimental import pallas as pl
from jax.experimental.pallas import tpu as pltpu
from jax.sharding import PartitionSpec as P

HEAD_DIM = 64
NEGATIVE = -1000000000.0
EPSILON = 1e-12
LOW = jnp.bfloat16
WIDE = jnp.float32

CORE, SIDE, ROW = 1, 2, 4
TEAM = 8
CHIPS = 4
VMEM_BYTES = 56 << 20


def partner(block, axis, bit):
    devices = range(lax.axis_size(axis))
    return lax.ppermute(block, axis, [(i, i ^ bit) for i in devices])


def dot(left, right):
    return jnp.dot(left, right, preferred_element_type=WIDE)


def dot_rt(left, right):
    return lax.dot_general(left, right, (((1,), (1,)), ((), ())), preferred_element_type=WIDE)


def dot_lt(left, right):
    return lax.dot_general(left, right, (((0,), (0,)), ((), ())), preferred_element_type=WIDE)


def shape(dims, dtype=LOW):
    return jax.ShapeDtypeStruct(tuple(dims), dtype)


def kernel(body, outs, *args, scratch=(), flops=0):
    spec = pl.BlockSpec(memory_space=pltpu.VMEM)
    nbytes = sum(a.size * a.dtype.itemsize for a in args)
    nbytes += sum(functools.reduce(lambda m, n: m * n, o.shape, 1) * o.dtype.itemsize for o in outs)
    return pl.pallas_call(
        body,
        out_shape=list(outs),
        in_specs=[pl.BlockSpec(memory_space=pltpu.SMEM)] + [spec] * (len(args) - 1),
        out_specs=[spec] * len(outs),
        scratch_shapes=list(scratch),
        compiler_params=pltpu.CompilerParams(vmem_limit_bytes=VMEM_BYTES),
        cost_estimate=pl.CostEstimate(
            flops=int(flops), bytes_accessed=int(nbytes), transcendentals=0
        ),
    )(*args)


def places(where):
    index, place = where[0], where[1]
    core, side, row = index & 1, (index >> 1) & 1, (index >> 2) & 1
    return core, side, row, (index >> 1) & 3, place


def rows_from(start, count):
    return pl.ds(pl.multiple_of(start, 16), count)


def normalized(values):
    center = values - jnp.mean(values, -1, keepdims=True)
    inverse = lax.rsqrt(jnp.mean(center * center, -1, keepdims=True) + EPSILON)
    return center * inverse, inverse


def norm_back(grad, unit, inverse, gain):
    scaled = grad * gain
    return inverse * (
        scaled
        - jnp.mean(scaled, -1, keepdims=True)
        - unit * jnp.mean(scaled * unit, -1, keepdims=True)
    )


def prepare_first(where, x, seg, wq, wk, wv, bias, own, mine):
    core, _, _, chip, _ = places(where)
    tokens, width = x.shape[1:]
    part, half = width // 4, width // 8
    own[:tokens] = x[0]
    seg_row = jnp.broadcast_to(seg[...].astype(WIDE), (16, tokens)).astype(LOW)
    own[tokens:, :tokens] = seg_row
    own[tokens:, tokens:] = jnp.zeros((16, width - tokens), LOW)
    for j, weight in enumerate((wq, wk, wv)):
        block = weight[rows_from(core * half, half)]
        for k in range(CHIPS):

            @pl.when(chip == k)
            def _():
                mine[:half, j * part : (j + 1) * part] = block[:, k * part : (k + 1) * part]

    mine[half:] = bias[...]


def prepare_rest(where, wo, wi, wu, vectors, first, second):
    core, side, row, _, _ = places(where)
    part, width = wo.shape
    quarter = part // 4
    span = width // 2
    t = 2 * row + core
    first[:quarter] = wo[rows_from(t * quarter, quarter)]
    block = wi[rows_from(t * quarter, quarter)]
    for s in range(2):

        @pl.when(side == s)
        def _():
            for k in range(4):
                start = k * width + s * span
                at_row = quarter * (1 + k // 2)
                first[at_row : at_row + quarter, (k % 2) * span : (k % 2 + 1) * span] = block[
                    :, start : start + span
                ]

    first[3 * quarter :] = vectors[...]
    second[...] = wu[rows_from(side * span + t * (span // 4), span // 4)]


def assemble_first(where, wo, wi, vectors, *refs):
    pieces, (w_output, w_inner, vec, b_inner, stage) = refs[:12], refs[12:]
    core, side, row, _, place = places(where)
    part, width = wo.shape
    quarter, span = part // 4, width // 2
    stage[place] = vectors[...].astype(WIDE)
    for n, piece in enumerate(pieces):
        far_core, far_row, r = n // 6, (n // 3) % 2, n % 3 + 1
        k = place ^ r
        t = 2 * (row ^ far_row) + (core ^ far_core)
        base = rows_from(k * part + t * quarter, quarter)
        w_output[base] = piece[:quarter]
        w_inner[base, :width] = piece[quarter : 2 * quarter]
        w_inner[base, width:] = piece[2 * quarter : 3 * quarter]
        if n < 3:
            stage[k] = piece[3 * quarter :].astype(WIDE)
    base = rows_from(place * part, part)
    w_output[base] = wo[...]
    for s in range(2):

        @pl.when(side == s)
        def _():
            for k in range(4):
                start = k * width + s * span
                w_inner[base, k * span : (k + 1) * span] = wi[:, start : start + span]

    for k in range(4):
        block = stage[k]
        for i in range(6):
            line, start = divmod(i * part, width)
            vec[i : i + 1, k * part : (k + 1) * part] = block[line : line + 1, start : start + part]
        for s in range(2):

            @pl.when(side == s)
            def _():
                line, start = divmod(6 * part + s * span, width)
                b_inner[:, k * span : (k + 1) * span] = block[line : line + 1, start : start + span]

    vec[6:] = jnp.zeros((2, width), WIDE)


def assemble_second(where, wu, *refs):
    pieces, (w_outer,) = refs[:12], refs[12:]
    core, side, row, _, place = places(where)
    span = wu.shape[1] // 2
    for n, piece in enumerate(pieces):
        far_core, far_row, r = n // 6, (n // 3) % 2, n % 3 + 1
        t = 2 * (row ^ far_row) + (core ^ far_core)
        w_outer[rows_from((place ^ r) * span + t * (span // 4), span // 4)] = piece[...]
    w_outer[rows_from(place * span, span)] = wu[rows_from(side * span, span)]


def project(where, x0, x1, x2, x3, *refs):
    pieces, (rows_in, w_qkv, queries, keys_values, segs, stage) = refs[:8], refs[8:]
    core, _, _, chip, place = places(where)
    width = x0.shape[1]
    tokens = rows_in.shape[0] // CHIPS
    part, half = width // 4, width // 8
    for s, x in enumerate((x0, x1, x2, x3)):
        rows_in[s * tokens : (s + 1) * tokens] = x[:tokens]
        segs[s : s + 1] = x[tokens : tokens + 1, :tokens].astype(WIDE)
    segs[CHIPS:] = jnp.zeros((8 - CHIPS, tokens), WIDE)
    for n, piece in enumerate(pieces):
        far_core, r = n // 4, n % 4
        k = place ^ r
        w_qkv[rows_from(k * part + (core ^ far_core) * half, half)] = piece[:half]
        if n < 4:
            stage[k] = piece[half:].astype(WIDE)
    bias = stage[chip]
    out = dot(rows_in[...], w_qkv[...])
    scale = HEAD_DIM ** (-0.5)
    queries[...] = ((out[:, :part] + bias[:1, :part]).astype(LOW).astype(WIDE) * scale).astype(LOW)
    keys_values[:, :part] = out[:, part : 2 * part].astype(LOW)
    keys_values[:, part:] = (out[:, 2 * part :] + bias[:1, part : 2 * part]).astype(LOW)


def attend(queries, seg_query, keys_values, seg_key, context, probs):
    part = queries.shape[1]
    block = seg_key.shape[1]
    seg_columns = seg_key[...].T
    allowed = jnp.concatenate(
        [seg_columns[:, b : b + 1] == seg_query[...] for b in range(seg_key.shape[0])]
    )
    for h in range(part // HEAD_DIM):
        keys = keys_values[:, h * HEAD_DIM : (h + 1) * HEAD_DIM]
        values = keys_values[:, part + h * HEAD_DIM : part + (h + 1) * HEAD_DIM]
        scores = dot_rt(keys, queries[:, h * HEAD_DIM : (h + 1) * HEAD_DIM])
        scores = jnp.where(allowed, scores, NEGATIVE)
        weights = jnp.exp(scores - jnp.max(scores, 0, keepdims=True))
        weights = (weights * (1.0 / jnp.sum(weights, 0, keepdims=True))).astype(LOW)
        probs[h] = weights
        out = dot_lt(values, weights)
        context[:, h * HEAD_DIM : (h + 1) * HEAD_DIM] = out.T.astype(LOW)


def attend_back(queries, keys_values, grad_context, probs, grad_queries, grad_keys_values):
    part = queries.shape[1]
    first = pl.program_id(0) == 0

    @pl.when(first)
    def _():
        grad_keys_values[...] = jnp.zeros(grad_keys_values.shape, WIDE)

    scale = HEAD_DIM ** (-0.5)
    for h in range(part // HEAD_DIM):
        span = slice(h * HEAD_DIM, (h + 1) * HEAD_DIM)
        span_v = slice(part + h * HEAD_DIM, part + (h + 1) * HEAD_DIM)
        keys, values = keys_values[:, span], keys_values[:, span_v]
        grads = grad_context[:, span]
        soft = probs[h]
        grad_values = dot(soft, grads)
        grad_probs = dot_rt(values, grads)
        wide = soft.astype(WIDE)
        delta = jnp.sum(wide * grad_probs, 0, keepdims=True)
        grad_scores = (wide * (grad_probs - delta)).astype(LOW)
        grad_queries[:, span] = (dot_lt(keys, grad_scores) * scale).T.astype(LOW)
        grad_keys_values[:, span] += dot(grad_scores, queries[:, span])
        grad_keys_values[:, span_v] += grad_values


def attention_blocks(queries, keys_values):
    count, keys = queries.shape[0], keys_values.shape[0]
    return min(count, 128 * max(1, 2048 // keys))


def attention(queries, seg_query, keys_values, seg_key):
    count, part = queries.shape
    keys = keys_values.shape[0]
    heads = part // HEAD_DIM
    block = attention_blocks(queries, keys_values)
    whole = lambda a: pl.BlockSpec(a.shape, lambda i: (0,) * a.ndim)
    return pl.pallas_call(
        attend,
        grid=(count // block,),
        in_specs=[
            pl.BlockSpec((block, part), lambda i: (i, 0)),
            pl.BlockSpec((1, block), lambda i: (0, i)),
            whole(keys_values),
            whole(seg_key),
        ],
        out_specs=[
            pl.BlockSpec((block, part), lambda i: (i, 0)),
            pl.BlockSpec((heads, keys, block), lambda i: (0, 0, i)),
        ],
        out_shape=[shape((count, part)), shape((heads, keys, count))],
        compiler_params=pltpu.CompilerParams(vmem_limit_bytes=VMEM_BYTES),
        cost_estimate=pl.CostEstimate(
            flops=4 * count * keys * part, bytes_accessed=4 << 20, transcendentals=count * keys * 3
        ),
    )(queries, seg_query, keys_values, seg_key)


def attention_back(queries, keys_values, grad_context, probs):
    count, part = queries.shape
    keys = keys_values.shape[0]
    block = attention_blocks(queries, keys_values)
    whole = lambda a: pl.BlockSpec(a.shape, lambda i: (0,) * a.ndim)
    rows = pl.BlockSpec((block, part), lambda i: (i, 0))
    return pl.pallas_call(
        attend_back,
        grid=(count // block,),
        in_specs=[
            rows,
            whole(keys_values),
            rows,
            pl.BlockSpec((probs.shape[0], keys, block), lambda i: (0, 0, i)),
        ],
        out_specs=[rows, pl.BlockSpec((keys, 2 * part), lambda i: (0, 0))],
        out_shape=[shape((count, part)), shape((keys, 2 * part), WIDE)],
        compiler_params=pltpu.CompilerParams(vmem_limit_bytes=VMEM_BYTES),
        cost_estimate=pl.CostEstimate(
            flops=8 * count * keys * part, bytes_accessed=6 << 20, transcendentals=0
        ),
    )(queries, keys_values, grad_context, probs)


def swapped(block):
    tokens = block.shape[0] // 2
    return jnp.concatenate([block[tokens:], block[:tokens]])


def forward(where, c0, c1, c2, c3, rows_in, w_output, vec, w_inner, b_inner, w_outer, *outs):
    outer_part, context_low, unit_one, inverse_one, normed_low, activated, slope, stage = outs
    _, _, _, chip, _ = places(where)
    count, part = c0.shape
    stage[chip] = c0[...]
    stage[chip ^ 1] = swapped(c1[...])
    stage[chip ^ 2] = c2[...]
    stage[chip ^ 3] = swapped(c3[...])
    for k in range(CHIPS):
        context_low[:, k * part : (k + 1) * part] = stage[k]
    residual = rows_in[:count].astype(WIDE) + dot(context_low[...], w_output[...]) + vec[0:1]
    unit, inverse = normalized(residual)
    unit_one[...] = unit
    inverse_one[...] = inverse
    normed_low[...] = (unit * vec[1:2] + vec[2:3]).astype(LOW)
    inner_pre = dot(normed_low[...], w_inner[...]) + b_inner[...]
    cdf = 0.5 * (1.0 + lax.erf(inner_pre * (0.5**0.5)))
    activated[...] = (inner_pre * cdf).astype(LOW)
    slope[...] = cdf + inner_pre * jnp.exp(-0.5 * inner_pre * inner_pre) * 0.3989422804014327
    outer_part[...] = dot(activated[...], w_outer[...]).astype(LOW)


def backward(where, part_own, part_far, unit_one, vec, cot, cot_far, slope, w_outer, w_inner, *outs):
    result, grad_summed, grad_outer, grad_inner, inner_part, sums, sums_inner = outs
    tokens = cot.shape[1]
    summed = unit_one[...] * vec[1:2] + vec[2:3] + vec[3:4]
    summed += part_own[...].astype(WIDE) + swapped(part_far[...]).astype(WIDE)
    unit, inverse = normalized(summed)
    result[0] = (unit[:tokens] * vec[4:5] + vec[5:6]).astype(LOW)
    c = jnp.concatenate([cot[0], cot_far[...]]).astype(WIDE)
    grad = norm_back(c, unit, inverse, vec[4:5])
    grad_summed[...] = grad
    grad_outer[...] = grad.astype(LOW)
    grad_inner[...] = (dot_rt(grad_outer[...], w_outer[...]) * slope[...]).astype(LOW)
    inner_part[...] = dot_rt(grad_inner[...], w_inner[...]).astype(LOW)
    sums[0:1] = jnp.sum(grad_outer[...].astype(WIDE), 0, keepdims=True)
    sums[1:2] = jnp.sum(c * unit, 0, keepdims=True)
    sums[2:3] = jnp.sum(c, 0, keepdims=True)
    sums[3:] = jnp.zeros((5, sums.shape[1]), WIDE)
    sums_inner[...] = jnp.sum(grad_inner[...].astype(WIDE), 0, keepdims=True)


def weight_grads(where, left, right, keep, send, stage):
    core, _, row, _, place = places(where)
    stage[...] = dot_lt(left[...], right[...]).astype(LOW)
    part = stage.shape[0] // 4
    n = part // 4
    for r in range(4):
        for y in range(2):
            for c, out in enumerate((keep, send)):
                start = (place ^ r) * part + (2 * (row ^ y) + (core ^ c)) * n
                out[r, y, :n] = stage[rows_from(start, n)]


def norm_backward(where, grad_summed, part_own, part_far, unit_one, inverse_one, vec, w_output, *outs):
    grad_own, grad_low, grad_context, grad_context_row, sums = outs
    _, _, _, chip, _ = places(where)
    tokens = grad_own.shape[0]
    part = grad_context.shape[1]
    grad = grad_summed[...] + part_own[...].astype(WIDE) + swapped(part_far[...]).astype(WIDE)
    unit = unit_one[...]
    branch = norm_back(grad, unit, inverse_one[...], vec[1:2])
    grad_own[...] = branch[:tokens]
    grad_low[...] = branch.astype(LOW)
    grad_context[...] = dot_rt(grad_low[...], w_output[rows_from(chip * part, part)]).astype(LOW)
    grad_context_row[...] = dot_rt(
        grad_low[...], w_output[rows_from((chip ^ 2) * part, part)]
    ).astype(LOW)
    sums[0:1] = jnp.sum(grad_low[...].astype(WIDE), 0, keepdims=True)
    sums[1:2] = jnp.sum(grad * unit, 0, keepdims=True)
    sums[2:3] = jnp.sum(grad, 0, keepdims=True)
    sums[3:] = jnp.zeros((5, sums.shape[1]), WIDE)


def output_grads(where, context_low, grad_low, sums_one, sums_two, sums_inner, keep, send, stage):
    core, side, row, _, place = places(where)
    width = grad_low.shape[1]
    part, span = width // 4, width // 2
    n = part // 4
    for s in range(2):

        @pl.when(side == s)
        def _():
            stage[...] = dot_lt(
                context_low[...], grad_low[:, s * span : (s + 1) * span]
            ).astype(LOW)

    for r in range(4):
        for y in range(2):
            for c, out in enumerate((keep, send)):
                start = (place ^ r) * part + (2 * (row ^ y) + (core ^ c)) * n
                out[r, y, :n] = stage[rows_from(start, n)]
    for k in range(4):
        cut = slice(k * part, (k + 1) * part)
        small = jnp.concatenate(
            [
                jnp.concatenate([sums_one[0:1, cut], sums_one[1:2, cut]], 1),
                jnp.concatenate([sums_one[2:3, cut], sums_two[0:1, cut]], 1),
                jnp.concatenate([sums_two[1:2, cut], sums_two[2:3, cut]], 1),
                sums_inner[:, k * span : (k + 1) * span],
                jnp.zeros((12, span), WIDE),
            ]
        ).astype(LOW)
        for y in range(2):
            keep[place ^ k, y, n:] = small
            send[place ^ k, y, n:] = small


def input_grads(where, grad_queries, grad_kv, grad_kv_far, w_qkv, grad_residual, *outs):
    grad_qkv, own, s1, s2, s3 = outs
    part = grad_queries.shape[1]
    tokens = own.shape[0]
    grad_qkv[:, :part] = grad_queries[...]
    grad_qkv[:, part:] = (grad_kv[...] + grad_kv_far[...].astype(WIDE)).astype(LOW)
    grads = dot_rt(grad_qkv[...], w_qkv[...])
    own[...] = grad_residual[...] + grads[:tokens]
    for s, out in enumerate((s1, s2, s3)):
        out[...] = grads[(s + 1) * tokens : (s + 2) * tokens].astype(LOW)


def projection_grads(where, rows_in, grad_qkv, keep, send, stage):
    core, _, _, _, place = places(where)
    stage[...] = dot_lt(rows_in[...], grad_qkv[...]).astype(LOW)
    half = stage.shape[0] // 8
    total = jnp.sum(grad_qkv[...].astype(WIDE), 0, keepdims=True)
    total = jnp.broadcast_to(total, (16, total.shape[1])).astype(LOW)
    for r in range(4):
        for c, out in enumerate((keep, send)):
            start = (2 * (place ^ r) + (core ^ c)) * half
            out[r, :half] = stage[rows_from(start, half)]
            out[r, half:] = total


def add_rows(where, kept, received, keep, send):
    total = kept[...].astype(WIDE) + received[...].astype(WIDE)
    keep[...] = total[:, 0].astype(LOW)
    send[...] = total[:, 1].astype(LOW)


def add_near(where, kept, received, keep, send):
    total = kept[...].astype(WIDE) + received[...].astype(WIDE)
    for r in range(2):
        keep[r] = total[2 * r].astype(LOW)
        send[r] = total[2 * r + 1].astype(LOW)


def add_far(where, kept, received, keep, send):
    total = kept[...].astype(WIDE) + received[...].astype(WIDE)
    keep[...] = total[0].astype(LOW)
    send[...] = total[1].astype(LOW)


def add_last(where, kept, received, out):
    out[...] = (kept[...].astype(WIDE) + received[...].astype(WIDE)).astype(LOW)


def unpack_outer(where, *refs):
    pieces, (out,) = refs[:8], refs[8:]
    core, _, _, chip, _ = places(where)
    n = pieces[0].shape[0]
    for m, piece in enumerate(pieces):
        far = chip ^ (m % 4)
        start = ((far & 1) * 4 + 2 * (far >> 1) + (core ^ (m // 4))) * n
        out[rows_from(start, n)] = piece[...].astype(WIDE)


def unpack_inner(where, *refs):
    pieces, (out,) = refs[:8], refs[8:]
    core, side, _, chip, _ = places(where)
    n = pieces[0].shape[0]
    span = pieces[0].shape[1] // 4
    for m, piece in enumerate(pieces):
        far = chip ^ (m % 4)
        base = rows_from((2 * (far >> 1) + (core ^ (m // 4))) * n, n)
        for s in range(2):

            @pl.when((far & 1) == s)
            def _():
                for k in range(4):
                    start = (2 * k + s) * span
                    out[base, start : start + span] = piece[:, k * span : (k + 1) * span].astype(
                        WIDE
                    )


def unpack_output(where, *refs):
    pieces, (out, vec, bias, stage) = refs[:8], refs[8:]
    core, side, _, chip, _ = places(where)
    span = pieces[0].shape[1]
    n = pieces[0].shape[0] - 16
    part = span // 2
    for m, piece in enumerate(pieces):
        far = chip ^ (m % 4)
        base = rows_from((2 * (far >> 1) + (core ^ (m // 4))) * n, n)
        for s in range(2):

            @pl.when((far & 1) == s)
            def _():
                out[base, s * span : (s + 1) * span] = piece[:n].astype(WIDE)

    small = pieces[0][n:].astype(WIDE)
    for i in range(6):
        vec[i : i + 1] = small[i // 2 : i // 2 + 1, (i % 2) * part : (i % 2 + 1) * part]
    vec[6:] = jnp.zeros((2, part), WIDE)
    stage[side] = small
    stage[side ^ 1] = pieces[1][n:].astype(WIDE)
    for s in range(2):
        bias[:, s * span : (s + 1) * span] = stage[s, 3:4]


def unpack_projections(where, *refs):
    pieces, (out_q, out_k, out_v, bias, stage) = refs[:8], refs[8:]
    core, _, _, chip, place = places(where)
    half = pieces[0].shape[0] - 16
    part = 2 * half
    for m, piece in enumerate(pieces):
        stage[core ^ (m // 4), chip ^ (m % 4)] = piece[...]
    for c in range(2):
        for k in range(CHIPS):
            for j, out in enumerate((out_q, out_k, out_v)):
                out[c * half : (c + 1) * half, k * part : (k + 1) * part] = stage[
                    c, k, :half, j * part : (j + 1) * part
                ].astype(WIDE)
    small = stage[0, place][half:].astype(WIDE)
    for j in range(3):
        bias[j : j + 1] = small[:1, j * part : (j + 1) * part]
    bias[3:] = jnp.zeros((5, part), WIDE)


def per_device(
    inputs,
    segments,
    query_weight,
    query_bias,
    key_weight,
    value_weight,
    value_bias,
    output_weight,
    output_bias,
    first_gain,
    first_shift,
    inner_weight,
    inner_bias,
    outer_weight,
    outer_bias,
    second_gain,
    second_shift,
    cotangent,
):
    where = jnp.stack([lax.axis_index("ctx"), lax.axis_index("fsdp")]).astype(jnp.int32)
    groups = lax.axis_size("ctx") // TEAM
    lines = [[m + TEAM * g for g in range(groups)] for m in range(TEAM)]
    tokens, width = inputs.shape[1:]
    part = query_weight.shape[0]
    hidden = outer_weight.shape[0]
    count, pair = CHIPS * tokens, 2 * tokens
    half, quarter, span = part // 2, part // 4, hidden // 2

    biases = jnp.pad(jnp.concatenate([query_bias, value_bias])[None], ((0, 15), (0, part)))
    own, mine = kernel(
        prepare_first,
        [shape((tokens + 16, width)), shape((half + 16, 3 * part))],
        where,
        inputs,
        segments,
        query_weight,
        key_weight,
        value_weight,
        biases,
    )
    seen = [own] + [partner(own, "ctx", s << 1) for s in (1, 2, 3)]
    line = [mine] + [partner(mine, "fsdp", r) for r in (1, 2, 3)]
    line += [partner(piece, "ctx", CORE) for piece in line]

    vectors = jnp.concatenate(
        [output_bias, first_gain, first_shift, outer_bias, second_gain, second_shift, inner_bias]
    )
    vectors = jnp.pad(vectors, (0, 16 * width - vectors.shape[0])).reshape(16, width)
    first, second = kernel(
        prepare_rest,
        [shape((3 * quarter + 16, width)), shape((span // 4, width))],
        where,
        output_weight,
        inner_weight,
        outer_weight,
        vectors,
    )

    def gathered(piece):
        far, near = partner(piece, "fsdp", 2), partner(piece, "fsdp", 1)
        found = [near, far, partner(far, "fsdp", 1)]
        found += [partner(block, "ctx", ROW) for block in found]
        return found + [partner(block, "ctx", CORE) for block in found]

    w_output, w_inner, vec, b_inner = kernel(
        assemble_first,
        [
            shape((width, width)),
            shape((width, 4 * span)),
            shape((8, width), WIDE),
            shape((1, 4 * span), WIDE),
        ],
        where,
        output_weight,
        inner_weight,
        vectors,
        *gathered(first),
        scratch=[pltpu.VMEM((4, 16, width), WIDE)],
    )
    (w_outer,) = kernel(
        assemble_second, [shape((4 * span, width))], where, outer_weight, *gathered(second)
    )

    rows_in, w_qkv, queries, kv_own, segs = kernel(
        project,
        [
            shape((count, width)),
            shape((width, 3 * part)),
            shape((count, part)),
            shape((count, 2 * part)),
            shape((8, tokens), WIDE),
        ],
        where,
        *seen,
        *line,
        scratch=[pltpu.VMEM((4, 16, 3 * part), WIDE)],
        flops=6 * count * width * part,
    )
    segs = segs[:CHIPS]
    kv = jnp.concatenate([kv_own, partner(kv_own, "ctx", CORE)])
    seg_key = jnp.concatenate([segs, partner(segs, "ctx", CORE)])
    if groups > 1:
        kv = lax.all_gather(kv, "ctx", axis=0, tiled=True, axis_index_groups=lines)
        seg_key = lax.all_gather(seg_key, "ctx", axis=0, tiled=True, axis_index_groups=lines)
    context, probs = attention(queries, segs.reshape(1, count), kv, seg_key)

    c0, c_row = context[:pair], context[pair:]
    outer_part, context_low, unit_one, inverse_one, normed_low, activated, slope = kernel(
        forward,
        [
            shape((pair, width)),
            shape((pair, width)),
            shape((pair, width), WIDE),
            shape((pair, 1), WIDE),
            shape((pair, width)),
            shape((pair, 4 * span)),
            shape((pair, 4 * span), WIDE),
        ],
        where,
        c0,
        partner(c0, "ctx", SIDE),
        partner(c_row, "ctx", ROW),
        partner(c_row, "ctx", SIDE | ROW),
        rows_in,
        w_output,
        vec,
        w_inner,
        b_inner,
        w_outer,
        scratch=[pltpu.VMEM((CHIPS, pair, part), LOW)],
        flops=2 * pair * width * (width + 8 * span),
    )
    result, grad_summed, grad_outer, grad_inner, inner_part, sums_one, sums_inner = kernel(
        backward,
        [
            shape((1, tokens, width)),
            shape((pair, width), WIDE),
            shape((pair, width)),
            shape((pair, 4 * span)),
            shape((pair, width)),
            shape((8, width), WIDE),
            shape((1, 4 * span), WIDE),
        ],
        where,
        outer_part,
        partner(outer_part, "ctx", SIDE),
        unit_one,
        vec,
        cotangent,
        partner(cotangent[0], "ctx", SIDE),
        slope,
        w_outer,
        w_inner,
        flops=2 * pair * width * 8 * span,
    )
    inner_far = partner(inner_part, "ctx", SIDE)

    def grads_of(left, right):
        rows, columns = left.shape[1], right.shape[1]
        cut = shape((4, 2, rows // 16, columns))
        return kernel(
            weight_grads,
            [cut, cut],
            where,
            left,
            right,
            scratch=[pltpu.VMEM((rows, columns), LOW)],
            flops=2 * pair * rows * columns,
        )

    outer_kept, outer_sent = grads_of(activated, grad_outer)
    inner_kept, inner_sent = grads_of(normed_low, grad_inner)
    grad_residual, grad_low, grad_context, grad_context_row, sums_two = kernel(
        norm_backward,
        [
            shape((tokens, width), WIDE),
            shape((pair, width)),
            shape((pair, part)),
            shape((pair, part)),
            shape((8, width), WIDE),
        ],
        where,
        grad_summed,
        inner_part,
        inner_far,
        unit_one,
        inverse_one,
        vec,
        w_output,
        flops=4 * pair * width * part,
    )
    grad_context = jnp.concatenate([grad_context, partner(grad_context_row, "ctx", ROW)])
    cut = shape((4, 2, quarter + 16, width // 2))
    output_kept, output_sent = kernel(
        output_grads,
        [cut, cut],
        where,
        context_low,
        grad_low,
        sums_one,
        sums_two,
        sums_inner,
        scratch=[pltpu.VMEM((width, width // 2), LOW)],
        flops=pair * width * width,
    )
    grad_queries, grad_kv = attention_back(queries, kv, grad_context, probs)
    if groups > 1:
        grad_kv = grad_kv.reshape(groups, 2, count, 2 * part).transpose(1, 0, 2, 3)
        grad_kv = lax.psum_scatter(
            grad_kv.reshape(2, groups * count, 2 * part),
            "ctx",
            scatter_dimension=1,
            tiled=True,
            axis_index_groups=lines,
        ).reshape(2 * count, 2 * part)
    grad_kv_far = partner(grad_kv[count:].astype(LOW), "ctx", CORE)
    grad_qkv, grad_tokens, *grads_sent = kernel(
        input_grads,
        [shape((count, 3 * part)), shape((tokens, width), WIDE)] + [shape((tokens, width))] * 3,
        where,
        grad_queries,
        grad_kv[:count],
        grad_kv_far,
        w_qkv,
        grad_residual,
        flops=6 * count * width * part,
    )
    cut = shape((4, half + 16, 3 * part))
    qkv_kept, qkv_sent = kernel(
        projection_grads,
        [cut, cut],
        where,
        rows_in,
        grad_qkv,
        scratch=[pltpu.VMEM((width, 3 * part), LOW)],
        flops=6 * count * width * part,
    )
    for s, block in enumerate(grads_sent):
        grad_tokens = grad_tokens + partner(block, "ctx", (s + 1) << 1).astype(WIDE)

    def summed(kept, sent):
        received = partner(sent, "ctx", CORE)
        if kept.ndim == 4:
            kept, sent = kernel(add_rows, [shape(kept.shape[:1] + kept.shape[2:])] * 2, where, kept, received)
            received = partner(sent, "ctx", ROW)
        piece = kept.shape[1:]
        kept, sent = kernel(add_near, [shape((2,) + piece)] * 2, where, kept, received)
        received = partner(sent, "fsdp", 1)
        kept, sent = kernel(add_far, [shape(piece)] * 2, where, kept, received)
        (total,) = kernel(add_last, [shape(piece)], where, kept, partner(sent, "fsdp", 2))
        if groups > 1:
            total = lax.psum(total.astype(WIDE), "ctx", axis_index_groups=lines).astype(LOW)
        chips = [total] + [partner(total, "ctx", s << 1) for s in (1, 2, 3)]
        return chips + [partner(block, "ctx", CORE) for block in chips]

    (g_outer,) = kernel(
        unpack_outer, [shape((hidden, width), WIDE)], where, *summed(outer_kept, outer_sent)
    )
    (g_inner,) = kernel(
        unpack_inner, [shape((part, 4 * hidden), WIDE)], where, *summed(inner_kept, inner_sent)
    )
    g_output, g_vec, g_b_inner = kernel(
        unpack_output,
        [shape((part, width), WIDE), shape((8, part), WIDE), shape((1, hidden), WIDE)],
        where,
        *summed(output_kept, output_sent),
        scratch=[pltpu.VMEM((2, 16, width // 2), WIDE)],
    )
    g_query, g_key, g_value, g_bias = kernel(
        unpack_projections,
        [shape((part, width), WIDE)] * 3 + [shape((8, part), WIDE)],
        where,
        *summed(qkv_kept, qkv_sent),
        scratch=[pltpu.VMEM((2, CHIPS, half + 16, 3 * part), LOW)],
    )
    return (
        result,
        grad_tokens.astype(LOW)[None],
        g_query,
        g_bias[0],
        g_key,
        g_value,
        g_bias[2],
        g_output,
        g_vec[3],
        g_vec[4],
        g_vec[5],
        g_inner,
        g_b_inner[0],
        g_outer,
        g_vec[0],
        g_vec[1],
        g_vec[2],
    )


def solution(mesh):
    rows, cuts, whole = P("fsdp", "ctx", None), P("fsdp", None), P("fsdp")
    params = (cuts, whole, cuts, cuts, whole, cuts, whole, whole, whole)
    params += (cuts, whole, cuts, whole, whole, whole)
    return jax.shard_map(
        per_device,
        mesh=mesh,
        in_specs=(rows, P("fsdp", "ctx")) + params + (rows,),
        out_specs=(rows, rows) + params,
        check_vma=False,
    )
```

```python
import functools

import jax
import jax.numpy as jnp
from jax import lax
from jax.experimental import pallas as pl
from jax.experimental.pallas import tpu as pltpu
from jax.sharding import PartitionSpec as P

HEAD_DIM = 64
NEGATIVE = -1000000000.0
EPSILON = 1e-12
LOW = jnp.bfloat16
WIDE = jnp.float32

CORE, SIDE, ROW = 1, 2, 4
TEAM = 8
CHIPS = 4
VMEM_BYTES = 56 << 20


def partner(block, axis, bit):
    devices = range(lax.axis_size(axis))
    return lax.ppermute(block, axis, [(i, i ^ bit) for i in devices])


def dot(left, right):
    return jnp.dot(left, right, preferred_element_type=WIDE)


def dot_rt(left, right):
    return lax.dot_general(left, right, (((1,), (1,)), ((), ())), preferred_element_type=WIDE)


def dot_lt(left, right):
    return lax.dot_general(left, right, (((0,), (0,)), ((), ())), preferred_element_type=WIDE)


def shape(dims, dtype=LOW):
    return jax.ShapeDtypeStruct(tuple(dims), dtype)


def kernel(body, outs, *args, scratch=(), room=8, last=(), after=(), loads=0):
    spec = pl.BlockSpec(memory_space=pltpu.VMEM)
    off = pl.BlockSpec(memory_space=pl.ANY)
    place = pltpu.HBM if loads else pltpu.VMEM
    args = tuple(pltpu.with_memory_space_constraint(a, place) for a in args)
    waits = len(after)

    def step(*refs):
        body(*refs[waits:])

    sems = [pltpu.SemaphoreType.DMA((loads,))] if loads else []
    return pl.pallas_call(
        step,
        out_shape=[
            o if n in last else pltpu.VMEM(o.shape, o.dtype) for n, o in enumerate(outs)
        ],
        in_specs=[off] * waits + [off if loads else spec] * len(args),
        out_specs=[spec] * len(outs),
        scratch_shapes=list(scratch) + sems,
        compiler_params=pltpu.CompilerParams(vmem_limit_bytes=room << 20),
        cost_estimate=pl.CostEstimate(flops=1, bytes_accessed=1, transcendentals=0),
    )(*after, *args)


def load(sems, *pairs):
    copies = [
        pltpu.make_async_copy(source, target, sems.at[n])
        for n, (source, target) in enumerate(pairs)
    ]
    for copy in copies:
        copy.start()
    return copies


def places():
    index, place = lax.axis_index("ctx"), lax.axis_index("fsdp")
    core, side, row = index & 1, (index >> 1) & 1, (index >> 2) & 1
    return core, side, row, (index >> 1) & 3, place


def rows_from(start, count):
    return pl.ds(pl.multiple_of(start, 16), count)


def normalized(values):
    center = values - jnp.mean(values, -1, keepdims=True)
    inverse = lax.rsqrt(jnp.mean(center * center, -1, keepdims=True) + EPSILON)
    return center * inverse, inverse


def norm_back(grad, unit, inverse, gain):
    scaled = grad * gain
    return inverse * (
        scaled
        - jnp.mean(scaled, -1, keepdims=True)
        - unit * jnp.mean(scaled * unit, -1, keepdims=True)
    )


def lines_of(*vectors):
    rows = [v[...].astype(WIDE).reshape(1, v.shape[0]) for v in vectors]
    return jnp.concatenate(rows + [jnp.zeros((16 - len(rows), rows[0].shape[1]), WIDE)])


def prepare_tokens(x, seg, own, line, sems):
    tokens, width = x.shape[1:]
    for copy in load(sems, (seg, line), (x.at[0], own.at[pl.ds(0, tokens)])):
        copy.wait()
    seg_row = jnp.broadcast_to(line[...].astype(WIDE), (16, tokens)).astype(LOW)
    own[tokens:, :tokens] = seg_row
    own[tokens:, tokens:] = jnp.zeros((16, width - tokens), LOW)


def prepare_weights(wq, wk, wv, wo, wi, wu, *refs):
    vectors, first, (blocks, block), lines, sems = (
        refs[:9],
        refs[9],
        refs[10:12],
        refs[12:21],
        refs[21],
    )
    core, _, _, chip, _ = places()
    part, width = wq.shape
    half = part // 2
    rows = rows_from(core * half, half)
    pairs = [(w.at[rows], blocks.at[j]) for j, w in enumerate((wq, wk, wv))]
    pairs += [(wi.at[rows], block), (wo.at[rows], first.at[pl.ds(half, half)])]
    rows = rows_from((2 * chip + core) * half, half)
    pairs += [(wu.at[rows], first.at[pl.ds(3 * half, half)])]
    for copy in load(sems, *pairs, *zip(vectors, lines)):
        copy.wait()
    six, bias_inner, biases = lines_of(*lines[:6]), lines_of(lines[6]), lines_of(*lines[7:])
    for p in range(CHIPS):

        @pl.when(chip == p)
        def _():
            span = slice(p * part, (p + 1) * part)
            for j in range(3):
                first[:half, j * part : (j + 1) * part] = blocks[j, :, span]
            for k in range(4):
                start = k * width + p * part
                first[2 * half : 3 * half, k * part : (k + 1) * part] = block[
                    :, start : start + part
                ]
            small = [six[:6], bias_inner[:1, span], biases[:2], jnp.zeros((half - 9, part), WIDE)]
            first[:half, 3 * part :] = jnp.concatenate(small).astype(LOW)


def first_rows(block, out):
    out[...] = block[: out.shape[0]]


def passed(block, out):
    out[...] = block[...]


def sort_pieces(own, near, far, farthest, projections, others, sent):
    half = farthest.shape[0]
    for r, piece in enumerate((own, near, far, farthest)):
        projections[r] = piece[:half]
    for r, piece in enumerate((own, near, far)):
        others[r] = piece[half:]
    sent[...] = far[half:]


def assemble(own, own_last, other, other_last, *weights):
    core, _, _, _, place = places()
    half = weights[0].shape[0] // 8
    for c, (pieces, last) in enumerate(((own, own_last), (other, other_last))):
        for r in range(4):
            piece = last if r == 3 else pieces.at[r]
            base = rows_from((2 * (place ^ r) + (core ^ c)) * half, half)
            for m, weight in enumerate(weights):
                weight[base] = piece[m * half : (m + 1) * half]


def project(seen, *refs):
    pieces, outs = refs[:2], refs[2:]
    rows_in, w_qkv, queries, keys_values, segs, vec, b_inner, stage = outs
    core, _, _, chip, place = places()
    width = seen.shape[2]
    tokens = rows_in.shape[0] // CHIPS
    part, half = width // 4, width // 8
    for s in range(CHIPS):
        x = seen.at[chip ^ s]
        rows_in[s * tokens : (s + 1) * tokens] = x[:tokens]
        segs[s : s + 1] = x[tokens : tokens + 1, :tokens].astype(WIDE)
    segs[CHIPS:] = jnp.zeros((8 - CHIPS, tokens), WIDE)
    for r in range(4):
        for c, piece in enumerate(pieces):
            base = rows_from((2 * (place ^ r) + (core ^ c)) * half, half)
            w_qkv[base] = piece[r, :, : 3 * part]
        stage[place ^ r] = pieces[0][r, :16, 3 * part :].astype(WIDE)
    for k in range(4):
        span = slice(k * part, (k + 1) * part)
        vec[:6, span] = stage[k, :6]
        b_inner[:, span] = stage[k, 6:7]
    vec[6:] = jnp.zeros((2, width), WIDE)
    bias = stage[chip]
    out = dot(rows_in[...], w_qkv[...])
    scale = HEAD_DIM ** (-0.5)
    queries[...] = ((out[:, :part] + bias[7:8]).astype(LOW).astype(WIDE) * scale).astype(LOW)
    keys_values[:, :part] = out[:, part : 2 * part].astype(LOW)
    keys_values[:, part:] = (out[:, 2 * part :] + bias[8:9]).astype(LOW)


def attend(queries, seg_query, keys_values, seg_key, context, probs):
    part = queries.shape[1]
    seg_columns = seg_key[...].T
    seg_row = seg_query[...]
    allowed = jnp.concatenate(
        [seg_columns[:, b : b + 1] == seg_row for b in range(seg_key.shape[0])]
    )
    for h in range(part // HEAD_DIM):
        keys = keys_values[:, h * HEAD_DIM : (h + 1) * HEAD_DIM]
        values = keys_values[:, part + h * HEAD_DIM : part + (h + 1) * HEAD_DIM]
        scores = dot_rt(keys, queries[:, h * HEAD_DIM : (h + 1) * HEAD_DIM])
        scores = jnp.where(allowed, scores, NEGATIVE)
        weights = jnp.exp(scores - jnp.max(scores, 0, keepdims=True))
        weights = (weights * (1.0 / jnp.sum(weights, 0, keepdims=True))).astype(LOW)
        probs[h] = weights
        out = dot_lt(values, weights)
        context[:, h * HEAD_DIM : (h + 1) * HEAD_DIM] = out.T.astype(LOW)


def attend_back(queries, keys_values, grad_context, probs, grad_queries, grad_keys_values):
    part = queries.shape[1]
    scale = HEAD_DIM ** (-0.5)
    for h in range(part // HEAD_DIM):
        span = slice(h * HEAD_DIM, (h + 1) * HEAD_DIM)
        span_v = slice(part + h * HEAD_DIM, part + (h + 1) * HEAD_DIM)
        keys, values = keys_values[:, span], keys_values[:, span_v]
        grads = grad_context[:, span]
        soft = probs[h]
        grad_keys_values[:, span_v] += dot(soft, grads)
        grad_probs = dot_rt(values, grads)
        wide = soft.astype(WIDE)
        delta = jnp.sum(wide * grad_probs, 0, keepdims=True)
        grad_scores = (wide * (grad_probs - delta)).astype(LOW)
        grad_queries[:, span] = (dot_lt(keys, grad_scores) * scale).T.astype(LOW)
        grad_keys_values[:, span] += dot(grad_scores, queries[:, span])


def attend_all(queries, kv_own, kv_far, seg_own, seg_far, context, probs, *scratch):
    keys_values, seg_key, seg_query = scratch
    count = kv_own.shape[0]
    tokens = seg_own.shape[1]
    keys_values[:count] = kv_own[...]
    keys_values[count:] = kv_far[...]
    seg_key[:CHIPS] = seg_own[:CHIPS]
    seg_key[CHIPS:] = seg_far[:CHIPS]
    for s in range(CHIPS):
        seg_query[:, s * tokens : (s + 1) * tokens] = seg_own[s : s + 1]
    attend(queries, seg_query, keys_values, seg_key, context, probs)


def context_back(g0, g1, g2, g3, w_output, grad_low, grad_context):
    _, _, _, chip, _ = places()
    tokens, part = g0.shape[0], grad_context.shape[1]
    for s, block in enumerate((g0, g1, g2, g3)):
        grad_low[s * tokens : (s + 1) * tokens] = block[...]
    grad_context[...] = dot_rt(grad_low[...], w_output[rows_from(chip * part, part)]).astype(LOW)


def attend_back_all(queries, kv_own, kv_far, g0, g1, g2, g3, w_output, probs, *refs):
    grad_low, grad_queries, grad_own, grad_far, keys_values, grad_context, total = refs
    count = kv_own.shape[0]
    keys_values[:count] = kv_own[...]
    keys_values[count:] = kv_far[...]
    context_back(g0, g1, g2, g3, w_output, grad_low, grad_context)
    total[...] = jnp.zeros(total.shape, WIDE)
    attend_back(queries, keys_values, grad_context, probs, grad_queries, total)
    grad_own[...] = total[:count]
    grad_far[...] = total[count:].astype(LOW)


def attend_back_block(queries, keys_values, grads, probs, grad_queries, grad_keys_values):
    @pl.when(pl.program_id(0) == 0)
    def _():
        grad_keys_values[...] = jnp.zeros(grad_keys_values.shape, WIDE)

    attend_back(queries, keys_values, grads, probs, grad_queries, grad_keys_values)


def attention_block(queries, keys_values):
    return min(queries.shape[0], 128 * max(1, 2048 // keys_values.shape[0]))


def whole(array):
    return pl.BlockSpec(array.shape, lambda i: (0,) * array.ndim)


def attention(queries, seg_query, keys_values, seg_key):
    count, part = queries.shape
    keys = keys_values.shape[0]
    heads = part // HEAD_DIM
    block = attention_block(queries, keys_values)
    return pl.pallas_call(
        attend,
        grid=(count // block,),
        in_specs=[
            pl.BlockSpec((block, part), lambda i: (i, 0)),
            pl.BlockSpec((1, block), lambda i: (0, i)),
            whole(keys_values),
            whole(seg_key),
        ],
        out_specs=[
            pl.BlockSpec((block, part), lambda i: (i, 0)),
            pl.BlockSpec((heads, keys, block), lambda i: (0, 0, i)),
        ],
        out_shape=[shape((count, part)), shape((heads, keys, count))],
        compiler_params=pltpu.CompilerParams(vmem_limit_bytes=VMEM_BYTES),
    )(queries, seg_query, keys_values, seg_key)


def attention_back(queries, keys_values, grad_context, probs):
    count, part = queries.shape
    keys = keys_values.shape[0]
    block = attention_block(queries, keys_values)
    rows = pl.BlockSpec((block, part), lambda i: (i, 0))
    return pl.pallas_call(
        attend_back_block,
        grid=(count // block,),
        in_specs=[
            rows,
            whole(keys_values),
            rows,
            pl.BlockSpec((probs.shape[0], keys, block), lambda i: (0, 0, i)),
        ],
        out_specs=[rows, pl.BlockSpec((keys, 2 * part), lambda i: (0, 0))],
        out_shape=[shape((count, part)), shape((keys, 2 * part), WIDE)],
        compiler_params=pltpu.CompilerParams(vmem_limit_bytes=VMEM_BYTES),
    )(queries, keys_values, grad_context, probs)


def forward(c0, c1, c2, c3, rows_in, w_output, vec, w_inner, b_inner, w_outer, *outs):
    context_low, unit_one, inverse_one, normed_low, activated, slope = outs[:6]
    own, sent, stage = outs[6], outs[7:10], outs[10]
    _, _, _, chip, _ = places()
    count, part = c0.shape
    tokens = count // CHIPS
    for s, block in enumerate((c0, c1, c2, c3)):
        for t in range(CHIPS):
            stage[chip ^ s, t * tokens : (t + 1) * tokens] = block[
                (t ^ s) * tokens : ((t ^ s) + 1) * tokens
            ]
    for k in range(CHIPS):
        context_low[:, k * part : (k + 1) * part] = stage[k]
    residual = rows_in[...].astype(WIDE) + dot(context_low[...], w_output[...]) + vec[0:1]
    unit, inverse = normalized(residual)
    unit_one[...] = unit[:tokens]
    inverse_one[...] = inverse[:tokens]
    normed_low[...] = (unit * vec[1:2] + vec[2:3]).astype(LOW)
    inner_pre = dot(normed_low[...], w_inner[...]) + b_inner[...]
    cdf = 0.5 * (1.0 + lax.erf(inner_pre * (0.5**0.5)))
    activated[...] = (inner_pre * cdf).astype(LOW)
    slope[...] = cdf + inner_pre * jnp.exp(-0.5 * inner_pre * inner_pre) * 0.3989422804014327
    parted(dot(activated[...], w_outer[...]), own, sent)


def parted(values, own, sent):
    tokens = own.shape[0]
    own[...] = values[:tokens]
    for s, out in enumerate(sent):
        out[...] = values[(s + 1) * tokens : (s + 2) * tokens].astype(LOW)


def total_of(own, blocks):
    total = own[...]
    for block in blocks:
        total = total + block[...].astype(WIDE)
    return total


def backward_first(own, s1, s2, s3, unit_one, vec, cot, result, grad_summed, grad_outer, sums):
    summed = unit_one[...] * vec[1:2] + vec[2:3] + vec[3:4] + total_of(own, (s1, s2, s3))
    unit, inverse = normalized(summed)
    result[0] = (unit * vec[4:5] + vec[5:6]).astype(LOW)
    c = cot[0].astype(WIDE)
    grad = norm_back(c, unit, inverse, vec[4:5])
    grad_summed[...] = grad
    grad_outer[...] = grad.astype(LOW)
    sums[0:1] = jnp.sum(grad_outer[...].astype(WIDE), 0, keepdims=True)
    sums[1:2] = jnp.sum(c * unit, 0, keepdims=True)
    sums[2:3] = jnp.sum(c, 0, keepdims=True)
    sums[3:] = jnp.zeros((5, sums.shape[1]), WIDE)


def backward_second(g0, g1, g2, g3, slope, w_outer, w_inner, grad_outer, grad_inner, sums, *outs):
    tokens = g0.shape[0]
    for s, block in enumerate((g0, g1, g2, g3)):
        grad_outer[s * tokens : (s + 1) * tokens] = block[...]
    grad_inner[...] = (dot_rt(grad_outer[...], w_outer[...]) * slope[...]).astype(LOW)
    parted(dot_rt(grad_inner[...], w_inner[...]), outs[0], outs[1:])
    sums[...] = jnp.sum(grad_inner[...].astype(WIDE), 0, keepdims=True)


def weight_grads(activated, grad_outer, normed_low, grad_inner, keep, send, stage):
    core, _, _, _, place = places()
    half = keep.shape[1] // 2
    for m, (left, right) in enumerate(((activated, grad_outer), (normed_low, grad_inner))):
        stage[...] = dot_lt(left[...], right[...]).astype(LOW)
        for r in range(4):
            for c, out in enumerate((keep, send)):
                start = (2 * (place ^ r) + (core ^ c)) * half
                out[r, m * half : (m + 1) * half] = stage[rows_from(start, half)]


def norm_backward(grad_summed, own, s1, s2, s3, unit_one, inverse_one, vec, grad_own, grad_low, sums):
    grad = grad_summed[...] + total_of(own, (s1, s2, s3))
    unit = unit_one[...]
    branch = norm_back(grad, unit, inverse_one[...], vec[1:2])
    grad_own[...] = branch
    grad_low[...] = branch.astype(LOW)
    sums[0:1] = jnp.sum(grad_low[...].astype(WIDE), 0, keepdims=True)
    sums[1:2] = jnp.sum(grad * unit, 0, keepdims=True)
    sums[2:3] = jnp.sum(grad, 0, keepdims=True)
    sums[3:] = jnp.zeros((5, sums.shape[1]), WIDE)


def output_grads(context_low, grad_low, out):
    _, _, _, chip, _ = places()
    part = out.shape[1]
    for p in range(CHIPS):

        @pl.when(chip == p)
        def _():
            block = grad_low[:, p * part : (p + 1) * part]
            out[...] = dot_lt(context_low[...], block).astype(LOW)


def projection_grads(
    rows_in, grad_queries, grad_kv, grad_kv_far, grad_o, sums_one, sums_two, sums_inner, *outs
):
    grad_qkv, keep, send, stage = outs
    core, _, _, _, place = places()
    part = grad_queries.shape[1]
    width = 4 * part
    grad_qkv[:, :part] = grad_queries[...]
    grad_qkv[:, part:] = (grad_kv[...] + grad_kv_far[...].astype(WIDE)).astype(LOW)
    stage[:, : 3 * part] = dot_lt(rows_in[...], grad_qkv[...]).astype(LOW)
    stage[:, 3 * part :] = grad_o[...]
    half = part // 2
    total = jnp.sum(grad_qkv[...].astype(WIDE), 0, keepdims=True)
    for k in range(4):
        span = slice(k * part, (k + 1) * part)
        small = jnp.concatenate(
            [
                sums_one[:3, span],
                sums_two[:3, span],
                sums_inner[:, span],
                total[:, :part],
                total[:, 2 * part :],
                jnp.zeros((7, part), WIDE),
            ]
        )
        small = jnp.concatenate([small, jnp.zeros((16, width - part), WIDE)], 1).astype(LOW)
        for c, out in enumerate((keep, send)):
            out[place ^ k, half:] = small
            out[place ^ k, :half] = stage[rows_from(k * part + (core ^ c) * half, half)]


def input_grads(grad_qkv, w_qkv, grad_residual, own, s1, s2, s3):
    tokens = own.shape[0]
    grads = dot_rt(grad_qkv[...], w_qkv[...])
    parted(grads, own, (s1, s2, s3))
    own[...] += grad_residual[...]


def add_tokens(own, s1, s2, s3, out):
    out[0] = total_of(own, (s1, s2, s3)).astype(LOW)


def add_near(kept, received, keep, send):
    total = kept[...].astype(WIDE) + received[...].astype(WIDE)
    for r in range(2):
        keep[r] = total[2 * r].astype(LOW)
        send[r] = total[2 * r + 1].astype(LOW)


def add_near_both(kept, received, *outs):
    half = outs[0].shape[1]
    for m in range(2):
        rows = pl.ds(m * half, half)
        add_near(kept.at[:, rows], received.at[:, rows], *outs[2 * m : 2 * m + 2])


def add_far(kept, received, keep, send):
    total = kept[...].astype(WIDE) + received[...].astype(WIDE)
    keep[...] = total[0].astype(LOW)
    send[...] = total[1].astype(LOW)


def add_far_passing(kept, received, other, keep, send, out):
    add_far(kept, received, keep, send)
    out[...] = other[...]


def add_last(kept, received, out):
    out[...] = (kept[...].astype(WIDE) + received[...].astype(WIDE)).astype(LOW)


def unpack_mlp(*refs):
    pieces, blocks, (outer, inner, stage) = refs[:8], refs[8:16], refs[16:]
    core, _, _, chip, _ = places()
    half, width = pieces[0].shape
    part = 2 * half
    for i, (piece, block) in enumerate(zip(pieces, blocks)):
        far, c = chip ^ (i % 4), core ^ (i // 4)
        outer[rows_from((2 * far + c) * half, half)] = piece[...].astype(WIDE)
        stage[c, far] = block[...]
    for c in range(2):
        for p in range(CHIPS):
            for k in range(4):
                start = k * width + p * part
                inner[c * half : (c + 1) * half, start : start + part] = stage[
                    c, p, :, k * part : (k + 1) * part
                ].astype(WIDE)


def unpack_rest(*refs):
    pieces, mats, vectors, (b_query, b_value, b_inner, stage, small) = (
        refs[:8],
        refs[8:12],
        refs[12:18],
        refs[18:],
    )
    core, _, _, chip, place = places()
    part = mats[0].shape[0]
    half = part // 2
    for i, piece in enumerate(pieces):
        far = chip ^ (i % 4)
        stage[core ^ (i // 4), far] = piece[:half]
        if i < 4:
            small[far] = piece[half:, :part].astype(WIDE)
    for c in range(2):
        for k in range(CHIPS):
            for j, out in enumerate(mats):
                out[c * half : (c + 1) * half, k * part : (k + 1) * part] = stage[
                    c, k, :, j * part : (j + 1) * part
                ].astype(WIDE)
    total = small[0] + small[1] + small[2] + small[3]
    for i, out in enumerate(vectors):
        out[...] = total[i]
    biases = small[place]
    b_query[...] = biases[7]
    b_value[...] = biases[8]
    for p in range(CHIPS):
        b_inner[p * part : (p + 1) * part] = small[p][6]


def per_device(
    inputs,
    segments,
    query_weight,
    query_bias,
    key_weight,
    value_weight,
    value_bias,
    output_weight,
    output_bias,
    first_gain,
    first_shift,
    inner_weight,
    inner_bias,
    outer_weight,
    outer_bias,
    second_gain,
    second_shift,
    cotangent,
):
    groups = lax.axis_size("ctx") // TEAM
    lines = [[m + TEAM * g for g in range(groups)] for m in range(TEAM)]
    tokens, width = inputs.shape[1:]
    part = query_weight.shape[0]
    hidden = outer_weight.shape[0]
    count, half = CHIPS * tokens, part // 2
    heads = part // HEAD_DIM

    def chips(block):
        return [partner(block, "ctx", s << 1) for s in (1, 2, 3)]

    def exchanged(blocks):
        return [partner(block, "ctx", (s + 1) << 1) for s, block in enumerate(blocks)]

    def joined(block):
        return partner(block, "ctx", CORE)

    (own,) = kernel(
        prepare_tokens,
        [shape((tokens + 16, width))],
        inputs,
        segments,
        scratch=[pltpu.VMEM((1, tokens), jnp.int32)],
        loads=2,
    )
    teams = [[c + TEAM * g + 2 * n for n in range(CHIPS)] for g in range(groups) for c in range(2)]
    seen = lax.all_gather(own, "ctx", axis_index_groups=teams)
    (first,) = kernel(
        prepare_weights,
        [shape((4 * half, width))],
        query_weight,
        key_weight,
        value_weight,
        output_weight,
        inner_weight,
        outer_weight,
        output_bias,
        first_gain,
        first_shift,
        outer_bias,
        second_gain,
        second_shift,
        inner_bias,
        query_bias,
        value_bias,
        scratch=[
            pltpu.VMEM((3, half, width), LOW),
            pltpu.VMEM((half, 4 * width), LOW),
            *[pltpu.VMEM((part,), LOW)] * 6,
            pltpu.VMEM((hidden,), LOW),
            *[pltpu.VMEM((part,), LOW)] * 2,
        ],
        loads=15,
    )
    (mine,) = kernel(first_rows, [shape((half, width))], first, after=(seen,))
    line = [first, partner(first, "fsdp", 1), partner(first, "fsdp", 2), partner(mine, "fsdp", 3)]
    projections, others, sent = kernel(
        sort_pieces,
        [shape((4, half, width)), shape((3, 3 * half, width)), shape((3 * half, width))],
        *line,
    )
    last = partner(sent, "fsdp", 1)

    rows_in, w_qkv, queries, kv_own, segs, vec, b_inner = kernel(
        project,
        [
            shape((count, width)),
            shape((width, 3 * part)),
            shape((count, part)),
            shape((count, 2 * part)),
            shape((8, tokens), WIDE),
            shape((8, width), WIDE),
            shape((1, width), WIDE),
        ],
        seen,
        projections,
        joined(projections),
        scratch=[pltpu.VMEM((4, 16, part), WIDE)],
    )
    kv_far, seg_far = partner(kv_own, "ctx", CORE), partner(segs, "ctx", CORE)
    if groups == 1:
        context, probs = kernel(
            attend_all,
            [shape((count, part)), shape((heads, 2 * count, count))],
            queries,
            kv_own,
            kv_far,
            segs,
            seg_far,
            scratch=[
                pltpu.VMEM((2 * count, 2 * part), LOW),
                pltpu.VMEM((2 * CHIPS, tokens), WIDE),
                pltpu.VMEM((1, count), WIDE),
            ],
            room=24,
        )
    else:
        kv = jnp.concatenate([kv_own, kv_far])
        seg_key = jnp.concatenate([segs[:CHIPS], seg_far[:CHIPS]])
        kv = lax.all_gather(kv, "ctx", axis=0, tiled=True, axis_index_groups=lines)
        seg_key = lax.all_gather(seg_key, "ctx", axis=0, tiled=True, axis_index_groups=lines)
        context, probs = attention(queries, segs[:CHIPS].reshape(1, count), kv, seg_key)

    contexts = [context] + chips(context)
    (last,) = kernel(passed, [shape(last.shape)], last, after=(context,))
    w_output, w_inner, w_outer = kernel(
        assemble, [shape((width, width))] * 3, others, last, joined(others), joined(last)
    )
    context_low, unit_one, inverse_one, normed_low, activated, slope, *outer_sent = kernel(
        forward,
        [
            shape((count, width)),
            shape((tokens, width), WIDE),
            shape((tokens, 1), WIDE),
            shape((count, width)),
            shape((count, width)),
            shape((count, width), WIDE),
            shape((tokens, width), WIDE),
        ]
        + [shape((tokens, width))] * 3,
        *contexts,
        rows_in,
        w_output,
        vec,
        w_inner,
        b_inner,
        w_outer,
        scratch=[pltpu.VMEM((CHIPS, count, part), LOW)],
        room=16,
    )
    result, grad_summed, grad_outer, sums_one = kernel(
        backward_first,
        [
            shape((1, tokens, width)),
            shape((tokens, width), WIDE),
            shape((tokens, width)),
            shape((8, width), WIDE),
        ],
        outer_sent[0],
        *exchanged(outer_sent[1:]),
        unit_one,
        vec,
        cotangent,
        last=(0,),
    )
    grad_outer, grad_inner, sums_inner, inner_own, *inner_sent = kernel(
        backward_second,
        [
            shape((count, width)),
            shape((count, width)),
            shape((1, width), WIDE),
            shape((tokens, width), WIDE),
        ]
        + [shape((tokens, width))] * 3,
        grad_outer,
        *chips(grad_outer),
        slope,
        w_outer,
        w_inner,
        room=12,
    )

    inner_far = exchanged(inner_sent)

    def near_sum(kept, sent):
        received = partner(sent, "ctx", CORE)
        return kernel(add_near, [shape((2,) + kept.shape[1:])] * 2, kept, received)

    def far_sum(kept, sent, after=()):
        received = partner(sent, "fsdp", 1)
        return kernel(add_far, [shape(kept.shape[1:])] * 2, kept, received, after=after)

    def last_sum(kept, sent, after=()):
        received = partner(sent, "fsdp", 2)
        (total,) = kernel(add_last, [shape(kept.shape)], kept, received, after=after)
        if groups > 1:
            total = lax.psum(total.astype(WIDE), "ctx", axis_index_groups=lines).astype(LOW)
        return total

    kept, sent = kernel(
        weight_grads,
        [shape((4, 2 * half, width))] * 2,
        activated,
        grad_outer,
        normed_low,
        grad_inner,
        scratch=[pltpu.VMEM((width, width), LOW)],
        room=12,
    )
    outer_kept, outer_sent, inner_kept, inner_sent = mlp_near = kernel(
        add_near_both, [shape((2, half, width))] * 4, kept, partner(sent, "ctx", CORE)
    )
    outer_kept, outer_sent, inner_sent = kernel(
        add_far_passing,
        [shape((half, width))] * 2 + [shape((2, half, width))],
        outer_kept,
        partner(outer_sent, "fsdp", 1),
        inner_sent,
    )
    outer_total = last_sum(outer_kept, outer_sent)
    mlp_far = far_sum(inner_kept, inner_sent)
    grad_residual, grad_low, sums_two = kernel(
        norm_backward,
        [shape((tokens, width), WIDE), shape((tokens, width)), shape((8, width), WIDE)],
        grad_summed,
        inner_own,
        *inner_far,
        unit_one,
        inverse_one,
        vec,
        after=tuple(mlp_near),
    )
    grads_low = [grad_low] + chips(grad_low)
    if groups == 1:
        grad_low, grad_queries, grad_kv, grad_kv_sent = kernel(
            attend_back_all,
            [
                shape((count, width)),
                shape((count, part)),
                shape((count, 2 * part), WIDE),
                shape((count, 2 * part)),
            ],
            queries,
            kv_own,
            kv_far,
            *grads_low,
            w_output,
            probs,
            scratch=[
                pltpu.VMEM((2 * count, 2 * part), LOW),
                pltpu.VMEM((count, part), LOW),
                pltpu.VMEM((2 * count, 2 * part), WIDE),
            ],
            room=24,
            after=(outer_total, *mlp_far),
        )
    else:
        grad_low, grad_context = kernel(
            context_back, [shape((count, width)), shape((count, part))], *grads_low, w_output
        )
        grad_queries, grad_kv = attention_back(queries, kv, grad_context, probs)
        grad_kv = grad_kv.reshape(groups, 2, count, 2 * part).transpose(1, 0, 2, 3)
        grad_kv = lax.psum_scatter(
            grad_kv.reshape(2, groups * count, 2 * part),
            "ctx",
            scatter_dimension=1,
            tiled=True,
            axis_index_groups=lines,
        )
        grad_kv, grad_kv_sent = grad_kv[0], grad_kv[1].astype(LOW)
    grad_kv_far = partner(grad_kv_sent, "ctx", CORE)
    (grad_o,) = kernel(output_grads, [shape((width, part))], context_low, grad_low)
    inner_total = last_sum(*mlp_far)
    cut = shape((4, half + 16, width))
    grad_qkv, rest_kept, rest_sent = kernel(
        projection_grads,
        [shape((count, 3 * part)), cut, cut],
        rows_in,
        grad_queries,
        grad_kv,
        grad_kv_far,
        grad_o,
        sums_one,
        sums_two,
        sums_inner,
        scratch=[pltpu.VMEM((width, width), LOW)],
    )
    rest_near = near_sum(rest_kept, rest_sent)
    input_own, *input_sent = kernel(
        input_grads,
        [shape((tokens, width), WIDE)] + [shape((tokens, width))] * 3,
        grad_qkv,
        w_qkv,
        grad_residual,
        after=tuple(rest_near),
    )
    input_far = exchanged(input_sent)

    outer_chips = [outer_total] + chips(outer_total)
    inner_chips = [inner_total] + chips(inner_total)
    rest_total = last_sum(
        *far_sum(*rest_near, after=(inner_total,)),
        after=(*outer_chips[1:], *inner_chips[1:], *input_far),
    )
    rest_chips = [rest_total] + chips(rest_total)
    (grad_input,) = kernel(
        add_tokens,
        [shape((1, tokens, width))],
        input_own,
        *input_far,
        last=(0,),
        after=(rest_total,),
    )
    g_outer, g_inner = kernel(
        unpack_mlp,
        [shape((hidden, width), WIDE), shape((part, 4 * hidden), WIDE)],
        *outer_chips,
        *map(joined, outer_chips),
        *inner_chips,
        *map(joined, inner_chips),
        last=(0, 1),
        scratch=[pltpu.VMEM((2, CHIPS, half, width), LOW)],
        room=12,
        after=(rest_total,),
    )
    g_query, g_key, g_value, g_output, *vec, g_b_query, g_b_value, g_b_inner = kernel(
        unpack_rest,
        [shape((part, width), WIDE)] * 4
        + [shape((part,), WIDE)] * 8
        + [shape((width,), WIDE)],
        *rest_chips,
        *map(joined, rest_chips),
        last=range(13),
        scratch=[
            pltpu.VMEM((2, CHIPS, half, width), LOW),
            pltpu.VMEM((CHIPS, 16, part), WIDE),
        ],
        room=12,
    )
    return (
        result,
        grad_input,
        g_query,
        g_b_query,
        g_key,
        g_value,
        g_b_value,
        g_output,
        vec[3],
        vec[4],
        vec[5],
        g_inner,
        g_b_inner,
        g_outer,
        vec[0],
        vec[1],
        vec[2],
    )


def solution(mesh):
    rows, cuts, whole = P("fsdp", "ctx", None), P("fsdp", None), P("fsdp")
    params = (cuts, whole, cuts, cuts, whole, cuts, whole, whole, whole)
    params += (cuts, whole, cuts, whole, whole, whole)
    return jax.shard_map(
        per_device,
        mesh=mesh,
        in_specs=(rows, P("fsdp", "ctx")) + params + (rows,),
        out_specs=(rows, rows) + params,
        check_vma=False,
    )
```

```python
import functools

import jax
import jax.numpy as jnp
from jax import lax
from jax.experimental import pallas as pl
from jax.experimental.pallas import tpu as pltpu
from jax.sharding import PartitionSpec as P

HEAD_DIM = 64
NEGATIVE = -1000000000.0
EPSILON = 1e-12
LOW = jnp.bfloat16
WIDE = jnp.float32

CORE, SIDE, ROW = 1, 2, 4
TEAM = 8
CHIPS = 4
VMEM_BYTES = 56 << 20


def partner(block, axis, bit):
    devices = range(lax.axis_size(axis))
    return lax.ppermute(block, axis, [(i, i ^ bit) for i in devices])


def dot(left, right):
    return jnp.dot(left, right, preferred_element_type=WIDE)


def dot_rt(left, right):
    return lax.dot_general(left, right, (((1,), (1,)), ((), ())), preferred_element_type=WIDE)


def dot_lt(left, right):
    return lax.dot_general(left, right, (((0,), (0,)), ((), ())), preferred_element_type=WIDE)


def shape(dims, dtype=LOW):
    return jax.ShapeDtypeStruct(tuple(dims), dtype)


def kernel(body, outs, *args, scratch=(), room=8, last=(), after=(), loads=0):
    spec = pl.BlockSpec(memory_space=pltpu.VMEM)
    off = pl.BlockSpec(memory_space=pl.ANY)
    place = pltpu.HBM if loads else pltpu.VMEM
    args = tuple(pltpu.with_memory_space_constraint(a, place) for a in args)
    waits = len(after)

    def step(*refs):
        body(*refs[waits:])

    sems = [pltpu.SemaphoreType.DMA((loads,))] if loads else []
    return pl.pallas_call(
        step,
        out_shape=[
            o if n in last else pltpu.VMEM(o.shape, o.dtype) for n, o in enumerate(outs)
        ],
        in_specs=[off] * waits + [off if loads else spec] * len(args),
        out_specs=[spec] * len(outs),
        scratch_shapes=list(scratch) + sems,
        compiler_params=pltpu.CompilerParams(vmem_limit_bytes=room << 20),
        cost_estimate=pl.CostEstimate(flops=1, bytes_accessed=1, transcendentals=0),
    )(*after, *args)


def load(sems, *pairs):
    copies = [
        pltpu.make_async_copy(source, target, sems.at[n])
        for n, (source, target) in enumerate(pairs)
    ]
    for copy in copies:
        copy.start()
    return copies


def places():
    index, place = lax.axis_index("ctx"), lax.axis_index("fsdp")
    core, side, row = index & 1, (index >> 1) & 1, (index >> 2) & 1
    return core, side, row, (index >> 1) & 3, place


def rows_from(start, count):
    return pl.ds(pl.multiple_of(start, 16), count)


def normalized(values):
    center = values - jnp.mean(values, -1, keepdims=True)
    inverse = lax.rsqrt(jnp.mean(center * center, -1, keepdims=True) + EPSILON)
    return center * inverse, inverse


def norm_back(grad, unit, inverse, gain):
    scaled = grad * gain
    return inverse * (
        scaled
        - jnp.mean(scaled, -1, keepdims=True)
        - unit * jnp.mean(scaled * unit, -1, keepdims=True)
    )


def lines_of(*vectors):
    rows = [v[...].astype(WIDE).reshape(1, v.shape[0]) for v in vectors]
    return jnp.concatenate(rows + [jnp.zeros((16 - len(rows), rows[0].shape[1]), WIDE)])


def prepare_tokens(x, seg, own, line, sems):
    tokens, width = x.shape[1:]
    for copy in load(sems, (seg, line), (x.at[0], own.at[pl.ds(0, tokens)])):
        copy.wait()
    seg_row = jnp.broadcast_to(line[...].astype(WIDE), (16, tokens)).astype(LOW)
    own[tokens:, :tokens] = seg_row
    own[tokens:, tokens:] = jnp.zeros((16, width - tokens), LOW)


def prepare_weights(wq, wk, wv, wo, wi, wu, *refs):
    vectors, first, (blocks, block), lines, sems = (
        refs[:9],
        refs[9],
        refs[10:12],
        refs[12:21],
        refs[21],
    )
    core, _, _, chip, _ = places()
    part, width = wq.shape
    half = part // 2
    rows = rows_from(core * half, half)
    pairs = [(w.at[rows], blocks.at[j]) for j, w in enumerate((wq, wk, wv))]
    pairs += [(wi.at[rows], block), (wo.at[rows], first.at[pl.ds(half, half)])]
    rows = rows_from((2 * chip + core) * half, half)
    pairs += [(wu.at[rows], first.at[pl.ds(3 * half, half)])]
    for copy in load(sems, *pairs, *zip(vectors, lines)):
        copy.wait()
    six, bias_inner, biases = lines_of(*lines[:6]), lines_of(lines[6]), lines_of(*lines[7:])
    for p in range(CHIPS):

        @pl.when(chip == p)
        def _():
            span = slice(p * part, (p + 1) * part)
            for j in range(3):
                first[:half, j * part : (j + 1) * part] = blocks[j, :, span]
            for k in range(4):
                start = k * width + p * part
                first[2 * half : 3 * half, k * part : (k + 1) * part] = block[
                    :, start : start + part
                ]
            small = [six[:6], bias_inner[:1, span], biases[:2], jnp.zeros((half - 9, part), WIDE)]
            first[:half, 3 * part :] = jnp.concatenate(small).astype(LOW)


def first_rows(block, out):
    out[...] = block[: out.shape[0]]


def passed(block, out):
    out[...] = block[...]


def split_rows(block, *outs):
    n = outs[0].shape[0]
    for m, out in enumerate(outs):
        out[...] = block[m * n : (m + 1) * n]


def sort_pieces(own, near, far, farthest, projections, others, sent):
    half = farthest.shape[0]
    for r, piece in enumerate((own, near, far, farthest)):
        projections[r] = piece[:half]
    for r, piece in enumerate((own, near, far)):
        others[r] = piece[half:]
    sent[...] = far[half:]


def assemble(*refs):
    own, own_last, other, other_last, weights = refs[0], refs[1:4], refs[4], refs[5:8], refs[8:]
    core, _, _, _, place = places()
    half = weights[0].shape[0] // 8
    for c, (pieces, last) in enumerate(((own, own_last), (other, other_last))):
        for r in range(4):
            base = rows_from((2 * (place ^ r) + (core ^ c)) * half, half)
            for m, weight in enumerate(weights):
                weight[base] = last[m][...] if r == 3 else pieces[r, m * half : (m + 1) * half]


def stack(own, near, far, farthest, out):
    for r, piece in enumerate((own, near, far, farthest)):
        out[r] = piece[...]


def project(seen, *refs):
    pieces, outs = refs[:2], refs[2:]
    rows_in, w_qkv, queries, keys_values, segs, vec, b_inner, stage = outs
    core, _, _, chip, place = places()
    width = seen.shape[2]
    tokens = rows_in.shape[0] // CHIPS
    part, half = width // 4, width // 8
    for s in range(CHIPS):
        x = seen.at[chip ^ s]
        rows_in[s * tokens : (s + 1) * tokens] = x[:tokens]
        segs[s : s + 1] = x[tokens : tokens + 1, :tokens].astype(WIDE)
    segs[CHIPS:] = jnp.zeros((8 - CHIPS, tokens), WIDE)
    for r in range(4):
        for c, piece in enumerate(pieces):
            base = rows_from((2 * (place ^ r) + (core ^ c)) * half, half)
            w_qkv[base] = piece[r, :, : 3 * part]
        stage[place ^ r] = pieces[0][r, :16, 3 * part :].astype(WIDE)
    for k in range(4):
        span = slice(k * part, (k + 1) * part)
        vec[:6, span] = stage[k, :6]
        b_inner[:, span] = stage[k, 6:7]
    vec[6:] = jnp.zeros((2, width), WIDE)
    bias = stage[chip]
    out = dot(rows_in[...], w_qkv[...])
    scale = HEAD_DIM ** (-0.5)
    queries[...] = ((out[:, :part] + bias[7:8]).astype(LOW).astype(WIDE) * scale).astype(LOW)
    keys_values[:, :part] = out[:, part : 2 * part].astype(LOW)
    keys_values[:, part:] = (out[:, 2 * part :] + bias[8:9]).astype(LOW)


def attend(queries, seg_query, keys_values, seg_key, context, probs):
    part = queries.shape[1]
    seg_columns = seg_key[...].T
    seg_row = seg_query[...]
    allowed = jnp.concatenate(
        [seg_columns[:, b : b + 1] == seg_row for b in range(seg_key.shape[0])]
    )
    for h in range(part // HEAD_DIM):
        keys = keys_values[:, h * HEAD_DIM : (h + 1) * HEAD_DIM]
        values = keys_values[:, part + h * HEAD_DIM : part + (h + 1) * HEAD_DIM]
        scores = dot_rt(keys, queries[:, h * HEAD_DIM : (h + 1) * HEAD_DIM])
        scores = jnp.where(allowed, scores, NEGATIVE)
        weights = jnp.exp(scores - jnp.max(scores, 0, keepdims=True))
        weights = (weights * (1.0 / jnp.sum(weights, 0, keepdims=True))).astype(LOW)
        probs[h] = weights
        out = dot_lt(values, weights)
        context[:, h * HEAD_DIM : (h + 1) * HEAD_DIM] = out.T.astype(LOW)


def attend_back(queries, keys_values, grad_context, probs, grad_queries, grad_keys_values):
    part = queries.shape[1]
    scale = HEAD_DIM ** (-0.5)
    for h in range(part // HEAD_DIM):
        span = slice(h * HEAD_DIM, (h + 1) * HEAD_DIM)
        span_v = slice(part + h * HEAD_DIM, part + (h + 1) * HEAD_DIM)
        keys, values = keys_values[:, span], keys_values[:, span_v]
        grads = grad_context[:, span]
        soft = probs[h]
        grad_keys_values[:, span_v] += dot(soft, grads)
        grad_probs = dot_rt(values, grads)
        wide = soft.astype(WIDE)
        delta = jnp.sum(wide * grad_probs, 0, keepdims=True)
        grad_scores = (wide * (grad_probs - delta)).astype(LOW)
        grad_queries[:, span] = (dot_lt(keys, grad_scores) * scale).T.astype(LOW)
        grad_keys_values[:, span] += dot(grad_scores, queries[:, span])


def beside(rows, out):
    tokens, part = out.shape[0], rows.shape[1]
    for t in range(CHIPS):
        out[:, t * part : (t + 1) * part] = rows[t * tokens : (t + 1) * tokens]


def attend_all(queries, kv_own, kv_far, seg_own, seg_far, context, probs, *scratch):
    keys_values, seg_key, seg_query, rows = scratch
    count = kv_own.shape[0]
    tokens = seg_own.shape[1]
    keys_values[:count] = kv_own[...]
    keys_values[count:] = kv_far[...]
    seg_key[:CHIPS] = seg_own[:CHIPS]
    seg_key[CHIPS:] = seg_far[:CHIPS]
    for s in range(CHIPS):
        seg_query[:, s * tokens : (s + 1) * tokens] = seg_own[s : s + 1]
    attend(queries, seg_query, keys_values, seg_key, rows, probs)
    beside(rows, context)


def context_back(g0, g1, g2, g3, w_output, grad_low, grad_context):
    _, _, _, chip, _ = places()
    tokens, part = g0.shape[0], grad_context.shape[1]
    for s, block in enumerate((g0, g1, g2, g3)):
        grad_low[s * tokens : (s + 1) * tokens] = block[...]
    grad_context[...] = dot_rt(grad_low[...], w_output[rows_from(chip * part, part)]).astype(LOW)


def attend_back_all(queries, kv_own, kv_far, g0, g1, g2, g3, w_output, probs, *refs):
    grad_low, grad_queries, grad_own, *grad_far, keys_values, grad_context, total = refs
    count = kv_own.shape[0]
    keys_values[:count] = kv_own[...]
    keys_values[count:] = kv_far[...]
    context_back(g0, g1, g2, g3, w_output, grad_low, grad_context)
    total[...] = jnp.zeros(total.shape, WIDE)
    attend_back(queries, keys_values, grad_context, probs, grad_queries, total)
    grad_own[...] = total[:count]
    tokens = count // CHIPS
    for t, out in enumerate(grad_far):
        out[...] = total[count + t * tokens : count + (t + 1) * tokens].astype(LOW)


def attend_back_block(queries, keys_values, grads, probs, grad_queries, grad_keys_values):
    @pl.when(pl.program_id(0) == 0)
    def _():
        grad_keys_values[...] = jnp.zeros(grad_keys_values.shape, WIDE)

    attend_back(queries, keys_values, grads, probs, grad_queries, grad_keys_values)


def attention_block(queries, keys_values):
    return min(queries.shape[0], 128 * max(1, 2048 // keys_values.shape[0]))


def whole(array):
    return pl.BlockSpec(array.shape, lambda i: (0,) * array.ndim)


def attention(queries, seg_query, keys_values, seg_key):
    count, part = queries.shape
    keys = keys_values.shape[0]
    heads = part // HEAD_DIM
    block = attention_block(queries, keys_values)
    return pl.pallas_call(
        attend,
        grid=(count // block,),
        in_specs=[
            pl.BlockSpec((block, part), lambda i: (i, 0)),
            pl.BlockSpec((1, block), lambda i: (0, i)),
            whole(keys_values),
            whole(seg_key),
        ],
        out_specs=[
            pl.BlockSpec((block, part), lambda i: (i, 0)),
            pl.BlockSpec((heads, keys, block), lambda i: (0, 0, i)),
        ],
        out_shape=[shape((count, part)), shape((heads, keys, count))],
        compiler_params=pltpu.CompilerParams(vmem_limit_bytes=VMEM_BYTES),
    )(queries, seg_query, keys_values, seg_key)


def attention_back(queries, keys_values, grad_context, probs):
    count, part = queries.shape
    keys = keys_values.shape[0]
    block = attention_block(queries, keys_values)
    rows = pl.BlockSpec((block, part), lambda i: (i, 0))
    return pl.pallas_call(
        attend_back_block,
        grid=(count // block,),
        in_specs=[
            rows,
            whole(keys_values),
            rows,
            pl.BlockSpec((probs.shape[0], keys, block), lambda i: (0, 0, i)),
        ],
        out_specs=[rows, pl.BlockSpec((keys, 2 * part), lambda i: (0, 0))],
        out_shape=[shape((count, part)), shape((keys, 2 * part), WIDE)],
        compiler_params=pltpu.CompilerParams(vmem_limit_bytes=VMEM_BYTES),
    )(queries, keys_values, grad_context, probs)


def forward(c0, c1, c2, c3, rows_in, w_output, vec, w_inner, b_inner, w_outer, *outs):
    context_low, unit_one, inverse_one, normed_low, activated, slope = outs[:6]
    own, sent, stage = outs[6], outs[7:10], outs[10]
    _, _, _, chip, _ = places()
    tokens, part = c0.shape[0], c0.shape[1] // CHIPS
    for s, block in enumerate((c0, c1, c2, c3)):
        for t in range(CHIPS):
            stage[chip ^ s, t * tokens : (t + 1) * tokens] = block[
                :, (t ^ s) * part : ((t ^ s) + 1) * part
            ]
    for k in range(CHIPS):
        context_low[:, k * part : (k + 1) * part] = stage[k]
    residual = rows_in[...].astype(WIDE) + dot(context_low[...], w_output[...]) + vec[0:1]
    unit, inverse = normalized(residual)
    unit_one[...] = unit[:tokens]
    inverse_one[...] = inverse[:tokens]
    normed_low[...] = (unit * vec[1:2] + vec[2:3]).astype(LOW)
    inner_pre = dot(normed_low[...], w_inner[...]) + b_inner[...]
    cdf = 0.5 * (1.0 + lax.erf(inner_pre * (0.5**0.5)))
    activated[...] = (inner_pre * cdf).astype(LOW)
    slope[...] = cdf + inner_pre * jnp.exp(-0.5 * inner_pre * inner_pre) * 0.3989422804014327
    parted(dot(activated[...], w_outer[...]), own, sent)


def parted(values, own, sent):
    tokens = own.shape[0]
    own[...] = values[:tokens]
    for s, out in enumerate(sent):
        out[...] = values[(s + 1) * tokens : (s + 2) * tokens].astype(LOW)


def total_of(own, blocks):
    total = own[...]
    for block in blocks:
        total = total + block[...].astype(WIDE)
    return total


def backward_first(own, s1, s2, s3, unit_one, vec, cot, result, grad_summed, grad_outer, sums):
    summed = unit_one[...] * vec[1:2] + vec[2:3] + vec[3:4] + total_of(own, (s1, s2, s3))
    unit, inverse = normalized(summed)
    result[0] = (unit * vec[4:5] + vec[5:6]).astype(LOW)
    c = cot[0].astype(WIDE)
    grad = norm_back(c, unit, inverse, vec[4:5])
    grad_summed[...] = grad
    grad_outer[...] = grad.astype(LOW)
    sums[0:1] = jnp.sum(grad_outer[...].astype(WIDE), 0, keepdims=True)
    sums[1:2] = jnp.sum(c * unit, 0, keepdims=True)
    sums[2:3] = jnp.sum(c, 0, keepdims=True)
    sums[3:] = jnp.zeros((5, sums.shape[1]), WIDE)


def backward_second(g0, g1, g2, g3, slope, w_outer, w_inner, grad_inner, sums, *outs):
    grad_outer = jnp.concatenate([g0[...], g1[...], g2[...], g3[...]])
    grad_inner[...] = (dot_rt(grad_outer, w_outer[...]) * slope[...]).astype(LOW)
    parted(dot_rt(grad_inner[...], w_inner[...]), outs[0], outs[1:])
    sums[...] = jnp.sum(grad_inner[...].astype(WIDE), 0, keepdims=True)


def cut_rows(stage, keep, sent):
    core, _, _, _, place = places()
    half = keep.shape[1]
    for r in range(4):
        for c, out in enumerate((keep.at[r], sent[r])):
            out[...] = stage[rows_from((2 * (place ^ r) + (core ^ c)) * half, half)]


def outer_grads(activated, g0, g1, g2, g3, keep, send, stage):
    grad_outer = jnp.concatenate([g0[...], g1[...], g2[...], g3[...]])
    stage[...] = dot_lt(activated[...], grad_outer).astype(LOW)
    cut_rows(stage, keep, [send.at[r] for r in range(4)])


def inner_grads(normed_low, grad_inner, keep, s0, s1, s2, s3, stage):
    stage[...] = dot_lt(normed_low[...], grad_inner[...]).astype(LOW)
    cut_rows(stage, keep, (s0, s1, s2, s3))


def norm_backward(grad_summed, own, s1, s2, s3, unit_one, inverse_one, vec, grad_own, grad_low, sums):
    grad = grad_summed[...] + total_of(own, (s1, s2, s3))
    unit = unit_one[...]
    branch = norm_back(grad, unit, inverse_one[...], vec[1:2])
    grad_own[...] = branch
    grad_low[...] = branch.astype(LOW)
    sums[0:1] = jnp.sum(grad_low[...].astype(WIDE), 0, keepdims=True)
    sums[1:2] = jnp.sum(grad * unit, 0, keepdims=True)
    sums[2:3] = jnp.sum(grad, 0, keepdims=True)
    sums[3:] = jnp.zeros((5, sums.shape[1]), WIDE)


def output_grads(context_low, grad_low, out):
    _, _, _, chip, _ = places()
    part = out.shape[1]
    for p in range(CHIPS):

        @pl.when(chip == p)
        def _():
            block = grad_low[:, p * part : (p + 1) * part]
            out[...] = dot_lt(context_low[...], block).astype(LOW)


def projection_grads(rows_in, grad_queries, grad_kv, f0, f1, f2, f3, grad_o, *refs):
    (sums_one, sums_two, sums_inner), outs = refs[:3], refs[3:]
    grad_qkv, keep, send, stage = outs
    core, _, _, _, place = places()
    part = grad_queries.shape[1]
    width = 4 * part
    grad_qkv[:, :part] = grad_queries[...]
    far = jnp.concatenate([f0[...], f1[...], f2[...], f3[...]]).astype(WIDE)
    grad_qkv[:, part:] = (grad_kv[...] + far).astype(LOW)
    stage[:, : 3 * part] = dot_lt(rows_in[...], grad_qkv[...]).astype(LOW)
    stage[:, 3 * part :] = grad_o[...]
    half = part // 2
    total = jnp.sum(grad_qkv[...].astype(WIDE), 0, keepdims=True)
    for k in range(4):
        span = slice(k * part, (k + 1) * part)
        small = jnp.concatenate(
            [
                sums_one[:3, span],
                sums_two[:3, span],
                sums_inner[:, span],
                total[:, :part],
                total[:, 2 * part :],
                jnp.zeros((7, part), WIDE),
            ]
        )
        small = jnp.concatenate([small, jnp.zeros((16, width - part), WIDE)], 1).astype(LOW)
        for c, out in enumerate((keep, send)):
            out[place ^ k, half:] = small
            out[place ^ k, :half] = stage[rows_from(k * part + (core ^ c) * half, half)]


def input_grads(grad_qkv, w_qkv, grad_residual, own, s1, s2, s3):
    tokens = own.shape[0]
    grads = dot_rt(grad_qkv[...], w_qkv[...])
    parted(grads, own, (s1, s2, s3))
    own[...] += grad_residual[...]


def add_tokens(own, s1, s2, s3, out, done):
    done[...] = jnp.zeros(done.shape, WIDE)
    out[0] = total_of(own, (s1, s2, s3)).astype(LOW)


def add_near(kept, received, keep, send):
    total = kept[...].astype(WIDE) + received[...].astype(WIDE)
    for r in range(2):
        keep[r] = total[2 * r].astype(LOW)
        send[r] = total[2 * r + 1].astype(LOW)


def add_near_parts(kept, r0, r1, r2, r3, keep, send):
    for r, received in enumerate((r0, r1, r2, r3)):
        out = (keep, send)[r % 2]
        out[r // 2] = (kept[r].astype(WIDE) + received[...].astype(WIDE)).astype(LOW)


def add_far(kept, received, keep, send):
    total = kept[...].astype(WIDE) + received[...].astype(WIDE)
    keep[...] = total[0].astype(LOW)
    send[...] = total[1].astype(LOW)


def add_far_passing(kept, received, other, keep, send, out):
    add_far(kept, received, keep, send)
    out[...] = other[...]


def add_last(kept, received, out):
    out[...] = (kept[...].astype(WIDE) + received[...].astype(WIDE)).astype(LOW)


def add_beside(other, kept, received, out):
    half = kept.shape[0]
    out[:half] = other[...]
    add_last(kept, received, out.at[half:])


def unpack_mlp(own, other, outer, inner, done, stage):
    core, _, _, chip, _ = places()
    half, width = own.shape[1] // 2, own.shape[2]
    part = 2 * half
    for s in range(CHIPS):
        for m, blocks in enumerate((own, other)):
            far, c = chip ^ s, core ^ m
            outer[rows_from((2 * far + c) * half, half)] = blocks[s, :half].astype(WIDE)
            stage[c, far] = blocks[s, half:]
    for c in range(2):
        for p in range(CHIPS):
            for k in range(4):
                start = k * width + p * part
                inner[c * half : (c + 1) * half, start : start + part] = stage[
                    c, p, :, k * part : (k + 1) * part
                ].astype(WIDE)
    done[...] = jnp.zeros(done.shape, WIDE)


def unpack_rest(*refs):
    pieces, mats, vectors, (b_query, b_value, b_inner, stage, small) = (
        refs[:2],
        refs[2:6],
        refs[6:12],
        refs[12:],
    )
    core, _, _, chip, place = places()
    part = mats[0].shape[0]
    half = part // 2
    for s in range(CHIPS):
        for m, blocks in enumerate(pieces):
            stage[core ^ m, s] = blocks[s, :half]
        small[s] = pieces[0][s, half:, :part].astype(WIDE)
    for c in range(2):
        for k in range(CHIPS):
            for j, out in enumerate(mats):
                out[c * half : (c + 1) * half, k * part : (k + 1) * part] = stage[
                    c, k, :, j * part : (j + 1) * part
                ].astype(WIDE)
    total = small[0] + small[1] + small[2] + small[3]
    for i, out in enumerate(vectors):
        out[...] = total[i]
    biases = small[place]
    b_query[...] = biases[7]
    b_value[...] = biases[8]
    for p in range(CHIPS):
        b_inner[p * part : (p + 1) * part] = small[p][6]


def per_device(
    inputs,
    segments,
    query_weight,
    query_bias,
    key_weight,
    value_weight,
    value_bias,
    output_weight,
    output_bias,
    first_gain,
    first_shift,
    inner_weight,
    inner_bias,
    outer_weight,
    outer_bias,
    second_gain,
    second_shift,
    cotangent,
):
    groups = lax.axis_size("ctx") // TEAM
    lines = [[m + TEAM * g for g in range(groups)] for m in range(TEAM)]
    tokens, width = inputs.shape[1:]
    part = query_weight.shape[0]
    hidden = outer_weight.shape[0]
    count, half = CHIPS * tokens, part // 2
    heads = part // HEAD_DIM

    def chips(block):
        return [partner(block, "ctx", s << 1) for s in (1, 2, 3)]

    def exchanged(blocks):
        return [partner(block, "ctx", (s + 1) << 1) for s, block in enumerate(blocks)]

    def joined(block):
        return partner(block, "ctx", CORE)

    (own,) = kernel(
        prepare_tokens,
        [shape((tokens + 16, width))],
        inputs,
        segments,
        scratch=[pltpu.VMEM((1, tokens), jnp.int32)],
        loads=2,
    )
    teams = [[c + TEAM * g + 2 * n for n in range(CHIPS)] for g in range(groups) for c in range(2)]
    seen = lax.all_gather(own, "ctx", axis_index_groups=teams)
    (first,) = kernel(
        prepare_weights,
        [shape((4 * half, width))],
        query_weight,
        key_weight,
        value_weight,
        output_weight,
        inner_weight,
        outer_weight,
        output_bias,
        first_gain,
        first_shift,
        outer_bias,
        second_gain,
        second_shift,
        inner_bias,
        query_bias,
        value_bias,
        scratch=[
            pltpu.VMEM((3, half, width), LOW),
            pltpu.VMEM((half, 4 * width), LOW),
            *[pltpu.VMEM((part,), LOW)] * 6,
            pltpu.VMEM((hidden,), LOW),
            *[pltpu.VMEM((part,), LOW)] * 2,
        ],
        loads=15,
    )
    (mine,) = kernel(first_rows, [shape((half, width))], first, after=(seen,))
    line = [first, partner(first, "fsdp", 1), partner(first, "fsdp", 2), partner(mine, "fsdp", 3)]
    projections, others, sent = kernel(
        sort_pieces,
        [shape((4, half, width)), shape((3, 3 * half, width)), shape((3 * half, width))],
        *line,
    )
    last = partner(sent, "fsdp", 1)

    rows_in, w_qkv, queries, kv_own, segs, vec, b_inner = kernel(
        project,
        [
            shape((count, width)),
            shape((width, 3 * part)),
            shape((count, part)),
            shape((count, 2 * part)),
            shape((8, tokens), WIDE),
            shape((8, width), WIDE),
            shape((1, width), WIDE),
        ],
        seen,
        projections,
        joined(projections),
        scratch=[pltpu.VMEM((4, 16, part), WIDE)],
    )
    kv_far, seg_far = partner(kv_own, "ctx", CORE), partner(segs, "ctx", CORE)
    if groups == 1:
        context, probs = kernel(
            attend_all,
            [shape((tokens, width)), shape((heads, 2 * count, count))],
            queries,
            kv_own,
            kv_far,
            segs,
            seg_far,
            scratch=[
                pltpu.VMEM((2 * count, 2 * part), LOW),
                pltpu.VMEM((2 * CHIPS, tokens), WIDE),
                pltpu.VMEM((1, count), WIDE),
                pltpu.VMEM((count, part), LOW),
            ],
            room=24,
        )
    else:
        kv = jnp.concatenate([kv_own, kv_far])
        seg_key = jnp.concatenate([segs[:CHIPS], seg_far[:CHIPS]])
        kv = lax.all_gather(kv, "ctx", axis=0, tiled=True, axis_index_groups=lines)
        seg_key = lax.all_gather(seg_key, "ctx", axis=0, tiled=True, axis_index_groups=lines)
        rows, probs = attention(queries, segs[:CHIPS].reshape(1, count), kv, seg_key)
        (context,) = kernel(beside, [shape((tokens, width))], rows)

    contexts = [context] + chips(context)
    last = kernel(
        split_rows, [shape((half, width))] * 3, last, after=(context,)
    )
    w_output, w_inner, w_outer = kernel(
        assemble, [shape((width, width))] * 3, others, *last, joined(others), *map(joined, last)
    )
    context_low, unit_one, inverse_one, normed_low, activated, slope, *outer_sent = kernel(
        forward,
        [
            shape((count, width)),
            shape((tokens, width), WIDE),
            shape((tokens, 1), WIDE),
            shape((count, width)),
            shape((count, width)),
            shape((count, width), WIDE),
            shape((tokens, width), WIDE),
        ]
        + [shape((tokens, width))] * 3,
        *contexts,
        rows_in,
        w_output,
        vec,
        w_inner,
        b_inner,
        w_outer,
        scratch=[pltpu.VMEM((CHIPS, count, part), LOW)],
        room=16,
    )
    result, grad_summed, grad_outer, sums_one = kernel(
        backward_first,
        [
            shape((1, tokens, width)),
            shape((tokens, width), WIDE),
            shape((tokens, width)),
            shape((8, width), WIDE),
        ],
        outer_sent[0],
        *exchanged(outer_sent[1:]),
        unit_one,
        vec,
        cotangent,
        last=(0,),
    )
    grads_outer = [grad_outer] + chips(grad_outer)
    outer_kept, outer_sent = kernel(
        outer_grads,
        [shape((4, half, width))] * 2,
        activated,
        *grads_outer,
        scratch=[pltpu.VMEM((width, width), LOW)],
    )
    grad_inner, sums_inner, inner_own, *inner_sent = kernel(
        backward_second,
        [shape((count, width)), shape((1, width), WIDE), shape((tokens, width), WIDE)]
        + [shape((tokens, width))] * 3,
        *grads_outer,
        slope,
        w_outer,
        w_inner,
        room=12,
    )
    inner_far = exchanged(inner_sent)

    def near_sum(kept, sent):
        received = partner(sent, "ctx", CORE)
        return kernel(add_near, [shape((2,) + kept.shape[1:])] * 2, kept, received)

    def far_sum(kept, sent, after=()):
        received = partner(sent, "fsdp", 1)
        return kernel(add_far, [shape(kept.shape[1:])] * 2, kept, received, after=after)

    def last_sum(kept, sent, after=()):
        received = partner(sent, "fsdp", 2)
        (total,) = kernel(add_last, [shape(kept.shape)], kept, received, after=after)
        if groups > 1:
            total = lax.psum(total.astype(WIDE), "ctx", axis_index_groups=lines).astype(LOW)
        return total

    inner_kept, *inner_sent = kernel(
        inner_grads,
        [shape((4, half, width))] + [shape((half, width))] * 4,
        normed_low,
        grad_inner,
        scratch=[pltpu.VMEM((width, width), LOW)],
    )
    inner_kept, inner_sent = kernel(
        add_near_parts,
        [shape((2, half, width))] * 2,
        inner_kept,
        *(partner(block, "ctx", CORE) for block in inner_sent),
    )
    outer_kept, outer_sent = near_sum(outer_kept, outer_sent)
    outer_kept, outer_sent, inner_sent = kernel(
        add_far_passing,
        [shape((half, width))] * 2 + [shape((2, half, width))],
        outer_kept,
        partner(outer_sent, "fsdp", 1),
        inner_sent,
    )
    inner_far_sum = far_sum(inner_kept, inner_sent)
    outer_total = last_sum(outer_kept, outer_sent)
    grad_residual, grad_low, sums_two = kernel(
        norm_backward,
        [shape((tokens, width), WIDE), shape((tokens, width)), shape((8, width), WIDE)],
        grad_summed,
        inner_own,
        *inner_far,
        unit_one,
        inverse_one,
        vec,
    )
    grads_low = [grad_low] + chips(grad_low)
    if groups == 1:
        grad_low, grad_queries, grad_kv, *grad_kv_sent = kernel(
            attend_back_all,
            [
                shape((count, width)),
                shape((count, part)),
                shape((count, 2 * part), WIDE),
            ]
            + [shape((tokens, 2 * part))] * CHIPS,
            queries,
            kv_own,
            kv_far,
            *grads_low,
            w_output,
            probs,
            scratch=[
                pltpu.VMEM((2 * count, 2 * part), LOW),
                pltpu.VMEM((count, part), LOW),
                pltpu.VMEM((2 * count, 2 * part), WIDE),
            ],
            room=24,
            after=(outer_kept,),
        )
    else:
        grad_low, grad_context = kernel(
            context_back, [shape((count, width)), shape((count, part))], *grads_low, w_output
        )
        grad_queries, grad_kv = attention_back(queries, kv, grad_context, probs)
        grad_kv = grad_kv.reshape(groups, 2, count, 2 * part).transpose(1, 0, 2, 3)
        grad_kv = lax.psum_scatter(
            grad_kv.reshape(2, groups * count, 2 * part),
            "ctx",
            scatter_dimension=1,
            tiled=True,
            axis_index_groups=lines,
        )
        grad_kv, grad_kv_sent = grad_kv[0], jnp.split(grad_kv[1].astype(LOW), CHIPS)
    grad_kv_far = [joined(block) for block in grad_kv_sent]
    (grad_o,) = kernel(output_grads, [shape((width, part))], context_low, grad_low)
    cut = shape((4, half + 16, width))
    grad_qkv, rest_kept, rest_sent = kernel(
        projection_grads,
        [shape((count, 3 * part)), cut, cut],
        rows_in,
        grad_queries,
        grad_kv,
        *grad_kv_far,
        grad_o,
        sums_one,
        sums_two,
        sums_inner,
        scratch=[pltpu.VMEM((width, width), LOW)],
        after=(outer_total, inner_far_sum[0]),
    )
    rest_near = near_sum(rest_kept, rest_sent)
    input_own, *input_sent = kernel(
        input_grads,
        [shape((tokens, width), WIDE)] + [shape((tokens, width))] * 3,
        grad_qkv,
        w_qkv,
        grad_residual,
        after=tuple(rest_near),
    )
    input_far = exchanged(input_sent)

    def shared(total, after=()):
        (found,) = kernel(stack, [shape((CHIPS,) + total.shape)], total, *chips(total), after=after)
        return found, joined(found)

    rest_far = far_sum(*rest_near)
    (mlp_total,) = kernel(
        add_beside,
        [shape((2 * half, width))],
        outer_total,
        inner_far_sum[0],
        partner(inner_far_sum[1], "fsdp", 2),
        after=(*input_far, rest_far[0]),
    )
    rest_total = last_sum(*rest_far)
    rest_all = lax.all_gather(rest_total, "ctx", axis_index_groups=teams)
    mlp_blocks = shared(mlp_total, after=(rest_all,))
    grad_input, done_input = kernel(
        add_tokens,
        [shape((1, tokens, width)), shape((8, 128), WIDE)],
        input_own,
        *input_far,
        last=(0,),
        after=(rest_total,),
    )
    g_outer, g_inner, done_mlp = kernel(
        unpack_mlp,
        [
            shape((hidden, width), WIDE),
            shape((part, 4 * hidden), WIDE),
            shape((8, 128), WIDE),
        ],
        *mlp_blocks,
        last=(0, 1),
        scratch=[pltpu.VMEM((2, CHIPS, half, width), LOW)],
        room=12,
        after=(rest_all,),
    )
    g_query, g_key, g_value, g_output, *vec, g_b_query, g_b_value, g_b_inner = kernel(
        unpack_rest,
        [shape((part, width), WIDE)] * 4
        + [shape((part,), WIDE)] * 8
        + [shape((width,), WIDE)],
        rest_all,
        joined(rest_all),
        last=range(13),
        scratch=[
            pltpu.VMEM((2, CHIPS, half, width), LOW),
            pltpu.VMEM((CHIPS, 16, part), WIDE),
        ],
        room=12,
    )
    return (
        result,
        grad_input,
        g_query,
        g_b_query,
        g_key,
        g_value,
        g_b_value,
        g_output,
        vec[3],
        vec[4],
        vec[5],
        g_inner,
        g_b_inner,
        g_outer,
        vec[0],
        vec[1],
        vec[2],
    )


def solution(mesh):
    rows, cuts, whole = P("fsdp", "ctx", None), P("fsdp", None), P("fsdp")
    params = (cuts, whole, cuts, cuts, whole, cuts, whole, whole, whole)
    params += (cuts, whole, cuts, whole, whole, whole)
    return jax.shard_map(
        per_device,
        mesh=mesh,
        in_specs=(rows, P("fsdp", "ctx")) + params + (rows,),
        out_specs=(rows, rows) + params,
        check_vma=False,
    )
```

```python
import functools

import jax
import jax.numpy as jnp
from jax import lax
from jax.experimental import pallas as pl
from jax.experimental.pallas import tpu as pltpu
from jax.sharding import PartitionSpec as P

HEAD_DIM = 64
NEGATIVE = -1000000000.0
EPSILON = 1e-12
LOW = jnp.bfloat16
WIDE = jnp.float32

CORE, SIDE, ROW = 1, 2, 4
TEAM = 8
CHIPS = 4
VMEM_BYTES = 56 << 20


def partner(block, axis, bit):
    devices = range(lax.axis_size(axis))
    return lax.ppermute(block, axis, [(i, i ^ bit) for i in devices])


def dot(left, right):
    return jnp.dot(left, right, preferred_element_type=WIDE)


def dot_rt(left, right):
    return lax.dot_general(left, right, (((1,), (1,)), ((), ())), preferred_element_type=WIDE)


def dot_lt(left, right):
    return lax.dot_general(left, right, (((0,), (0,)), ((), ())), preferred_element_type=WIDE)


def shape(dims, dtype=LOW):
    return jax.ShapeDtypeStruct(tuple(dims), dtype)


def kernel(body, outs, *args, scratch=(), room=8, last=(), after=(), loads=0):
    spec = pl.BlockSpec(memory_space=pltpu.VMEM)
    off = pl.BlockSpec(memory_space=pl.ANY)
    place = pltpu.HBM if loads else pltpu.VMEM
    args = tuple(pltpu.with_memory_space_constraint(a, place) for a in args)
    waits = len(after)

    def step(*refs):
        body(*refs[waits:])

    sems = [pltpu.SemaphoreType.DMA((loads,))] if loads else []
    return pl.pallas_call(
        step,
        out_shape=[
            o if n in last else pltpu.VMEM(o.shape, o.dtype) for n, o in enumerate(outs)
        ],
        in_specs=[off] * waits + [off if loads else spec] * len(args),
        out_specs=[spec] * len(outs),
        scratch_shapes=list(scratch) + sems,
        compiler_params=pltpu.CompilerParams(vmem_limit_bytes=room << 20),
        cost_estimate=pl.CostEstimate(flops=1, bytes_accessed=1, transcendentals=0),
    )(*after, *args)


def load(sems, *pairs):
    copies = [
        pltpu.make_async_copy(source, target, sems.at[n])
        for n, (source, target) in enumerate(pairs)
    ]
    for copy in copies:
        copy.start()
    return copies


def places():
    index, place = lax.axis_index("ctx"), lax.axis_index("fsdp")
    core, side, row = index & 1, (index >> 1) & 1, (index >> 2) & 1
    return core, side, row, (index >> 1) & 3, place


def rows_from(start, count):
    return pl.ds(pl.multiple_of(start, 16), count)


def normalized(values):
    center = values - jnp.mean(values, -1, keepdims=True)
    inverse = lax.rsqrt(jnp.mean(center * center, -1, keepdims=True) + EPSILON)
    return center * inverse, inverse


def norm_back(grad, unit, inverse, gain):
    scaled = grad * gain
    return inverse * (
        scaled
        - jnp.mean(scaled, -1, keepdims=True)
        - unit * jnp.mean(scaled * unit, -1, keepdims=True)
    )


def lines_of(*vectors):
    rows = [v[...].astype(WIDE).reshape(1, v.shape[0]) for v in vectors]
    return jnp.concatenate(rows + [jnp.zeros((16 - len(rows), rows[0].shape[1]), WIDE)])


def prepare_tokens(x, seg, own, line, sems):
    tokens, width = x.shape[1:]
    for copy in load(sems, (seg, line), (x.at[0], own.at[pl.ds(0, tokens)])):
        copy.wait()
    seg_row = jnp.broadcast_to(line[...].astype(WIDE), (16, tokens)).astype(LOW)
    own[tokens:, :tokens] = seg_row
    own[tokens:, tokens:] = jnp.zeros((16, width - tokens), LOW)


def prepare_weights(wq, wk, wv, wo, wi, wu, *refs):
    vectors, first, (blocks, block), lines, sems = (
        refs[:9],
        refs[9],
        refs[10:12],
        refs[12:21],
        refs[21],
    )
    core, _, _, chip, _ = places()
    part, width = wq.shape
    half = part // 2
    rows = rows_from(core * half, half)
    pairs = [(w.at[rows], blocks.at[j]) for j, w in enumerate((wq, wk, wv))]
    pairs += [(wi.at[rows], block), (wo.at[rows], first.at[pl.ds(half, half)])]
    rows = rows_from((2 * chip + core) * half, half)
    pairs += [(wu.at[rows], first.at[pl.ds(3 * half, half)])]
    for copy in load(sems, *pairs, *zip(vectors, lines)):
        copy.wait()
    six, bias_inner, biases = lines_of(*lines[:6]), lines_of(lines[6]), lines_of(*lines[7:])
    for p in range(CHIPS):

        @pl.when(chip == p)
        def _():
            span = slice(p * part, (p + 1) * part)
            for j in range(3):
                first[:half, j * part : (j + 1) * part] = blocks[j, :, span]
            for k in range(4):
                start = k * width + p * part
                first[2 * half : 3 * half, k * part : (k + 1) * part] = block[
                    :, start : start + part
                ]
            small = [six[:6], bias_inner[:1, span], biases[:2], jnp.zeros((half - 9, part), WIDE)]
            first[:half, 3 * part :] = jnp.concatenate(small).astype(LOW)


def first_rows(block, out):
    out[...] = block[: out.shape[0]]


def passed(block, out):
    out[...] = block[...]


def split_rows(block, *outs):
    n = outs[0].shape[0]
    for m, out in enumerate(outs):
        out[...] = block[m * n : (m + 1) * n]


def sort_pieces(own, near, far, farthest, projections, others, sent):
    half = farthest.shape[0]
    for r, piece in enumerate((own, near, far, farthest)):
        projections[r] = piece[:half]
    for r, piece in enumerate((own, near, far)):
        others[r] = piece[half:]
    sent[...] = far[half:]


def assemble(*refs):
    own, own_last, other, other_last, weights = refs[0], refs[1:4], refs[4], refs[5:8], refs[8:]
    core, _, _, _, place = places()
    half = weights[0].shape[0] // 8
    for c, (pieces, last) in enumerate(((own, own_last), (other, other_last))):
        for r in range(4):
            base = rows_from((2 * (place ^ r) + (core ^ c)) * half, half)
            for m, weight in enumerate(weights):
                weight[base] = last[m][...] if r == 3 else pieces[r, m * half : (m + 1) * half]


def stack(own, near, far, farthest, out):
    for r, piece in enumerate((own, near, far, farthest)):
        out[r] = piece[...]


def project(seen, *refs):
    pieces, outs = refs[:2], refs[2:]
    rows_in, w_qkv, queries, keys_values, segs, vec, b_inner, stage = outs
    core, _, _, chip, place = places()
    width = seen.shape[2]
    tokens = rows_in.shape[0] // CHIPS
    part, half = width // 4, width // 8
    for s in range(CHIPS):
        x = seen.at[chip ^ s]
        rows_in[s * tokens : (s + 1) * tokens] = x[:tokens]
        segs[s : s + 1] = x[tokens : tokens + 1, :tokens].astype(WIDE)
    segs[CHIPS:] = jnp.zeros((8 - CHIPS, tokens), WIDE)
    for r in range(4):
        for c, piece in enumerate(pieces):
            base = rows_from((2 * (place ^ r) + (core ^ c)) * half, half)
            w_qkv[base] = piece[r, :, : 3 * part]
        stage[place ^ r] = pieces[0][r, :16, 3 * part :].astype(WIDE)
    for k in range(4):
        span = slice(k * part, (k + 1) * part)
        vec[:6, span] = stage[k, :6]
        b_inner[:, span] = stage[k, 6:7]
    vec[6:] = jnp.zeros((2, width), WIDE)
    bias = stage[chip]
    out = dot(rows_in[...], w_qkv[...])
    scale = HEAD_DIM ** (-0.5)
    queries[...] = ((out[:, :part] + bias[7:8]).astype(LOW).astype(WIDE) * scale).astype(LOW)
    keys_values[:, :part] = out[:, part : 2 * part].astype(LOW)
    keys_values[:, part:] = (out[:, 2 * part :] + bias[8:9]).astype(LOW)


def attend(queries, seg_query, keys_values, seg_key, context, probs):
    part = queries.shape[1]
    seg_columns = seg_key[...].T
    seg_row = seg_query[...]
    allowed = jnp.concatenate(
        [seg_columns[:, b : b + 1] == seg_row for b in range(seg_key.shape[0])]
    )
    for h in range(part // HEAD_DIM):
        keys = keys_values[:, h * HEAD_DIM : (h + 1) * HEAD_DIM]
        values = keys_values[:, part + h * HEAD_DIM : part + (h + 1) * HEAD_DIM]
        scores = dot_rt(keys, queries[:, h * HEAD_DIM : (h + 1) * HEAD_DIM])
        scores = jnp.where(allowed, scores, NEGATIVE)
        weights = jnp.exp(scores - jnp.max(scores, 0, keepdims=True))
        weights = (weights * (1.0 / jnp.sum(weights, 0, keepdims=True))).astype(LOW)
        probs[h] = weights
        out = dot_lt(values, weights)
        context[:, h * HEAD_DIM : (h + 1) * HEAD_DIM] = out.T.astype(LOW)


def attend_back(queries, keys_values, grad_context, probs, grad_queries, grad_keys_values):
    part = queries.shape[1]
    scale = HEAD_DIM ** (-0.5)
    for h in range(part // HEAD_DIM):
        span = slice(h * HEAD_DIM, (h + 1) * HEAD_DIM)
        span_v = slice(part + h * HEAD_DIM, part + (h + 1) * HEAD_DIM)
        keys, values = keys_values[:, span], keys_values[:, span_v]
        grads = grad_context[:, span]
        soft = probs[h]
        grad_keys_values[:, span_v] += dot(soft, grads)
        grad_probs = dot_rt(values, grads)
        wide = soft.astype(WIDE)
        delta = jnp.sum(wide * grad_probs, 0, keepdims=True)
        grad_scores = (wide * (grad_probs - delta)).astype(LOW)
        grad_queries[:, span] = (dot_lt(keys, grad_scores) * scale).T.astype(LOW)
        grad_keys_values[:, span] += dot(grad_scores, queries[:, span])


def beside(rows, out):
    tokens, part = out.shape[0], rows.shape[1]
    for t in range(CHIPS):
        out[:, t * part : (t + 1) * part] = rows[t * tokens : (t + 1) * tokens]


def attend_all(queries, kv_own, kv_far, seg_own, seg_far, context, probs, *scratch):
    keys_values, seg_key, seg_query, rows = scratch
    count = kv_own.shape[0]
    tokens = seg_own.shape[1]
    keys_values[:count] = kv_own[...]
    keys_values[count:] = kv_far[...]
    seg_key[:CHIPS] = seg_own[:CHIPS]
    seg_key[CHIPS:] = seg_far[:CHIPS]
    for s in range(CHIPS):
        seg_query[:, s * tokens : (s + 1) * tokens] = seg_own[s : s + 1]
    attend(queries, seg_query, keys_values, seg_key, rows, probs)
    beside(rows, context)


def context_back(g0, g1, g2, g3, w_output, grad_low, grad_context):
    _, _, _, chip, _ = places()
    tokens, part = g0.shape[0], grad_context.shape[1]
    for s, block in enumerate((g0, g1, g2, g3)):
        grad_low[s * tokens : (s + 1) * tokens] = block[...]
    grad_context[...] = dot_rt(grad_low[...], w_output[rows_from(chip * part, part)]).astype(LOW)


def attend_back_all(queries, kv_own, kv_far, g0, g1, g2, g3, w_output, probs, *refs):
    grad_low, grad_queries, grad_own, *grad_far, keys_values, grad_context, total = refs
    count = kv_own.shape[0]
    keys_values[:count] = kv_own[...]
    keys_values[count:] = kv_far[...]
    context_back(g0, g1, g2, g3, w_output, grad_low, grad_context)
    total[...] = jnp.zeros(total.shape, WIDE)
    attend_back(queries, keys_values, grad_context, probs, grad_queries, total)
    grad_own[...] = total[:count]
    tokens = count // CHIPS
    for t, out in enumerate(grad_far):
        out[...] = total[count + t * tokens : count + (t + 1) * tokens].astype(LOW)


def attend_back_block(queries, keys_values, grads, probs, grad_queries, grad_keys_values):
    @pl.when(pl.program_id(0) == 0)
    def _():
        grad_keys_values[...] = jnp.zeros(grad_keys_values.shape, WIDE)

    attend_back(queries, keys_values, grads, probs, grad_queries, grad_keys_values)


def attention_block(queries, keys_values):
    return min(queries.shape[0], 128 * max(1, 2048 // keys_values.shape[0]))


def whole(array):
    return pl.BlockSpec(array.shape, lambda i: (0,) * array.ndim)


def attention(queries, seg_query, keys_values, seg_key):
    count, part = queries.shape
    keys = keys_values.shape[0]
    heads = part // HEAD_DIM
    block = attention_block(queries, keys_values)
    return pl.pallas_call(
        attend,
        grid=(count // block,),
        in_specs=[
            pl.BlockSpec((block, part), lambda i: (i, 0)),
            pl.BlockSpec((1, block), lambda i: (0, i)),
            whole(keys_values),
            whole(seg_key),
        ],
        out_specs=[
            pl.BlockSpec((block, part), lambda i: (i, 0)),
            pl.BlockSpec((heads, keys, block), lambda i: (0, 0, i)),
        ],
        out_shape=[shape((count, part)), shape((heads, keys, count))],
        compiler_params=pltpu.CompilerParams(vmem_limit_bytes=VMEM_BYTES),
    )(queries, seg_query, keys_values, seg_key)


def attention_back(queries, keys_values, grad_context, probs):
    count, part = queries.shape
    keys = keys_values.shape[0]
    block = attention_block(queries, keys_values)
    rows = pl.BlockSpec((block, part), lambda i: (i, 0))
    return pl.pallas_call(
        attend_back_block,
        grid=(count // block,),
        in_specs=[
            rows,
            whole(keys_values),
            rows,
            pl.BlockSpec((probs.shape[0], keys, block), lambda i: (0, 0, i)),
        ],
        out_specs=[rows, pl.BlockSpec((keys, 2 * part), lambda i: (0, 0))],
        out_shape=[shape((count, part)), shape((keys, 2 * part), WIDE)],
        compiler_params=pltpu.CompilerParams(vmem_limit_bytes=VMEM_BYTES),
    )(queries, keys_values, grad_context, probs)


def forward(c0, c1, c2, c3, rows_in, w_output, vec, w_inner, b_inner, w_outer, *outs):
    context_low, unit_one, inverse_one, normed_low, activated, slope = outs[:6]
    own, sent, stage = outs[6], outs[7:10], outs[10]
    _, _, _, chip, _ = places()
    tokens, part = c0.shape[0], c0.shape[1] // CHIPS
    for s, block in enumerate((c0, c1, c2, c3)):
        for t in range(CHIPS):
            stage[chip ^ s, t * tokens : (t + 1) * tokens] = block[
                :, (t ^ s) * part : ((t ^ s) + 1) * part
            ]
    for k in range(CHIPS):
        context_low[:, k * part : (k + 1) * part] = stage[k]
    residual = rows_in[...].astype(WIDE) + dot(context_low[...], w_output[...]) + vec[0:1]
    unit, inverse = normalized(residual)
    unit_one[...] = unit[:tokens]
    inverse_one[...] = inverse[:tokens]
    normed_low[...] = (unit * vec[1:2] + vec[2:3]).astype(LOW)
    inner_pre = dot(normed_low[...], w_inner[...]) + b_inner[...]
    cdf = 0.5 * (1.0 + lax.erf(inner_pre * (0.5**0.5)))
    activated[...] = (inner_pre * cdf).astype(LOW)
    slope[...] = cdf + inner_pre * jnp.exp(-0.5 * inner_pre * inner_pre) * 0.3989422804014327
    parted(dot(activated[...], w_outer[...]), own, sent)


def parted(values, own, sent):
    tokens = own.shape[0]
    own[...] = values[:tokens]
    for s, out in enumerate(sent):
        out[...] = values[(s + 1) * tokens : (s + 2) * tokens].astype(LOW)


def total_of(own, blocks):
    total = own[...]
    for block in blocks:
        total = total + block[...].astype(WIDE)
    return total


def backward_first(own, s1, s2, s3, unit_one, vec, cot, result, grad_summed, grad_outer, sums):
    summed = unit_one[...] * vec[1:2] + vec[2:3] + vec[3:4] + total_of(own, (s1, s2, s3))
    unit, inverse = normalized(summed)
    result[0] = (unit * vec[4:5] + vec[5:6]).astype(LOW)
    c = cot[0].astype(WIDE)
    grad = norm_back(c, unit, inverse, vec[4:5])
    grad_summed[...] = grad
    grad_outer[...] = grad.astype(LOW)
    sums[0:1] = jnp.sum(grad_outer[...].astype(WIDE), 0, keepdims=True)
    sums[1:2] = jnp.sum(c * unit, 0, keepdims=True)
    sums[2:3] = jnp.sum(c, 0, keepdims=True)
    sums[3:] = jnp.zeros((5, sums.shape[1]), WIDE)


def backward_second(g0, g1, g2, g3, slope, w_outer, w_inner, grad_inner, sums, *outs):
    grad_outer = jnp.concatenate([g0[...], g1[...], g2[...], g3[...]])
    grad_inner[...] = (dot_rt(grad_outer, w_outer[...]) * slope[...]).astype(LOW)
    parted(dot_rt(grad_inner[...], w_inner[...]), outs[0], outs[1:])
    sums[...] = jnp.sum(grad_inner[...].astype(WIDE), 0, keepdims=True)


def cut_rows(stage, keep, sent):
    core, _, _, _, place = places()
    half = keep.shape[1]
    for r in range(4):
        for c, out in enumerate((keep.at[r], sent[r])):
            out[...] = stage[rows_from((2 * (place ^ r) + (core ^ c)) * half, half)]


def outer_grads(activated, g0, g1, g2, g3, keep, send, stage):
    grad_outer = jnp.concatenate([g0[...], g1[...], g2[...], g3[...]])
    stage[...] = dot_lt(activated[...], grad_outer).astype(LOW)
    cut_rows(stage, keep, [send.at[r] for r in range(4)])


def inner_grads(normed_low, grad_inner, keep, s0, s1, s2, s3, stage):
    stage[...] = dot_lt(normed_low[...], grad_inner[...]).astype(LOW)
    cut_rows(stage, keep, (s0, s1, s2, s3))


def norm_backward(grad_summed, own, s1, s2, s3, unit_one, inverse_one, vec, grad_own, grad_low, sums):
    grad = grad_summed[...] + total_of(own, (s1, s2, s3))
    unit = unit_one[...]
    branch = norm_back(grad, unit, inverse_one[...], vec[1:2])
    grad_own[...] = branch
    grad_low[...] = branch.astype(LOW)
    sums[0:1] = jnp.sum(grad_low[...].astype(WIDE), 0, keepdims=True)
    sums[1:2] = jnp.sum(grad * unit, 0, keepdims=True)
    sums[2:3] = jnp.sum(grad, 0, keepdims=True)
    sums[3:] = jnp.zeros((5, sums.shape[1]), WIDE)


def output_grads(context_low, grad_low, out):
    _, _, _, chip, _ = places()
    part = out.shape[1]
    for p in range(CHIPS):

        @pl.when(chip == p)
        def _():
            block = grad_low[:, p * part : (p + 1) * part]
            out[...] = dot_lt(context_low[...], block).astype(LOW)


def projection_grads(rows_in, grad_queries, grad_kv, f0, f1, f2, f3, grad_o, *refs):
    (sums_one, sums_two, sums_inner), outs = refs[:3], refs[3:]
    grad_qkv, keep, send, stage = outs
    core, _, _, _, place = places()
    part = grad_queries.shape[1]
    width = 4 * part
    grad_qkv[:, :part] = grad_queries[...]
    far = jnp.concatenate([f0[...], f1[...], f2[...], f3[...]]).astype(WIDE)
    grad_qkv[:, part:] = (grad_kv[...] + far).astype(LOW)
    stage[:, : 3 * part] = dot_lt(rows_in[...], grad_qkv[...]).astype(LOW)
    stage[:, 3 * part :] = grad_o[...]
    half = part // 2
    total = jnp.sum(grad_qkv[...].astype(WIDE), 0, keepdims=True)
    for k in range(4):
        span = slice(k * part, (k + 1) * part)
        small = jnp.concatenate(
            [
                sums_one[:3, span],
                sums_two[:3, span],
                sums_inner[:, span],
                total[:, :part],
                total[:, 2 * part :],
                jnp.zeros((7, part), WIDE),
            ]
        )
        small = jnp.concatenate([small, jnp.zeros((16, width - part), WIDE)], 1).astype(LOW)
        for c, out in enumerate((keep, send)):
            out[place ^ k, half:] = small
            out[place ^ k, :half] = stage[rows_from(k * part + (core ^ c) * half, half)]


def input_grads(grad_qkv, w_qkv, grad_residual, own, s1, s2, s3):
    tokens = own.shape[0]
    grads = dot_rt(grad_qkv[...], w_qkv[...])
    parted(grads, own, (s1, s2, s3))
    own[...] += grad_residual[...]


def add_tokens(own, s1, s2, s3, out, done):
    done[...] = jnp.zeros(done.shape, WIDE)
    out[0] = total_of(own, (s1, s2, s3)).astype(LOW)


def add_near(kept, received, keep, send):
    total = kept[...].astype(WIDE) + received[...].astype(WIDE)
    for r in range(2):
        keep[r] = total[2 * r].astype(LOW)
        send[r] = total[2 * r + 1].astype(LOW)


def add_near_parts(kept, r0, r1, r2, r3, keep, send):
    for r, received in enumerate((r0, r1, r2, r3)):
        out = (keep, send)[r % 2]
        out[r // 2] = (kept[r].astype(WIDE) + received[...].astype(WIDE)).astype(LOW)


def add_far(kept, received, keep, send):
    total = kept[...].astype(WIDE) + received[...].astype(WIDE)
    keep[...] = total[0].astype(LOW)
    send[...] = total[1].astype(LOW)


def add_far_passing(kept, received, other, keep, send, out):
    add_far(kept, received, keep, send)
    out[...] = other[...]


def add_last(kept, received, out):
    out[...] = (kept[...].astype(WIDE) + received[...].astype(WIDE)).astype(LOW)


def add_beside(other, kept, received, out):
    half = kept.shape[0]
    out[:half] = other[...]
    add_last(kept, received, out.at[half:])


def stack_halves(own, near, far, farthest, first, second):
    half = first.shape[1]
    for s, block in enumerate((own, near, far, farthest)):
        first[s] = block[:half]
        second[s] = block[half:]


def unpack_mlp(outer_own, inner_own, outer_other, inner_other, outer, inner, done, stage):
    core, _, _, chip, _ = places()
    half, width = outer_own.shape[1:]
    part = 2 * half
    for s in range(CHIPS):
        for m, (one, two) in enumerate(((outer_own, inner_own), (outer_other, inner_other))):
            far, c = chip ^ s, core ^ m
            outer[rows_from((2 * far + c) * half, half)] = one[s].astype(WIDE)
            stage[c, far] = two[s]
    for c in range(2):
        for p in range(CHIPS):
            for k in range(4):
                start = k * width + p * part
                inner[c * half : (c + 1) * half, start : start + part] = stage[
                    c, p, :, k * part : (k + 1) * part
                ].astype(WIDE)
    done[...] = jnp.zeros(done.shape, WIDE)


def unpack_rest(*refs):
    pieces, mats, vectors, (b_query, b_value, b_inner, stage, small) = (
        refs[:2],
        refs[2:6],
        refs[6:12],
        refs[12:],
    )
    core, _, _, chip, place = places()
    part = mats[0].shape[0]
    half = part // 2
    for s in range(CHIPS):
        for m, blocks in enumerate(pieces):
            stage[core ^ m, s] = blocks[s, :half]
        small[s] = pieces[0][s, half:, :part].astype(WIDE)
    for c in range(2):
        for k in range(CHIPS):
            for j, out in enumerate(mats):
                out[c * half : (c + 1) * half, k * part : (k + 1) * part] = stage[
                    c, k, :, j * part : (j + 1) * part
                ].astype(WIDE)
    total = small[0] + small[1] + small[2] + small[3]
    for i, out in enumerate(vectors):
        out[...] = total[i]
    biases = small[place]
    b_query[...] = biases[7]
    b_value[...] = biases[8]
    for p in range(CHIPS):
        b_inner[p * part : (p + 1) * part] = small[p][6]


def per_device(
    inputs,
    segments,
    query_weight,
    query_bias,
    key_weight,
    value_weight,
    value_bias,
    output_weight,
    output_bias,
    first_gain,
    first_shift,
    inner_weight,
    inner_bias,
    outer_weight,
    outer_bias,
    second_gain,
    second_shift,
    cotangent,
):
    groups = lax.axis_size("ctx") // TEAM
    lines = [[m + TEAM * g for g in range(groups)] for m in range(TEAM)]
    tokens, width = inputs.shape[1:]
    part = query_weight.shape[0]
    hidden = outer_weight.shape[0]
    count, half = CHIPS * tokens, part // 2
    heads = part // HEAD_DIM

    def chips(block):
        return [partner(block, "ctx", s << 1) for s in (1, 2, 3)]

    def exchanged(blocks):
        return [partner(block, "ctx", (s + 1) << 1) for s, block in enumerate(blocks)]

    def joined(block):
        return partner(block, "ctx", CORE)

    (own,) = kernel(
        prepare_tokens,
        [shape((tokens + 16, width))],
        inputs,
        segments,
        scratch=[pltpu.VMEM((1, tokens), jnp.int32)],
        loads=2,
    )
    teams = [[c + TEAM * g + 2 * n for n in range(CHIPS)] for g in range(groups) for c in range(2)]
    seen = lax.all_gather(own, "ctx", axis_index_groups=teams)
    (first,) = kernel(
        prepare_weights,
        [shape((4 * half, width))],
        query_weight,
        key_weight,
        value_weight,
        output_weight,
        inner_weight,
        outer_weight,
        output_bias,
        first_gain,
        first_shift,
        outer_bias,
        second_gain,
        second_shift,
        inner_bias,
        query_bias,
        value_bias,
        scratch=[
            pltpu.VMEM((3, half, width), LOW),
            pltpu.VMEM((half, 4 * width), LOW),
            *[pltpu.VMEM((part,), LOW)] * 6,
            pltpu.VMEM((hidden,), LOW),
            *[pltpu.VMEM((part,), LOW)] * 2,
        ],
        loads=15,
    )
    (mine,) = kernel(first_rows, [shape((half, width))], first, after=(seen,))
    line = [first, partner(first, "fsdp", 1), partner(first, "fsdp", 2), partner(mine, "fsdp", 3)]
    projections, others, sent = kernel(
        sort_pieces,
        [shape((4, half, width)), shape((3, 3 * half, width)), shape((3 * half, width))],
        *line,
    )
    last = partner(sent, "fsdp", 1)

    rows_in, w_qkv, queries, kv_own, segs, vec, b_inner = kernel(
        project,
        [
            shape((count, width)),
            shape((width, 3 * part)),
            shape((count, part)),
            shape((count, 2 * part)),
            shape((8, tokens), WIDE),
            shape((8, width), WIDE),
            shape((1, width), WIDE),
        ],
        seen,
        projections,
        joined(projections),
        scratch=[pltpu.VMEM((4, 16, part), WIDE)],
    )
    kv_far, seg_far = partner(kv_own, "ctx", CORE), partner(segs, "ctx", CORE)
    if groups == 1:
        context, probs = kernel(
            attend_all,
            [shape((tokens, width)), shape((heads, 2 * count, count))],
            queries,
            kv_own,
            kv_far,
            segs,
            seg_far,
            scratch=[
                pltpu.VMEM((2 * count, 2 * part), LOW),
                pltpu.VMEM((2 * CHIPS, tokens), WIDE),
                pltpu.VMEM((1, count), WIDE),
                pltpu.VMEM((count, part), LOW),
            ],
            room=24,
        )
    else:
        kv = jnp.concatenate([kv_own, kv_far])
        seg_key = jnp.concatenate([segs[:CHIPS], seg_far[:CHIPS]])
        kv = lax.all_gather(kv, "ctx", axis=0, tiled=True, axis_index_groups=lines)
        seg_key = lax.all_gather(seg_key, "ctx", axis=0, tiled=True, axis_index_groups=lines)
        rows, probs = attention(queries, segs[:CHIPS].reshape(1, count), kv, seg_key)
        (context,) = kernel(beside, [shape((tokens, width))], rows)

    contexts = [context] + chips(context)
    last = kernel(
        split_rows, [shape((half, width))] * 3, last, after=(context,)
    )
    w_output, w_inner, w_outer = kernel(
        assemble, [shape((width, width))] * 3, others, *last, joined(others), *map(joined, last)
    )
    context_low, unit_one, inverse_one, normed_low, activated, slope, *outer_sent = kernel(
        forward,
        [
            shape((count, width)),
            shape((tokens, width), WIDE),
            shape((tokens, 1), WIDE),
            shape((count, width)),
            shape((count, width)),
            shape((count, width), WIDE),
            shape((tokens, width), WIDE),
        ]
        + [shape((tokens, width))] * 3,
        *contexts,
        rows_in,
        w_output,
        vec,
        w_inner,
        b_inner,
        w_outer,
        scratch=[pltpu.VMEM((CHIPS, count, part), LOW)],
        room=16,
    )
    result, grad_summed, grad_outer, sums_one = kernel(
        backward_first,
        [
            shape((1, tokens, width)),
            shape((tokens, width), WIDE),
            shape((tokens, width)),
            shape((8, width), WIDE),
        ],
        outer_sent[0],
        *exchanged(outer_sent[1:]),
        unit_one,
        vec,
        cotangent,
        last=(0,),
    )
    grads_outer = [grad_outer] + chips(grad_outer)
    outer_kept, outer_sent = kernel(
        outer_grads,
        [shape((4, half, width))] * 2,
        activated,
        *grads_outer,
        scratch=[pltpu.VMEM((width, width), LOW)],
    )
    grad_inner, sums_inner, inner_own, *inner_sent = kernel(
        backward_second,
        [shape((count, width)), shape((1, width), WIDE), shape((tokens, width), WIDE)]
        + [shape((tokens, width))] * 3,
        *grads_outer,
        slope,
        w_outer,
        w_inner,
        room=12,
    )
    inner_far = exchanged(inner_sent)

    def near_sum(kept, sent):
        received = partner(sent, "ctx", CORE)
        return kernel(add_near, [shape((2,) + kept.shape[1:])] * 2, kept, received)

    def far_sum(kept, sent, after=()):
        received = partner(sent, "fsdp", 1)
        return kernel(add_far, [shape(kept.shape[1:])] * 2, kept, received, after=after)

    def last_sum(kept, sent, after=()):
        received = partner(sent, "fsdp", 2)
        (total,) = kernel(add_last, [shape(kept.shape)], kept, received, after=after)
        if groups > 1:
            total = lax.psum(total.astype(WIDE), "ctx", axis_index_groups=lines).astype(LOW)
        return total

    inner_kept, *inner_sent = kernel(
        inner_grads,
        [shape((4, half, width))] + [shape((half, width))] * 4,
        normed_low,
        grad_inner,
        scratch=[pltpu.VMEM((width, width), LOW)],
    )
    inner_kept, inner_sent = kernel(
        add_near_parts,
        [shape((2, half, width))] * 2,
        inner_kept,
        *(partner(block, "ctx", CORE) for block in inner_sent),
    )
    outer_kept, outer_sent = near_sum(outer_kept, outer_sent)
    outer_kept, outer_sent, inner_sent = kernel(
        add_far_passing,
        [shape((half, width))] * 2 + [shape((2, half, width))],
        outer_kept,
        partner(outer_sent, "fsdp", 1),
        inner_sent,
    )
    inner_far_sum = far_sum(inner_kept, inner_sent)
    outer_total = last_sum(outer_kept, outer_sent)
    grad_residual, grad_low, sums_two = kernel(
        norm_backward,
        [shape((tokens, width), WIDE), shape((tokens, width)), shape((8, width), WIDE)],
        grad_summed,
        inner_own,
        *inner_far,
        unit_one,
        inverse_one,
        vec,
    )
    grads_low = [grad_low] + chips(grad_low)
    if groups == 1:
        grad_low, grad_queries, grad_kv, *grad_kv_sent = kernel(
            attend_back_all,
            [
                shape((count, width)),
                shape((count, part)),
                shape((count, 2 * part), WIDE),
            ]
            + [shape((tokens, 2 * part))] * CHIPS,
            queries,
            kv_own,
            kv_far,
            *grads_low,
            w_output,
            probs,
            scratch=[
                pltpu.VMEM((2 * count, 2 * part), LOW),
                pltpu.VMEM((count, part), LOW),
                pltpu.VMEM((2 * count, 2 * part), WIDE),
            ],
            room=24,
            after=(outer_kept,),
        )
    else:
        grad_low, grad_context = kernel(
            context_back, [shape((count, width)), shape((count, part))], *grads_low, w_output
        )
        grad_queries, grad_kv = attention_back(queries, kv, grad_context, probs)
        grad_kv = grad_kv.reshape(groups, 2, count, 2 * part).transpose(1, 0, 2, 3)
        grad_kv = lax.psum_scatter(
            grad_kv.reshape(2, groups * count, 2 * part),
            "ctx",
            scatter_dimension=1,
            tiled=True,
            axis_index_groups=lines,
        )
        grad_kv, grad_kv_sent = grad_kv[0], jnp.split(grad_kv[1].astype(LOW), CHIPS)
    grad_kv_far = [joined(block) for block in grad_kv_sent]
    (grad_o,) = kernel(output_grads, [shape((width, part))], context_low, grad_low)
    cut = shape((4, half + 16, width))
    grad_qkv, rest_kept, rest_sent = kernel(
        projection_grads,
        [shape((count, 3 * part)), cut, cut],
        rows_in,
        grad_queries,
        grad_kv,
        *grad_kv_far,
        grad_o,
        sums_one,
        sums_two,
        sums_inner,
        scratch=[pltpu.VMEM((width, width), LOW)],
        after=(outer_total, inner_far_sum[0]),
    )
    rest_near = near_sum(rest_kept, rest_sent)
    input_own, *input_sent = kernel(
        input_grads,
        [shape((tokens, width), WIDE)] + [shape((tokens, width))] * 3,
        grad_qkv,
        w_qkv,
        grad_residual,
        after=tuple(rest_near),
    )
    input_far = exchanged(input_sent)

    rest_far = far_sum(*rest_near)
    (mlp_total,) = kernel(
        add_beside,
        [shape((2 * half, width))],
        outer_total,
        inner_far_sum[0],
        partner(inner_far_sum[1], "fsdp", 2),
        after=(*input_far, rest_far[0]),
    )
    rest_total = last_sum(*rest_far)
    rest_all = lax.all_gather(rest_total, "ctx", axis_index_groups=teams)
    mlp_blocks = kernel(
        stack_halves,
        [shape((CHIPS, half, width))] * 2,
        mlp_total,
        *chips(mlp_total),
        after=(rest_all,),
    )
    grad_input, done_input = kernel(
        add_tokens,
        [shape((1, tokens, width)), shape((8, 128), WIDE)],
        input_own,
        *input_far,
        last=(0,),
        after=(rest_total,),
    )
    g_outer, g_inner, done_mlp = kernel(
        unpack_mlp,
        [
            shape((hidden, width), WIDE),
            shape((part, 4 * hidden), WIDE),
            shape((8, 128), WIDE),
        ],
        *mlp_blocks,
        *map(joined, mlp_blocks),
        last=(0, 1),
        scratch=[pltpu.VMEM((2, CHIPS, half, width), LOW)],
        room=12,
        after=(rest_all,),
    )
    g_query, g_key, g_value, g_output, *vec, g_b_query, g_b_value, g_b_inner = kernel(
        unpack_rest,
        [shape((part, width), WIDE)] * 4
        + [shape((part,), WIDE)] * 8
        + [shape((width,), WIDE)],
        rest_all,
        joined(rest_all),
        last=range(13),
        scratch=[
            pltpu.VMEM((2, CHIPS, half, width), LOW),
            pltpu.VMEM((CHIPS, 16, part), WIDE),
        ],
        room=12,
    )
    return (
        result,
        grad_input,
        g_query,
        g_b_query,
        g_key,
        g_value,
        g_b_value,
        g_output,
        vec[3],
        vec[4],
        vec[5],
        g_inner,
        g_b_inner,
        g_outer,
        vec[0],
        vec[1],
        vec[2],
    )


def solution(mesh):
    rows, cuts, whole = P("fsdp", "ctx", None), P("fsdp", None), P("fsdp")
    params = (cuts, whole, cuts, cuts, whole, cuts, whole, whole, whole)
    params += (cuts, whole, cuts, whole, whole, whole)
    return jax.shard_map(
        per_device,
        mesh=mesh,
        in_specs=(rows, P("fsdp", "ctx")) + params + (rows,),
        out_specs=(rows, rows) + params,
        check_vma=False,
    )
```

```python
import functools

import jax
import jax.numpy as jnp
from jax import lax
from jax.experimental import pallas as pl
from jax.experimental.pallas import tpu as pltpu
from jax.sharding import PartitionSpec as P

HEAD_DIM = 64
NEGATIVE = -1000000000.0
EPSILON = 1e-12
LOW = jnp.bfloat16
WIDE = jnp.float32

CORE, SIDE, ROW = 1, 2, 4
TEAM = 8
CHIPS = 4
VMEM_BYTES = 56 << 20


def partner(block, axis, bit):
    devices = range(lax.axis_size(axis))
    return lax.ppermute(block, axis, [(i, i ^ bit) for i in devices])


def dot(left, right):
    return jnp.dot(left, right, preferred_element_type=WIDE)


def dot_rt(left, right):
    return lax.dot_general(left, right, (((1,), (1,)), ((), ())), preferred_element_type=WIDE)


def dot_lt(left, right):
    return lax.dot_general(left, right, (((0,), (0,)), ((), ())), preferred_element_type=WIDE)


def shape(dims, dtype=LOW):
    return jax.ShapeDtypeStruct(tuple(dims), dtype)


def kernel(body, outs, *args, scratch=(), room=8, last=(), after=(), loads=0):
    spec = pl.BlockSpec(memory_space=pltpu.VMEM)
    off = pl.BlockSpec(memory_space=pl.ANY)
    place = pltpu.HBM if loads else pltpu.VMEM
    args = tuple(pltpu.with_memory_space_constraint(a, place) for a in args)
    waits = len(after)

    def step(*refs):
        body(*refs[waits:])

    sems = [pltpu.SemaphoreType.DMA((loads,))] if loads else []
    return pl.pallas_call(
        step,
        out_shape=[
            o if n in last else pltpu.VMEM(o.shape, o.dtype) for n, o in enumerate(outs)
        ],
        in_specs=[off] * waits + [off if loads else spec] * len(args),
        out_specs=[spec] * len(outs),
        scratch_shapes=list(scratch) + sems,
        compiler_params=pltpu.CompilerParams(vmem_limit_bytes=room << 20),
        cost_estimate=pl.CostEstimate(flops=1, bytes_accessed=1, transcendentals=0),
    )(*after, *args)


def load(sems, *pairs):
    copies = [
        pltpu.make_async_copy(source, target, sems.at[n])
        for n, (source, target) in enumerate(pairs)
    ]
    for copy in copies:
        copy.start()
    return copies


def places():
    index, place = lax.axis_index("ctx"), lax.axis_index("fsdp")
    core, side, row = index & 1, (index >> 1) & 1, (index >> 2) & 1
    return core, side, row, (index >> 1) & 3, place


def rows_from(start, count):
    return pl.ds(pl.multiple_of(start, 16), count)


def normalized(values):
    center = values - jnp.mean(values, -1, keepdims=True)
    inverse = lax.rsqrt(jnp.mean(center * center, -1, keepdims=True) + EPSILON)
    return center * inverse, inverse


def norm_back(grad, unit, inverse, gain):
    scaled = grad * gain
    return inverse * (
        scaled
        - jnp.mean(scaled, -1, keepdims=True)
        - unit * jnp.mean(scaled * unit, -1, keepdims=True)
    )


def lines_of(*vectors):
    rows = [v[...].astype(WIDE).reshape(1, v.shape[0]) for v in vectors]
    return jnp.concatenate(rows + [jnp.zeros((16 - len(rows), rows[0].shape[1]), WIDE)])


def prepare_tokens(x, seg, own, line, sems):
    tokens, width = x.shape[1:]
    for copy in load(sems, (seg, line), (x.at[0], own.at[pl.ds(0, tokens)])):
        copy.wait()
    seg_row = jnp.broadcast_to(line[...].astype(WIDE), (16, tokens)).astype(LOW)
    own[tokens:, :tokens] = seg_row
    own[tokens:, tokens:] = jnp.zeros((16, width - tokens), LOW)


def prepare_weights(wq, wk, wv, wo, wi, wu, *refs):
    vectors, first, (blocks, block), lines, sems = (
        refs[:9],
        refs[9],
        refs[10:12],
        refs[12:21],
        refs[21],
    )
    core, _, _, chip, _ = places()
    part, width = wq.shape
    half = part // 2
    most = 3 * half // 4
    head = most + 8
    rows = rows_from(core * half, half)
    pairs = [(w.at[rows], blocks.at[j]) for j, w in enumerate((wq, wk, wv))]
    pairs += [(wi.at[rows], block), (wo.at[rows], first.at[pl.ds(head, half)])]
    rows = rows_from((2 * chip + core) * half, half)
    pairs += [(wu.at[rows], first.at[pl.ds(head + 2 * half, half)])]
    for copy in load(sems, *pairs, *zip(vectors, lines)):
        copy.wait()
    six, bias_inner, biases = lines_of(*lines[:6]), lines_of(lines[6]), lines_of(*lines[7:])
    for p in range(CHIPS):

        @pl.when(chip == p)
        def _():
            span = slice(p * part, (p + 1) * part)
            three = [blocks[j, :, span].astype(WIDE) for j in range(3)]
            for k in range(4):
                start = k * width + p * part
                first[head + half : head + 2 * half, k * part : (k + 1) * part] = block[
                    :, start : start + part
                ]
            small = jnp.concatenate([six[:6], bias_inner[:1, span], biases[:1]])
            after = jnp.concatenate([biases[1:2], jnp.zeros((7, part), WIDE)])
            small = jnp.concatenate([small, after, jnp.zeros((8, 2 * part), WIDE)], 1)
            beside = jnp.concatenate([block[most:] for block in three])
            rows_q = jnp.concatenate([block[:most] for block in three] + [beside], 1)
            first[:head] = jnp.concatenate([rows_q, small]).astype(LOW)


def first_rows(block, out):
    out[...] = block[: out.shape[0]]


def passed(block, out):
    out[...] = block[...]


def split_rows(block, *outs):
    n = outs[0].shape[0]
    for m, out in enumerate(outs):
        out[...] = block[m * n : (m + 1) * n]


def sort_pieces(own, near, far, farthest, projections, others, sent):
    half = farthest.shape[0]
    for r, piece in enumerate((own, near, far, farthest)):
        projections[r] = piece[:half]
    for r, piece in enumerate((own, near, far)):
        others[r] = piece[half:]
    sent[...] = far[half:]


def assemble(*refs):
    own, own_last, other, other_last, weights = refs[0], refs[1:4], refs[4], refs[5:8], refs[8:]
    core, _, _, _, place = places()
    half = weights[0].shape[0] // 8
    for c, (pieces, last) in enumerate(((own, own_last), (other, other_last))):
        for r in range(4):
            base = rows_from((2 * (place ^ r) + (core ^ c)) * half, half)
            for m, weight in enumerate(weights):
                weight[base] = last[m][...] if r == 3 else pieces[r, m * half : (m + 1) * half]


def stack(own, near, far, farthest, out):
    for r, piece in enumerate((own, near, far, farthest)):
        out[r] = piece[...]


def project(seen, *refs):
    pieces, outs = refs[:2], refs[2:]
    rows_in, w_qkv, queries, keys_values, segs, vec, b_inner, stage = outs
    core, _, _, chip, place = places()
    width = seen.shape[2]
    n = width // 32
    tokens = rows_in.shape[0] // CHIPS
    part, half = width // 4, width // 8
    for s in range(CHIPS):
        x = seen.at[chip ^ s]
        rows_in[s * tokens : (s + 1) * tokens] = x[:tokens]
        segs[s : s + 1] = x[tokens : tokens + 1, :tokens].astype(WIDE)
    segs[CHIPS:] = jnp.zeros((8 - CHIPS, tokens), WIDE)
    for r in range(4):
        for c, piece in enumerate(pieces):
            base = rows_from((2 * (place ^ r) + (core ^ c)) * half, half)
            rows = piece[r].astype(WIDE)
            beside = [rows[j * n : (j + 1) * n, 3 * part :] for j in range(3)]
            whole_rows = jnp.concatenate([rows[: 3 * n, : 3 * part], jnp.concatenate(beside, 1)])
            w_qkv[base] = whole_rows.astype(LOW)
            if not c:
                small = [rows[3 * n :, :part], rows[3 * n :, part : 2 * part]]
                stage[place ^ r] = jnp.concatenate(small)
    for k in range(4):
        span = slice(k * part, (k + 1) * part)
        vec[:6, span] = stage[k, :6]
        b_inner[:, span] = stage[k, 6:7]
    vec[6:] = jnp.zeros((2, width), WIDE)
    bias = stage[chip]
    out = dot(rows_in[...], w_qkv[...])
    scale = HEAD_DIM ** (-0.5)
    queries[...] = ((out[:, :part] + bias[7:8]).astype(LOW).astype(WIDE) * scale).astype(LOW)
    keys_values[:, :part] = out[:, part : 2 * part].astype(LOW)
    keys_values[:, part:] = (out[:, 2 * part :] + bias[8:9]).astype(LOW)


def attend(queries, seg_query, keys_values, seg_key, context, probs):
    part = queries.shape[1]
    seg_columns = seg_key[...].T
    seg_row = seg_query[...]
    allowed = jnp.concatenate(
        [seg_columns[:, b : b + 1] == seg_row for b in range(seg_key.shape[0])]
    )
    for h in range(part // HEAD_DIM):
        keys = keys_values[:, h * HEAD_DIM : (h + 1) * HEAD_DIM]
        values = keys_values[:, part + h * HEAD_DIM : part + (h + 1) * HEAD_DIM]
        scores = dot_rt(keys, queries[:, h * HEAD_DIM : (h + 1) * HEAD_DIM])
        scores = jnp.where(allowed, scores, NEGATIVE)
        weights = jnp.exp(scores - jnp.max(scores, 0, keepdims=True))
        weights = (weights * (1.0 / jnp.sum(weights, 0, keepdims=True))).astype(LOW)
        probs[h] = weights
        out = dot_lt(values, weights)
        context[:, h * HEAD_DIM : (h + 1) * HEAD_DIM] = out.T.astype(LOW)


def attend_back(queries, keys_values, grad_context, probs, grad_queries, grad_keys_values):
    part = queries.shape[1]
    scale = HEAD_DIM ** (-0.5)
    for h in range(part // HEAD_DIM):
        span = slice(h * HEAD_DIM, (h + 1) * HEAD_DIM)
        span_v = slice(part + h * HEAD_DIM, part + (h + 1) * HEAD_DIM)
        keys, values = keys_values[:, span], keys_values[:, span_v]
        grads = grad_context[:, span]
        soft = probs[h]
        grad_keys_values[:, span_v] += dot(soft, grads)
        grad_probs = dot_rt(values, grads)
        wide = soft.astype(WIDE)
        delta = jnp.sum(wide * grad_probs, 0, keepdims=True)
        grad_scores = (wide * (grad_probs - delta)).astype(LOW)
        grad_queries[:, span] = (dot_lt(keys, grad_scores) * scale).T.astype(LOW)
        grad_keys_values[:, span] += dot(grad_scores, queries[:, span])


def beside(rows, out):
    tokens, part = out.shape[0], rows.shape[1]
    for t in range(CHIPS):
        out[:, t * part : (t + 1) * part] = rows[t * tokens : (t + 1) * tokens]


def attend_all(queries, kv_own, kv_far, seg_own, seg_far, context, probs, *scratch):
    keys_values, seg_key, seg_query, rows = scratch
    count = kv_own.shape[0]
    tokens = seg_own.shape[1]
    keys_values[:count] = kv_own[...]
    keys_values[count:] = kv_far[...]
    seg_key[:CHIPS] = seg_own[:CHIPS]
    seg_key[CHIPS:] = seg_far[:CHIPS]
    for s in range(CHIPS):
        seg_query[:, s * tokens : (s + 1) * tokens] = seg_own[s : s + 1]
    attend(queries, seg_query, keys_values, seg_key, rows, probs)
    beside(rows, context)


def context_back(g0, g1, g2, g3, w_output, grad_low, grad_context):
    _, _, _, chip, _ = places()
    tokens, part = g0.shape[0], grad_context.shape[1]
    for s, block in enumerate((g0, g1, g2, g3)):
        grad_low[s * tokens : (s + 1) * tokens] = block[...]
    grad_context[...] = dot_rt(grad_low[...], w_output[rows_from(chip * part, part)]).astype(LOW)


def attend_back_all(queries, kv_own, kv_far, g0, g1, g2, g3, w_output, probs, *refs):
    grad_low, grad_queries, grad_own, *grad_far, keys_values, grad_context, total = refs
    count = kv_own.shape[0]
    keys_values[:count] = kv_own[...]
    keys_values[count:] = kv_far[...]
    context_back(g0, g1, g2, g3, w_output, grad_low, grad_context)
    total[...] = jnp.zeros(total.shape, WIDE)
    attend_back(queries, keys_values, grad_context, probs, grad_queries, total)
    grad_own[...] = total[:count]
    tokens = count // CHIPS
    for t, out in enumerate(grad_far):
        out[...] = total[count + t * tokens : count + (t + 1) * tokens].astype(LOW)


def attend_back_block(queries, keys_values, grads, probs, grad_queries, grad_keys_values):
    @pl.when(pl.program_id(0) == 0)
    def _():
        grad_keys_values[...] = jnp.zeros(grad_keys_values.shape, WIDE)

    attend_back(queries, keys_values, grads, probs, grad_queries, grad_keys_values)


def attention_block(queries, keys_values):
    return min(queries.shape[0], 128 * max(1, 2048 // keys_values.shape[0]))


def whole(array):
    return pl.BlockSpec(array.shape, lambda i: (0,) * array.ndim)


def attention(queries, seg_query, keys_values, seg_key):
    count, part = queries.shape
    keys = keys_values.shape[0]
    heads = part // HEAD_DIM
    block = attention_block(queries, keys_values)
    return pl.pallas_call(
        attend,
        grid=(count // block,),
        in_specs=[
            pl.BlockSpec((block, part), lambda i: (i, 0)),
            pl.BlockSpec((1, block), lambda i: (0, i)),
            whole(keys_values),
            whole(seg_key),
        ],
        out_specs=[
            pl.BlockSpec((block, part), lambda i: (i, 0)),
            pl.BlockSpec((heads, keys, block), lambda i: (0, 0, i)),
        ],
        out_shape=[shape((count, part)), shape((heads, keys, count))],
        compiler_params=pltpu.CompilerParams(vmem_limit_bytes=VMEM_BYTES),
    )(queries, seg_query, keys_values, seg_key)


def attention_back(queries, keys_values, grad_context, probs):
    count, part = queries.shape
    keys = keys_values.shape[0]
    block = attention_block(queries, keys_values)
    rows = pl.BlockSpec((block, part), lambda i: (i, 0))
    return pl.pallas_call(
        attend_back_block,
        grid=(count // block,),
        in_specs=[
            rows,
            whole(keys_values),
            rows,
            pl.BlockSpec((probs.shape[0], keys, block), lambda i: (0, 0, i)),
        ],
        out_specs=[rows, pl.BlockSpec((keys, 2 * part), lambda i: (0, 0))],
        out_shape=[shape((count, part)), shape((keys, 2 * part), WIDE)],
        compiler_params=pltpu.CompilerParams(vmem_limit_bytes=VMEM_BYTES),
    )(queries, keys_values, grad_context, probs)


def forward(c0, c1, c2, c3, rows_in, w_output, vec, w_inner, b_inner, w_outer, *outs):
    context_low, unit_one, inverse_one, normed_low, activated, slope = outs[:6]
    own, sent, stage = outs[6], outs[7:10], outs[10]
    _, _, _, chip, _ = places()
    tokens, part = c0.shape[0], c0.shape[1] // CHIPS
    for s, block in enumerate((c0, c1, c2, c3)):
        for t in range(CHIPS):
            stage[chip ^ s, t * tokens : (t + 1) * tokens] = block[
                :, (t ^ s) * part : ((t ^ s) + 1) * part
            ]
    for k in range(CHIPS):
        context_low[:, k * part : (k + 1) * part] = stage[k]
    residual = rows_in[...].astype(WIDE) + dot(context_low[...], w_output[...]) + vec[0:1]
    unit, inverse = normalized(residual)
    unit_one[...] = unit[:tokens]
    inverse_one[...] = inverse[:tokens]
    normed_low[...] = (unit * vec[1:2] + vec[2:3]).astype(LOW)
    inner_pre = dot(normed_low[...], w_inner[...]) + b_inner[...]
    cdf = 0.5 * (1.0 + lax.erf(inner_pre * (0.5**0.5)))
    activated[...] = (inner_pre * cdf).astype(LOW)
    slope[...] = cdf + inner_pre * jnp.exp(-0.5 * inner_pre * inner_pre) * 0.3989422804014327
    parted(dot(activated[...], w_outer[...]), own, sent)


def parted(values, own, sent):
    tokens = own.shape[0]
    own[...] = values[:tokens]
    for s, out in enumerate(sent):
        out[...] = values[(s + 1) * tokens : (s + 2) * tokens].astype(LOW)


def total_of(own, blocks):
    total = own[...]
    for block in blocks:
        total = total + block[...].astype(WIDE)
    return total


def backward_first(own, s1, s2, s3, unit_one, vec, cot, result, grad_summed, grad_outer, sums):
    summed = unit_one[...] * vec[1:2] + vec[2:3] + vec[3:4] + total_of(own, (s1, s2, s3))
    unit, inverse = normalized(summed)
    result[0] = (unit * vec[4:5] + vec[5:6]).astype(LOW)
    c = cot[0].astype(WIDE)
    grad = norm_back(c, unit, inverse, vec[4:5])
    grad_summed[...] = grad
    grad_outer[...] = grad.astype(LOW)
    sums[0:1] = jnp.sum(grad_outer[...].astype(WIDE), 0, keepdims=True)
    sums[1:2] = jnp.sum(c * unit, 0, keepdims=True)
    sums[2:3] = jnp.sum(c, 0, keepdims=True)
    sums[3:] = jnp.zeros((5, sums.shape[1]), WIDE)


def backward_second(g0, g1, g2, g3, slope, w_outer, w_inner, grad_inner, sums, *outs):
    grad_outer = jnp.concatenate([g0[...], g1[...], g2[...], g3[...]])
    grad_inner[...] = (dot_rt(grad_outer, w_outer[...]) * slope[...]).astype(LOW)
    parted(dot_rt(grad_inner[...], w_inner[...]), outs[0], outs[1:])
    sums[...] = jnp.sum(grad_inner[...].astype(WIDE), 0, keepdims=True)


def cut_rows(stage, keep, sent):
    core, _, _, _, place = places()
    half = keep.shape[1]
    for r in range(4):
        for c, out in enumerate((keep.at[r], sent[r])):
            out[...] = stage[rows_from((2 * (place ^ r) + (core ^ c)) * half, half)]


def outer_grads(activated, g0, g1, g2, g3, keep, send, stage):
    grad_outer = jnp.concatenate([g0[...], g1[...], g2[...], g3[...]])
    stage[...] = dot_lt(activated[...], grad_outer).astype(LOW)
    cut_rows(stage, keep, [send.at[r] for r in range(4)])


def inner_grads(normed_low, grad_inner, keep, s0, s1, s2, s3, stage):
    stage[...] = dot_lt(normed_low[...], grad_inner[...]).astype(LOW)
    cut_rows(stage, keep, (s0, s1, s2, s3))


def norm_backward(grad_summed, own, s1, s2, s3, unit_one, inverse_one, vec, grad_own, grad_low, sums):
    grad = grad_summed[...] + total_of(own, (s1, s2, s3))
    unit = unit_one[...]
    branch = norm_back(grad, unit, inverse_one[...], vec[1:2])
    grad_own[...] = branch
    grad_low[...] = branch.astype(LOW)
    sums[0:1] = jnp.sum(grad_low[...].astype(WIDE), 0, keepdims=True)
    sums[1:2] = jnp.sum(grad * unit, 0, keepdims=True)
    sums[2:3] = jnp.sum(grad, 0, keepdims=True)
    sums[3:] = jnp.zeros((5, sums.shape[1]), WIDE)


def output_grads(context_low, grad_low, out):
    _, _, _, chip, _ = places()
    part = out.shape[1]
    for p in range(CHIPS):

        @pl.when(chip == p)
        def _():
            block = grad_low[:, p * part : (p + 1) * part]
            out[...] = dot_lt(context_low[...], block).astype(LOW)


def projection_grads(rows_in, grad_queries, grad_kv, f0, f1, f2, f3, grad_o, *refs):
    (sums_one, sums_two, sums_inner), outs = refs[:3], refs[3:]
    grad_qkv, keep, send, stage = outs
    core, _, _, _, place = places()
    part = grad_queries.shape[1]
    width = 4 * part
    grad_qkv[:, :part] = grad_queries[...]
    far = jnp.concatenate([f0[...], f1[...], f2[...], f3[...]]).astype(WIDE)
    grad_qkv[:, part:] = (grad_kv[...] + far).astype(LOW)
    stage[:, : 3 * part] = dot_lt(rows_in[...], grad_qkv[...]).astype(LOW)
    stage[:, 3 * part :] = grad_o[...]
    half = part // 2
    total = jnp.sum(grad_qkv[...].astype(WIDE), 0, keepdims=True)
    for k in range(4):
        span = slice(k * part, (k + 1) * part)
        small = jnp.concatenate(
            [
                sums_one[:3, span],
                sums_two[:3, span],
                sums_inner[:, span],
                total[:, :part],
                total[:, 2 * part :],
                jnp.zeros((7, part), WIDE),
            ]
        )
        small = jnp.concatenate([small, jnp.zeros((16, width - part), WIDE)], 1).astype(LOW)
        for c, out in enumerate((keep, send)):
            out[place ^ k, half:] = small
            out[place ^ k, :half] = stage[rows_from(k * part + (core ^ c) * half, half)]


def input_grads(grad_qkv, w_qkv, grad_residual, own, s1, s2, s3):
    tokens = own.shape[0]
    grads = dot_rt(grad_qkv[...], w_qkv[...])
    parted(grads, own, (s1, s2, s3))
    own[...] += grad_residual[...]


def add_tokens(own, s1, s2, s3, out, done):
    done[...] = jnp.zeros(done.shape, WIDE)
    out[0] = total_of(own, (s1, s2, s3)).astype(LOW)


def add_near(kept, received, keep, send):
    total = kept[...].astype(WIDE) + received[...].astype(WIDE)
    for r in range(2):
        keep[r] = total[2 * r].astype(LOW)
        send[r] = total[2 * r + 1].astype(LOW)


def add_near_parts(kept, r0, r1, r2, r3, keep, send):
    for r, received in enumerate((r0, r1, r2, r3)):
        out = (keep, send)[r % 2]
        out[r // 2] = (kept[r].astype(WIDE) + received[...].astype(WIDE)).astype(LOW)


def add_far(kept, received, keep, send):
    total = kept[...].astype(WIDE) + received[...].astype(WIDE)
    keep[...] = total[0].astype(LOW)
    send[...] = total[1].astype(LOW)


def add_far_passing(kept, received, other, keep, send, out):
    add_far(kept, received, keep, send)
    out[...] = other[...]


def add_last(kept, received, out):
    out[...] = (kept[...].astype(WIDE) + received[...].astype(WIDE)).astype(LOW)


def add_beside(other, kept, received, out):
    half = kept.shape[0]
    out[:half] = other[...]
    add_last(kept, received, out.at[half:])


def stack_halves(own, near, far, farthest, first, second):
    half = first.shape[1]
    for s, block in enumerate((own, near, far, farthest)):
        first[s] = block[:half]
        second[s] = block[half:]


def unpack_mlp(outer_own, inner_own, outer_other, inner_other, outer, inner, done, stage):
    core, _, _, chip, _ = places()
    half, width = outer_own.shape[1:]
    part = 2 * half
    for s in range(CHIPS):
        for m, (one, two) in enumerate(((outer_own, inner_own), (outer_other, inner_other))):
            far, c = chip ^ s, core ^ m
            outer[rows_from((2 * far + c) * half, half)] = one[s].astype(WIDE)
            stage[c, far] = two[s]
    for c in range(2):
        for p in range(CHIPS):
            for k in range(4):
                start = k * width + p * part
                inner[c * half : (c + 1) * half, start : start + part] = stage[
                    c, p, :, k * part : (k + 1) * part
                ].astype(WIDE)
    done[...] = jnp.zeros(done.shape, WIDE)


def unpack_rest(*refs):
    pieces, mats, vectors, (b_query, b_value, b_inner, stage, small) = (
        refs[:2],
        refs[2:6],
        refs[6:12],
        refs[12:],
    )
    core, _, _, chip, place = places()
    part = mats[0].shape[0]
    half = part // 2
    for s in range(CHIPS):
        for m, blocks in enumerate(pieces):
            stage[core ^ m, s] = blocks[s, :half]
        small[s] = pieces[0][s, half:, :part].astype(WIDE)
    for c in range(2):
        for k in range(CHIPS):
            for j, out in enumerate(mats):
                out[c * half : (c + 1) * half, k * part : (k + 1) * part] = stage[
                    c, k, :, j * part : (j + 1) * part
                ].astype(WIDE)
    total = small[0] + small[1] + small[2] + small[3]
    for i, out in enumerate(vectors):
        out[...] = total[i]
    biases = small[place]
    b_query[...] = biases[7]
    b_value[...] = biases[8]
    for p in range(CHIPS):
        b_inner[p * part : (p + 1) * part] = small[p][6]


def per_device(
    inputs,
    segments,
    query_weight,
    query_bias,
    key_weight,
    value_weight,
    value_bias,
    output_weight,
    output_bias,
    first_gain,
    first_shift,
    inner_weight,
    inner_bias,
    outer_weight,
    outer_bias,
    second_gain,
    second_shift,
    cotangent,
):
    groups = lax.axis_size("ctx") // TEAM
    lines = [[m + TEAM * g for g in range(groups)] for m in range(TEAM)]
    tokens, width = inputs.shape[1:]
    part = query_weight.shape[0]
    hidden = outer_weight.shape[0]
    count, half = CHIPS * tokens, part // 2
    heads = part // HEAD_DIM
    head = 3 * half // 4 + 8

    def chips(block):
        return [partner(block, "ctx", s << 1) for s in (1, 2, 3)]

    def exchanged(blocks):
        return [partner(block, "ctx", (s + 1) << 1) for s, block in enumerate(blocks)]

    def joined(block):
        return partner(block, "ctx", CORE)

    (own,) = kernel(
        prepare_tokens,
        [shape((tokens + 16, width))],
        inputs,
        segments,
        scratch=[pltpu.VMEM((1, tokens), jnp.int32)],
        loads=2,
    )
    teams = [[c + TEAM * g + 2 * n for n in range(CHIPS)] for g in range(groups) for c in range(2)]
    seen = lax.all_gather(own, "ctx", axis_index_groups=teams)
    (first,) = kernel(
        prepare_weights,
        [shape((head + 3 * half, width))],
        query_weight,
        key_weight,
        value_weight,
        output_weight,
        inner_weight,
        outer_weight,
        output_bias,
        first_gain,
        first_shift,
        outer_bias,
        second_gain,
        second_shift,
        inner_bias,
        query_bias,
        value_bias,
        scratch=[
            pltpu.VMEM((3, half, width), LOW),
            pltpu.VMEM((half, 4 * width), LOW),
            *[pltpu.VMEM((part,), LOW)] * 6,
            pltpu.VMEM((hidden,), LOW),
            *[pltpu.VMEM((part,), LOW)] * 2,
        ],
        loads=15,
    )
    (mine,) = kernel(first_rows, [shape((head, width))], first, after=(seen,))
    line = [first, partner(first, "fsdp", 1), partner(first, "fsdp", 2), partner(mine, "fsdp", 3)]
    projections, others, sent = kernel(
        sort_pieces,
        [shape((4, head, width)), shape((3, 3 * half, width)), shape((3 * half, width))],
        *line,
    )
    last = partner(sent, "fsdp", 1)

    rows_in, w_qkv, queries, kv_own, segs, vec, b_inner = kernel(
        project,
        [
            shape((count, width)),
            shape((width, 3 * part)),
            shape((count, part)),
            shape((count, 2 * part)),
            shape((8, tokens), WIDE),
            shape((8, width), WIDE),
            shape((1, width), WIDE),
        ],
        seen,
        projections,
        joined(projections),
        scratch=[pltpu.VMEM((4, 16, part), WIDE)],
    )
    kv_far, seg_far = partner(kv_own, "ctx", CORE), partner(segs, "ctx", CORE)
    if groups == 1:
        context, probs = kernel(
            attend_all,
            [shape((tokens, width)), shape((heads, 2 * count, count))],
            queries,
            kv_own,
            kv_far,
            segs,
            seg_far,
            scratch=[
                pltpu.VMEM((2 * count, 2 * part), LOW),
                pltpu.VMEM((2 * CHIPS, tokens), WIDE),
                pltpu.VMEM((1, count), WIDE),
                pltpu.VMEM((count, part), LOW),
            ],
            room=24,
        )
    else:
        kv = jnp.concatenate([kv_own, kv_far])
        seg_key = jnp.concatenate([segs[:CHIPS], seg_far[:CHIPS]])
        kv = lax.all_gather(kv, "ctx", axis=0, tiled=True, axis_index_groups=lines)
        seg_key = lax.all_gather(seg_key, "ctx", axis=0, tiled=True, axis_index_groups=lines)
        rows, probs = attention(queries, segs[:CHIPS].reshape(1, count), kv, seg_key)
        (context,) = kernel(beside, [shape((tokens, width))], rows)

    contexts = [context] + chips(context)
    last = kernel(
        split_rows, [shape((half, width))] * 3, last, after=(context,)
    )
    w_output, w_inner, w_outer = kernel(
        assemble, [shape((width, width))] * 3, others, *last, joined(others), *map(joined, last)
    )
    context_low, unit_one, inverse_one, normed_low, activated, slope, *outer_sent = kernel(
        forward,
        [
            shape((count, width)),
            shape((tokens, width), WIDE),
            shape((tokens, 1), WIDE),
            shape((count, width)),
            shape((count, width)),
            shape((count, width), WIDE),
            shape((tokens, width), WIDE),
        ]
        + [shape((tokens, width))] * 3,
        *contexts,
        rows_in,
        w_output,
        vec,
        w_inner,
        b_inner,
        w_outer,
        scratch=[pltpu.VMEM((CHIPS, count, part), LOW)],
        room=16,
    )
    result, grad_summed, grad_outer, sums_one = kernel(
        backward_first,
        [
            shape((1, tokens, width)),
            shape((tokens, width), WIDE),
            shape((tokens, width)),
            shape((8, width), WIDE),
        ],
        outer_sent[0],
        *exchanged(outer_sent[1:]),
        unit_one,
        vec,
        cotangent,
        last=(0,),
    )
    grads_outer = [grad_outer] + chips(grad_outer)
    outer_kept, outer_sent = kernel(
        outer_grads,
        [shape((4, half, width))] * 2,
        activated,
        *grads_outer,
        scratch=[pltpu.VMEM((width, width), LOW)],
    )
    grad_inner, sums_inner, inner_own, *inner_sent = kernel(
        backward_second,
        [shape((count, width)), shape((1, width), WIDE), shape((tokens, width), WIDE)]
        + [shape((tokens, width))] * 3,
        *grads_outer,
        slope,
        w_outer,
        w_inner,
        room=12,
    )
    inner_far = exchanged(inner_sent)

    def near_sum(kept, sent):
        received = partner(sent, "ctx", CORE)
        return kernel(add_near, [shape((2,) + kept.shape[1:])] * 2, kept, received)

    def far_sum(kept, sent, after=()):
        received = partner(sent, "fsdp", 1)
        return kernel(add_far, [shape(kept.shape[1:])] * 2, kept, received, after=after)

    def last_sum(kept, sent, after=()):
        received = partner(sent, "fsdp", 2)
        (total,) = kernel(add_last, [shape(kept.shape)], kept, received, after=after)
        if groups > 1:
            total = lax.psum(total.astype(WIDE), "ctx", axis_index_groups=lines).astype(LOW)
        return total

    inner_kept, *inner_sent = kernel(
        inner_grads,
        [shape((4, half, width))] + [shape((half, width))] * 4,
        normed_low,
        grad_inner,
        scratch=[pltpu.VMEM((width, width), LOW)],
    )
    inner_kept, inner_sent = kernel(
        add_near_parts,
        [shape((2, half, width))] * 2,
        inner_kept,
        *(partner(block, "ctx", CORE) for block in inner_sent),
    )
    outer_kept, outer_sent = near_sum(outer_kept, outer_sent)
    outer_kept, outer_sent, inner_sent = kernel(
        add_far_passing,
        [shape((half, width))] * 2 + [shape((2, half, width))],
        outer_kept,
        partner(outer_sent, "fsdp", 1),
        inner_sent,
    )
    inner_far_sum = far_sum(inner_kept, inner_sent)
    outer_total = last_sum(outer_kept, outer_sent)
    grad_residual, grad_low, sums_two = kernel(
        norm_backward,
        [shape((tokens, width), WIDE), shape((tokens, width)), shape((8, width), WIDE)],
        grad_summed,
        inner_own,
        *inner_far,
        unit_one,
        inverse_one,
        vec,
    )
    grads_low = [grad_low] + chips(grad_low)
    if groups == 1:
        grad_low, grad_queries, grad_kv, *grad_kv_sent = kernel(
            attend_back_all,
            [
                shape((count, width)),
                shape((count, part)),
                shape((count, 2 * part), WIDE),
            ]
            + [shape((tokens, 2 * part))] * CHIPS,
            queries,
            kv_own,
            kv_far,
            *grads_low,
            w_output,
            probs,
            scratch=[
                pltpu.VMEM((2 * count, 2 * part), LOW),
                pltpu.VMEM((count, part), LOW),
                pltpu.VMEM((2 * count, 2 * part), WIDE),
            ],
            room=24,
            after=(outer_kept,),
        )
    else:
        grad_low, grad_context = kernel(
            context_back, [shape((count, width)), shape((count, part))], *grads_low, w_output
        )
        grad_queries, grad_kv = attention_back(queries, kv, grad_context, probs)
        grad_kv = grad_kv.reshape(groups, 2, count, 2 * part).transpose(1, 0, 2, 3)
        grad_kv = lax.psum_scatter(
            grad_kv.reshape(2, groups * count, 2 * part),
            "ctx",
            scatter_dimension=1,
            tiled=True,
            axis_index_groups=lines,
        )
        grad_kv, grad_kv_sent = grad_kv[0], jnp.split(grad_kv[1].astype(LOW), CHIPS)
    grad_kv_far = [joined(block) for block in grad_kv_sent]
    (grad_o,) = kernel(output_grads, [shape((width, part))], context_low, grad_low)
    cut = shape((4, half + 16, width))
    grad_qkv, rest_kept, rest_sent = kernel(
        projection_grads,
        [shape((count, 3 * part)), cut, cut],
        rows_in,
        grad_queries,
        grad_kv,
        *grad_kv_far,
        grad_o,
        sums_one,
        sums_two,
        sums_inner,
        scratch=[pltpu.VMEM((width, width), LOW)],
        after=(outer_total, inner_far_sum[0]),
    )
    rest_near = near_sum(rest_kept, rest_sent)
    input_own, *input_sent = kernel(
        input_grads,
        [shape((tokens, width), WIDE)] + [shape((tokens, width))] * 3,
        grad_qkv,
        w_qkv,
        grad_residual,
        after=tuple(rest_near),
    )
    input_far = exchanged(input_sent)

    rest_far = far_sum(*rest_near)
    (mlp_total,) = kernel(
        add_beside,
        [shape((2 * half, width))],
        outer_total,
        inner_far_sum[0],
        partner(inner_far_sum[1], "fsdp", 2),
        after=(*input_far, rest_far[0]),
    )
    rest_total = last_sum(*rest_far)
    rest_all = lax.all_gather(rest_total, "ctx", axis_index_groups=teams)
    mlp_blocks = kernel(
        stack_halves,
        [shape((CHIPS, half, width))] * 2,
        mlp_total,
        *chips(mlp_total),
        after=(rest_all,),
    )
    grad_input, done_input = kernel(
        add_tokens,
        [shape((1, tokens, width)), shape((8, 128), WIDE)],
        input_own,
        *input_far,
        last=(0,),
        after=(rest_total,),
    )
    g_outer, g_inner, done_mlp = kernel(
        unpack_mlp,
        [
            shape((hidden, width), WIDE),
            shape((part, 4 * hidden), WIDE),
            shape((8, 128), WIDE),
        ],
        *mlp_blocks,
        *map(joined, mlp_blocks),
        last=(0, 1),
        scratch=[pltpu.VMEM((2, CHIPS, half, width), LOW)],
        room=12,
        after=(rest_all,),
    )
    g_query, g_key, g_value, g_output, *vec, g_b_query, g_b_value, g_b_inner = kernel(
        unpack_rest,
        [shape((part, width), WIDE)] * 4
        + [shape((part,), WIDE)] * 8
        + [shape((width,), WIDE)],
        rest_all,
        joined(rest_all),
        last=range(13),
        scratch=[
            pltpu.VMEM((2, CHIPS, half, width), LOW),
            pltpu.VMEM((CHIPS, 16, part), WIDE),
        ],
        room=12,
    )
    return (
        result,
        grad_input,
        g_query,
        g_b_query,
        g_key,
        g_value,
        g_b_value,
        g_output,
        vec[3],
        vec[4],
        vec[5],
        g_inner,
        g_b_inner,
        g_outer,
        vec[0],
        vec[1],
        vec[2],
    )


def solution(mesh):
    rows, cuts, whole = P("fsdp", "ctx", None), P("fsdp", None), P("fsdp")
    params = (cuts, whole, cuts, cuts, whole, cuts, whole, whole, whole)
    params += (cuts, whole, cuts, whole, whole, whole)
    return jax.shard_map(
        per_device,
        mesh=mesh,
        in_specs=(rows, P("fsdp", "ctx")) + params + (rows,),
        out_specs=(rows, rows) + params,
        check_vma=False,
    )
```

```python
import functools

import jax
import jax.numpy as jnp
from jax import lax
from jax.experimental import pallas as pl
from jax.experimental.pallas import tpu as pltpu
from jax.sharding import PartitionSpec as P

HEAD_DIM = 64
NEGATIVE = -1000000000.0
EPSILON = 1e-12
LOW = jnp.bfloat16
WIDE = jnp.float32

CORE, SIDE, ROW = 1, 2, 4
TEAM = 8
CHIPS = 4
VMEM_BYTES = 56 << 20


def partner(block, axis, bit):
    devices = range(lax.axis_size(axis))
    return lax.ppermute(block, axis, [(i, i ^ bit) for i in devices])


def dot(left, right):
    return jnp.dot(left, right, preferred_element_type=WIDE)


def dot_rt(left, right):
    return lax.dot_general(left, right, (((1,), (1,)), ((), ())), preferred_element_type=WIDE)


def dot_lt(left, right):
    return lax.dot_general(left, right, (((0,), (0,)), ((), ())), preferred_element_type=WIDE)


def shape(dims, dtype=LOW):
    return jax.ShapeDtypeStruct(tuple(dims), dtype)


def kernel(body, outs, *args, scratch=(), room=8, last=(), after=(), loads=0):
    spec = pl.BlockSpec(memory_space=pltpu.VMEM)
    off = pl.BlockSpec(memory_space=pl.ANY)
    place = pltpu.HBM if loads else pltpu.VMEM
    args = tuple(pltpu.with_memory_space_constraint(a, place) for a in args)
    waits = len(after)

    def step(*refs):
        body(*refs[waits:])

    sems = [pltpu.SemaphoreType.DMA((loads,))] if loads else []
    return pl.pallas_call(
        step,
        out_shape=[
            o if n in last else pltpu.VMEM(o.shape, o.dtype) for n, o in enumerate(outs)
        ],
        in_specs=[off] * waits + [off if loads else spec] * len(args),
        out_specs=[spec] * len(outs),
        scratch_shapes=list(scratch) + sems,
        compiler_params=pltpu.CompilerParams(vmem_limit_bytes=room << 20),
        cost_estimate=pl.CostEstimate(flops=1, bytes_accessed=1, transcendentals=0),
    )(*after, *args)


def load(sems, *pairs):
    copies = [
        pltpu.make_async_copy(source, target, sems.at[n])
        for n, (source, target) in enumerate(pairs)
    ]
    for copy in copies:
        copy.start()
    return copies


def places():
    index, place = lax.axis_index("ctx"), lax.axis_index("fsdp")
    core, side, row = index & 1, (index >> 1) & 1, (index >> 2) & 1
    return core, side, row, (index >> 1) & 3, place


def rows_from(start, count):
    return pl.ds(pl.multiple_of(start, 16), count)


def normalized(values):
    center = values - jnp.mean(values, -1, keepdims=True)
    inverse = lax.rsqrt(jnp.mean(center * center, -1, keepdims=True) + EPSILON)
    return center * inverse, inverse


def norm_back(grad, unit, inverse, gain):
    scaled = grad * gain
    return inverse * (
        scaled
        - jnp.mean(scaled, -1, keepdims=True)
        - unit * jnp.mean(scaled * unit, -1, keepdims=True)
    )


def lines_of(*vectors):
    rows = [v[...].astype(WIDE).reshape(1, v.shape[0]) for v in vectors]
    return jnp.concatenate(rows + [jnp.zeros((16 - len(rows), rows[0].shape[1]), WIDE)])


def prepare_tokens(x, seg, own, line, sems):
    tokens, width = x.shape[1:]
    for copy in load(sems, (seg, line), (x.at[0], own.at[pl.ds(0, tokens)])):
        copy.wait()
    seg_row = jnp.broadcast_to(line[...].astype(WIDE), (16, tokens)).astype(LOW)
    own[tokens:, :tokens] = seg_row
    own[tokens:, tokens:] = jnp.zeros((16, width - tokens), LOW)


def prepare_weights(wq, wk, wv, wo, wi, wu, *refs):
    vectors, first, (blocks, block), lines, sems = (
        refs[:9],
        refs[9],
        refs[10:12],
        refs[12:21],
        refs[21],
    )
    core, _, _, chip, _ = places()
    part, width = wq.shape
    half = part // 2
    most = 3 * half // 4
    head = most + 8
    rows = rows_from(core * half, half)
    pairs = [(w.at[rows], blocks.at[j]) for j, w in enumerate((wq, wk, wv))]
    pairs += [(wi.at[rows], block), (wo.at[rows], first.at[pl.ds(head, half)])]
    rows = rows_from((2 * chip + core) * half, half)
    pairs += [(wu.at[rows], first.at[pl.ds(head + 2 * half, half)])]
    for copy in load(sems, *pairs, *zip(vectors, lines)):
        copy.wait()
    six, bias_inner, biases = lines_of(*lines[:6]), lines_of(lines[6]), lines_of(*lines[7:])
    for p in range(CHIPS):

        @pl.when(chip == p)
        def _():
            span = slice(p * part, (p + 1) * part)
            three = [blocks[j, :, span].astype(WIDE) for j in range(3)]
            for k in range(4):
                start = k * width + p * part
                first[head + half : head + 2 * half, k * part : (k + 1) * part] = block[
                    :, start : start + part
                ]
            small = jnp.concatenate([six[:6], bias_inner[:1, span], biases[:1]])
            after = jnp.concatenate([biases[1:2], jnp.zeros((7, part), WIDE)])
            small = jnp.concatenate([small, after, jnp.zeros((8, 2 * part), WIDE)], 1)
            beside = jnp.concatenate([block[most:] for block in three])
            rows_q = jnp.concatenate([block[:most] for block in three] + [beside], 1)
            first[:head] = jnp.concatenate([rows_q, small]).astype(LOW)


def first_rows(block, out):
    out[...] = block[: out.shape[0]]


def passed(block, out):
    out[...] = block[...]


def split_rows(block, *outs):
    n = outs[0].shape[0]
    for m, out in enumerate(outs):
        out[...] = block[m * n : (m + 1) * n]


def sort_pieces(own, near, far, farthest, projections, others, sent):
    half = farthest.shape[0]
    for r, piece in enumerate((own, near, far, farthest)):
        projections[r] = piece[:half]
    for r, piece in enumerate((own, near, far)):
        others[r] = piece[half:]
    sent[...] = far[half:]


def assemble(*refs):
    own, own_last, other, other_last, weights = refs[0], refs[1:4], refs[4], refs[5:8], refs[8:]
    core, _, _, _, place = places()
    half = weights[0].shape[0] // 8
    for c, (pieces, last) in enumerate(((own, own_last), (other, other_last))):
        for r in range(4):
            base = rows_from((2 * (place ^ r) + (core ^ c)) * half, half)
            for m, weight in enumerate(weights):
                weight[base] = last[m][...] if r == 3 else pieces[r, m * half : (m + 1) * half]


def stack(own, near, far, farthest, out):
    for r, piece in enumerate((own, near, far, farthest)):
        out[r] = piece[...]


def project(seen, *refs):
    pieces, outs = refs[:2], refs[2:]
    rows_in, w_qkv, queries, keys_values, segs, vec, b_inner, stage = outs
    core, _, _, chip, place = places()
    width = seen.shape[2]
    n = width // 32
    tokens = rows_in.shape[0] // CHIPS
    part, half = width // 4, width // 8
    for s in range(CHIPS):
        x = seen.at[chip ^ s]
        rows_in[s * tokens : (s + 1) * tokens] = x[:tokens]
        segs[s : s + 1] = x[tokens : tokens + 1, :tokens].astype(WIDE)
    segs[CHIPS:] = jnp.zeros((8 - CHIPS, tokens), WIDE)
    for r in range(4):
        for c, piece in enumerate(pieces):
            base = rows_from((2 * (place ^ r) + (core ^ c)) * half, half)
            rows = piece[r].astype(WIDE)
            beside = [rows[j * n : (j + 1) * n, 3 * part :] for j in range(3)]
            whole_rows = jnp.concatenate([rows[: 3 * n, : 3 * part], jnp.concatenate(beside, 1)])
            w_qkv[base] = whole_rows.astype(LOW)
            if not c:
                small = [rows[3 * n :, :part], rows[3 * n :, part : 2 * part]]
                stage[place ^ r] = jnp.concatenate(small)
    for k in range(4):
        span = slice(k * part, (k + 1) * part)
        vec[:6, span] = stage[k, :6]
        b_inner[:, span] = stage[k, 6:7]
    vec[6:] = jnp.zeros((2, width), WIDE)
    bias = stage[chip]
    out = dot(rows_in[...], w_qkv[...])
    scale = HEAD_DIM ** (-0.5)
    queries[...] = ((out[:, :part] + bias[7:8]).astype(LOW).astype(WIDE) * scale).astype(LOW)
    keys_values[:, :part] = out[:, part : 2 * part].astype(LOW)
    keys_values[:, part:] = (out[:, 2 * part :] + bias[8:9]).astype(LOW)


def attend(queries, seg_query, keys_values, seg_key, context, probs):
    part = queries.shape[1]
    seg_columns = seg_key[...].T
    seg_row = seg_query[...]
    allowed = jnp.concatenate(
        [seg_columns[:, b : b + 1] == seg_row for b in range(seg_key.shape[0])]
    )
    for h in range(part // HEAD_DIM):
        keys = keys_values[:, h * HEAD_DIM : (h + 1) * HEAD_DIM]
        values = keys_values[:, part + h * HEAD_DIM : part + (h + 1) * HEAD_DIM]
        scores = dot_rt(keys, queries[:, h * HEAD_DIM : (h + 1) * HEAD_DIM])
        scores = jnp.where(allowed, scores, NEGATIVE)
        weights = jnp.exp(scores - jnp.max(scores, 0, keepdims=True))
        weights = (weights * (1.0 / jnp.sum(weights, 0, keepdims=True))).astype(LOW)
        probs[h] = weights
        out = dot_lt(values, weights)
        context[:, h * HEAD_DIM : (h + 1) * HEAD_DIM] = out.T.astype(LOW)


def attend_back(
    queries, keys_values, grad_context, probs, grad_queries, grad_keys_values, whole=True
):
    def add(span, term):
        return term if whole else grad_keys_values[:, span] + term

    part = queries.shape[1]
    scale = HEAD_DIM ** (-0.5)
    for h in range(part // HEAD_DIM):
        span = slice(h * HEAD_DIM, (h + 1) * HEAD_DIM)
        span_v = slice(part + h * HEAD_DIM, part + (h + 1) * HEAD_DIM)
        keys, values = keys_values[:, span], keys_values[:, span_v]
        grads = grad_context[:, span]
        soft = probs[h]
        grad_keys_values[:, span_v] = add(span_v, dot(soft, grads))
        grad_probs = dot_rt(values, grads)
        wide = soft.astype(WIDE)
        delta = jnp.sum(wide * grad_probs, 0, keepdims=True)
        grad_scores = (wide * (grad_probs - delta)).astype(LOW)
        grad_queries[:, span] = (dot_lt(keys, grad_scores) * scale).T.astype(LOW)
        grad_keys_values[:, span] = add(span, dot(grad_scores, queries[:, span]))


def beside(rows, out):
    tokens, part = out.shape[0], rows.shape[1]
    for t in range(CHIPS):
        out[:, t * part : (t + 1) * part] = rows[t * tokens : (t + 1) * tokens]


def attend_all(queries, kv_own, kv_far, seg_own, seg_far, context, probs, *scratch):
    keys_values, seg_key, seg_query, rows = scratch
    count = kv_own.shape[0]
    tokens = seg_own.shape[1]
    keys_values[:count] = kv_own[...]
    keys_values[count:] = kv_far[...]
    seg_key[:CHIPS] = seg_own[:CHIPS]
    seg_key[CHIPS:] = seg_far[:CHIPS]
    for s in range(CHIPS):
        seg_query[:, s * tokens : (s + 1) * tokens] = seg_own[s : s + 1]
    attend(queries, seg_query, keys_values, seg_key, rows, probs)
    beside(rows, context)


def context_back(g0, g1, g2, g3, w_output, grad_low, grad_context):
    _, _, _, chip, _ = places()
    tokens, part = g0.shape[0], grad_context.shape[1]
    for s, block in enumerate((g0, g1, g2, g3)):
        grad_low[s * tokens : (s + 1) * tokens] = block[...]
    grad_context[...] = dot_rt(grad_low[...], w_output[rows_from(chip * part, part)]).astype(LOW)


def attend_back_all(queries, kv_own, kv_far, g0, g1, g2, g3, w_output, probs, *refs):
    grad_low, grad_queries, grad_own, *grad_far, keys_values, grad_context, total = refs
    count = kv_own.shape[0]
    keys_values[:count] = kv_own[...]
    keys_values[count:] = kv_far[...]
    context_back(g0, g1, g2, g3, w_output, grad_low, grad_context)
    attend_back(queries, keys_values, grad_context, probs, grad_queries, total)
    grad_own[...] = total[:count]
    tokens = count // CHIPS
    for t, out in enumerate(grad_far):
        out[...] = total[count + t * tokens : count + (t + 1) * tokens].astype(LOW)


def attend_back_block(queries, keys_values, grads, probs, grad_queries, grad_keys_values):
    @pl.when(pl.program_id(0) == 0)
    def _():
        grad_keys_values[...] = jnp.zeros(grad_keys_values.shape, WIDE)

    attend_back(queries, keys_values, grads, probs, grad_queries, grad_keys_values, False)


def attention_block(queries, keys_values):
    return min(queries.shape[0], 128 * max(1, 2048 // keys_values.shape[0]))


def whole(array):
    return pl.BlockSpec(array.shape, lambda i: (0,) * array.ndim)


def attention(queries, seg_query, keys_values, seg_key):
    count, part = queries.shape
    keys = keys_values.shape[0]
    heads = part // HEAD_DIM
    block = attention_block(queries, keys_values)
    return pl.pallas_call(
        attend,
        grid=(count // block,),
        in_specs=[
            pl.BlockSpec((block, part), lambda i: (i, 0)),
            pl.BlockSpec((1, block), lambda i: (0, i)),
            whole(keys_values),
            whole(seg_key),
        ],
        out_specs=[
            pl.BlockSpec((block, part), lambda i: (i, 0)),
            pl.BlockSpec((heads, keys, block), lambda i: (0, 0, i)),
        ],
        out_shape=[shape((count, part)), shape((heads, keys, count))],
        compiler_params=pltpu.CompilerParams(vmem_limit_bytes=VMEM_BYTES),
    )(queries, seg_query, keys_values, seg_key)


def attention_back(queries, keys_values, grad_context, probs):
    count, part = queries.shape
    keys = keys_values.shape[0]
    block = attention_block(queries, keys_values)
    rows = pl.BlockSpec((block, part), lambda i: (i, 0))
    return pl.pallas_call(
        attend_back_block,
        grid=(count // block,),
        in_specs=[
            rows,
            whole(keys_values),
            rows,
            pl.BlockSpec((probs.shape[0], keys, block), lambda i: (0, 0, i)),
        ],
        out_specs=[rows, pl.BlockSpec((keys, 2 * part), lambda i: (0, 0))],
        out_shape=[shape((count, part)), shape((keys, 2 * part), WIDE)],
        compiler_params=pltpu.CompilerParams(vmem_limit_bytes=VMEM_BYTES),
    )(queries, keys_values, grad_context, probs)


def forward(c0, c1, c2, c3, rows_in, w_output, vec, w_inner, b_inner, w_outer, *outs):
    context_low, unit_one, inverse_one, normed_low, activated, slope = outs[:6]
    own, sent, stage = outs[6], outs[7:10], outs[10]
    _, _, _, chip, _ = places()
    tokens, part = c0.shape[0], c0.shape[1] // CHIPS
    for s, block in enumerate((c0, c1, c2, c3)):
        for t in range(CHIPS):
            stage[chip ^ s, t * tokens : (t + 1) * tokens] = block[
                :, (t ^ s) * part : ((t ^ s) + 1) * part
            ]
    for k in range(CHIPS):
        context_low[:, k * part : (k + 1) * part] = stage[k]
    residual = rows_in[...].astype(WIDE) + dot(context_low[...], w_output[...]) + vec[0:1]
    unit, inverse = normalized(residual)
    unit_one[...] = unit[:tokens]
    inverse_one[...] = inverse[:tokens]
    normed_low[...] = (unit * vec[1:2] + vec[2:3]).astype(LOW)
    inner_pre = dot(normed_low[...], w_inner[...]) + b_inner[...]
    cdf = 0.5 * (1.0 + lax.erf(inner_pre * (0.5**0.5)))
    activated[...] = (inner_pre * cdf).astype(LOW)
    slope[...] = cdf + inner_pre * jnp.exp(-0.5 * inner_pre * inner_pre) * 0.3989422804014327
    parted(dot(activated[...], w_outer[...]), own, sent)


def parted(values, own, sent):
    tokens = own.shape[0]
    own[...] = values[:tokens]
    for s, out in enumerate(sent):
        out[...] = values[(s + 1) * tokens : (s + 2) * tokens].astype(LOW)


def total_of(own, blocks):
    total = own[...]
    for block in blocks:
        total = total + block[...].astype(WIDE)
    return total


def backward_first(own, s1, s2, s3, unit_one, vec, cot, result, grad_summed, grad_outer, sums):
    summed = unit_one[...] * vec[1:2] + vec[2:3] + vec[3:4] + total_of(own, (s1, s2, s3))
    unit, inverse = normalized(summed)
    result[0] = (unit * vec[4:5] + vec[5:6]).astype(LOW)
    c = cot[0].astype(WIDE)
    grad = norm_back(c, unit, inverse, vec[4:5])
    grad_summed[...] = grad
    grad_outer[...] = grad.astype(LOW)
    sums[0:1] = jnp.sum(grad_outer[...].astype(WIDE), 0, keepdims=True)
    sums[1:2] = jnp.sum(c * unit, 0, keepdims=True)
    sums[2:3] = jnp.sum(c, 0, keepdims=True)
    sums[3:] = jnp.zeros((5, sums.shape[1]), WIDE)


def backward_second(g0, g1, g2, g3, slope, w_outer, w_inner, grad_inner, sums, *outs):
    grad_outer = jnp.concatenate([g0[...], g1[...], g2[...], g3[...]])
    grad_inner[...] = (dot_rt(grad_outer, w_outer[...]) * slope[...]).astype(LOW)
    parted(dot_rt(grad_inner[...], w_inner[...]), outs[0], outs[1:])
    sums[...] = jnp.sum(grad_inner[...].astype(WIDE), 0, keepdims=True)


def cut_rows(stage, keep, sent):
    core, _, _, _, place = places()
    half = keep.shape[1]
    for r in range(4):
        for c, out in enumerate((keep.at[r], sent[r])):
            out[...] = stage[rows_from((2 * (place ^ r) + (core ^ c)) * half, half)]


def outer_grads(activated, g0, g1, g2, g3, keep, send, stage):
    grad_outer = jnp.concatenate([g0[...], g1[...], g2[...], g3[...]])
    stage[...] = dot_lt(activated[...], grad_outer).astype(LOW)
    cut_rows(stage, keep, [send.at[r] for r in range(4)])


def inner_grads(normed_low, grad_inner, keep, s0, s1, s2, s3, stage):
    stage[...] = dot_lt(normed_low[...], grad_inner[...]).astype(LOW)
    cut_rows(stage, keep, (s0, s1, s2, s3))


def norm_backward(grad_summed, own, s1, s2, s3, unit_one, inverse_one, vec, grad_own, grad_low, sums):
    grad = grad_summed[...] + total_of(own, (s1, s2, s3))
    unit = unit_one[...]
    branch = norm_back(grad, unit, inverse_one[...], vec[1:2])
    grad_own[...] = branch
    grad_low[...] = branch.astype(LOW)
    sums[0:1] = jnp.sum(grad_low[...].astype(WIDE), 0, keepdims=True)
    sums[1:2] = jnp.sum(grad * unit, 0, keepdims=True)
    sums[2:3] = jnp.sum(grad, 0, keepdims=True)
    sums[3:] = jnp.zeros((5, sums.shape[1]), WIDE)


def output_grads(context_low, grad_low, out):
    _, _, _, chip, _ = places()
    part = out.shape[1]
    for p in range(CHIPS):

        @pl.when(chip == p)
        def _():
            block = grad_low[:, p * part : (p + 1) * part]
            out[...] = dot_lt(context_low[...], block).astype(LOW)


def projection_grads(rows_in, grad_queries, grad_kv, f0, f1, f2, f3, grad_o, *refs):
    (sums_one, sums_two, sums_inner), outs = refs[:3], refs[3:]
    grad_qkv, keep, send, stage = outs
    core, _, _, _, place = places()
    part = grad_queries.shape[1]
    width = 4 * part
    grad_qkv[:, :part] = grad_queries[...]
    far = jnp.concatenate([f0[...], f1[...], f2[...], f3[...]]).astype(WIDE)
    grad_qkv[:, part:] = (grad_kv[...] + far).astype(LOW)
    stage[:, : 3 * part] = dot_lt(rows_in[...], grad_qkv[...]).astype(LOW)
    stage[:, 3 * part :] = grad_o[...]
    half = part // 2
    total = jnp.sum(grad_qkv[...].astype(WIDE), 0, keepdims=True)
    for k in range(4):
        span = slice(k * part, (k + 1) * part)
        small = jnp.concatenate(
            [
                sums_one[:3, span],
                sums_two[:3, span],
                sums_inner[:, span],
                total[:, :part],
                total[:, 2 * part :],
                jnp.zeros((7, part), WIDE),
            ]
        )
        small = jnp.concatenate([small, jnp.zeros((16, width - part), WIDE)], 1).astype(LOW)
        for c, out in enumerate((keep, send)):
            out[place ^ k, half:] = small
            out[place ^ k, :half] = stage[rows_from(k * part + (core ^ c) * half, half)]


def input_grads(grad_qkv, w_qkv, grad_residual, own, s1, s2, s3):
    tokens = own.shape[0]
    grads = dot_rt(grad_qkv[...], w_qkv[...])
    parted(grads, own, (s1, s2, s3))
    own[...] += grad_residual[...]


def add_tokens(own, s1, s2, s3, out, done):
    done[...] = jnp.zeros(done.shape, WIDE)
    out[0] = total_of(own, (s1, s2, s3)).astype(LOW)


def add_near(kept, received, keep, send):
    total = kept[...].astype(WIDE) + received[...].astype(WIDE)
    for r in range(2):
        keep[r] = total[2 * r].astype(LOW)
        send[r] = total[2 * r + 1].astype(LOW)


def add_near_parts(kept, r0, r1, r2, r3, keep, send):
    for r, received in enumerate((r0, r1, r2, r3)):
        out = (keep, send)[r % 2]
        out[r // 2] = (kept[r].astype(WIDE) + received[...].astype(WIDE)).astype(LOW)


def add_far(kept, received, keep, send):
    total = kept[...].astype(WIDE) + received[...].astype(WIDE)
    keep[...] = total[0].astype(LOW)
    send[...] = total[1].astype(LOW)


def add_far_passing(kept, received, other, keep, send, out):
    add_far(kept, received, keep, send)
    out[...] = other[...]


def add_last(kept, received, out):
    out[...] = (kept[...].astype(WIDE) + received[...].astype(WIDE)).astype(LOW)


def add_beside(other, kept, received, out):
    half = kept.shape[0]
    out[:half] = other[...]
    add_last(kept, received, out.at[half:])


def stack_halves(own, near, far, farthest, first, second):
    half = first.shape[1]
    for s, block in enumerate((own, near, far, farthest)):
        first[s] = block[:half]
        second[s] = block[half:]


def unpack_mlp(outer_own, inner_own, outer_other, inner_other, outer, inner, done, stage):
    core, _, _, chip, _ = places()
    half, width = outer_own.shape[1:]
    part = 2 * half
    for s in range(CHIPS):
        for m, (one, two) in enumerate(((outer_own, inner_own), (outer_other, inner_other))):
            far, c = chip ^ s, core ^ m
            outer[rows_from((2 * far + c) * half, half)] = one[s].astype(WIDE)
            stage[c, far] = two[s]
    for c in range(2):
        for p in range(CHIPS):
            for k in range(4):
                start = k * width + p * part
                inner[c * half : (c + 1) * half, start : start + part] = stage[
                    c, p, :, k * part : (k + 1) * part
                ].astype(WIDE)
    done[...] = jnp.zeros(done.shape, WIDE)


def unpack_rest(*refs):
    pieces, mats, vectors, (b_query, b_value, b_inner, stage, small) = (
        refs[:2],
        refs[2:6],
        refs[6:12],
        refs[12:],
    )
    core, _, _, chip, place = places()
    part = mats[0].shape[0]
    half = part // 2
    for s in range(CHIPS):
        for m, blocks in enumerate(pieces):
            stage[core ^ m, s] = blocks[s, :half]
        small[s] = pieces[0][s, half:, :part].astype(WIDE)
    for c in range(2):
        for k in range(CHIPS):
            for j, out in enumerate(mats):
                out[c * half : (c + 1) * half, k * part : (k + 1) * part] = stage[
                    c, k, :, j * part : (j + 1) * part
                ].astype(WIDE)
    total = small[0] + small[1] + small[2] + small[3]
    for i, out in enumerate(vectors):
        out[...] = total[i]
    biases = small[place]
    b_query[...] = biases[7]
    b_value[...] = biases[8]
    for p in range(CHIPS):
        b_inner[p * part : (p + 1) * part] = small[p][6]


def per_device(
    inputs,
    segments,
    query_weight,
    query_bias,
    key_weight,
    value_weight,
    value_bias,
    output_weight,
    output_bias,
    first_gain,
    first_shift,
    inner_weight,
    inner_bias,
    outer_weight,
    outer_bias,
    second_gain,
    second_shift,
    cotangent,
):
    groups = lax.axis_size("ctx") // TEAM
    lines = [[m + TEAM * g for g in range(groups)] for m in range(TEAM)]
    tokens, width = inputs.shape[1:]
    part = query_weight.shape[0]
    hidden = outer_weight.shape[0]
    count, half = CHIPS * tokens, part // 2
    heads = part // HEAD_DIM
    head = 3 * half // 4 + 8

    def chips(block):
        return [partner(block, "ctx", s << 1) for s in (1, 2, 3)]

    def exchanged(blocks):
        return [partner(block, "ctx", (s + 1) << 1) for s, block in enumerate(blocks)]

    def joined(block):
        return partner(block, "ctx", CORE)

    (own,) = kernel(
        prepare_tokens,
        [shape((tokens + 16, width))],
        inputs,
        segments,
        scratch=[pltpu.VMEM((1, tokens), jnp.int32)],
        loads=2,
    )
    teams = [[c + TEAM * g + 2 * n for n in range(CHIPS)] for g in range(groups) for c in range(2)]
    seen = lax.all_gather(own, "ctx", axis_index_groups=teams)
    (first,) = kernel(
        prepare_weights,
        [shape((head + 3 * half, width))],
        query_weight,
        key_weight,
        value_weight,
        output_weight,
        inner_weight,
        outer_weight,
        output_bias,
        first_gain,
        first_shift,
        outer_bias,
        second_gain,
        second_shift,
        inner_bias,
        query_bias,
        value_bias,
        scratch=[
            pltpu.VMEM((3, half, width), LOW),
            pltpu.VMEM((half, 4 * width), LOW),
            *[pltpu.VMEM((part,), LOW)] * 6,
            pltpu.VMEM((hidden,), LOW),
            *[pltpu.VMEM((part,), LOW)] * 2,
        ],
        loads=15,
    )
    (mine,) = kernel(first_rows, [shape((head, width))], first, after=(seen,))
    line = [first, partner(first, "fsdp", 1), partner(first, "fsdp", 2), partner(mine, "fsdp", 3)]
    projections, others, sent = kernel(
        sort_pieces,
        [shape((4, head, width)), shape((3, 3 * half, width)), shape((3 * half, width))],
        *line,
    )
    last = partner(sent, "fsdp", 1)

    rows_in, w_qkv, queries, kv_own, segs, vec, b_inner = kernel(
        project,
        [
            shape((count, width)),
            shape((width, 3 * part)),
            shape((count, part)),
            shape((count, 2 * part)),
            shape((8, tokens), WIDE),
            shape((8, width), WIDE),
            shape((1, width), WIDE),
        ],
        seen,
        projections,
        joined(projections),
        scratch=[pltpu.VMEM((4, 16, part), WIDE)],
    )
    kv_far, seg_far = partner(kv_own, "ctx", CORE), partner(segs, "ctx", CORE)
    if groups == 1:
        context, probs = kernel(
            attend_all,
            [shape((tokens, width)), shape((heads, 2 * count, count))],
            queries,
            kv_own,
            kv_far,
            segs,
            seg_far,
            scratch=[
                pltpu.VMEM((2 * count, 2 * part), LOW),
                pltpu.VMEM((2 * CHIPS, tokens), WIDE),
                pltpu.VMEM((1, count), WIDE),
                pltpu.VMEM((count, part), LOW),
            ],
            room=24,
        )
    else:
        kv = jnp.concatenate([kv_own, kv_far])
        seg_key = jnp.concatenate([segs[:CHIPS], seg_far[:CHIPS]])
        kv = lax.all_gather(kv, "ctx", axis=0, tiled=True, axis_index_groups=lines)
        seg_key = lax.all_gather(seg_key, "ctx", axis=0, tiled=True, axis_index_groups=lines)
        rows, probs = attention(queries, segs[:CHIPS].reshape(1, count), kv, seg_key)
        (context,) = kernel(beside, [shape((tokens, width))], rows)

    contexts = [context] + chips(context)
    last = kernel(
        split_rows, [shape((half, width))] * 3, last, after=(context,)
    )
    w_output, w_inner, w_outer = kernel(
        assemble, [shape((width, width))] * 3, others, *last, joined(others), *map(joined, last)
    )
    context_low, unit_one, inverse_one, normed_low, activated, slope, *outer_sent = kernel(
        forward,
        [
            shape((count, width)),
            shape((tokens, width), WIDE),
            shape((tokens, 1), WIDE),
            shape((count, width)),
            shape((count, width)),
            shape((count, width), WIDE),
            shape((tokens, width), WIDE),
        ]
        + [shape((tokens, width))] * 3,
        *contexts,
        rows_in,
        w_output,
        vec,
        w_inner,
        b_inner,
        w_outer,
        scratch=[pltpu.VMEM((CHIPS, count, part), LOW)],
        room=16,
    )
    result, grad_summed, grad_outer, sums_one = kernel(
        backward_first,
        [
            shape((1, tokens, width)),
            shape((tokens, width), WIDE),
            shape((tokens, width)),
            shape((8, width), WIDE),
        ],
        outer_sent[0],
        *exchanged(outer_sent[1:]),
        unit_one,
        vec,
        cotangent,
        last=(0,),
    )
    grads_outer = [grad_outer] + chips(grad_outer)
    outer_kept, outer_sent = kernel(
        outer_grads,
        [shape((4, half, width))] * 2,
        activated,
        *grads_outer,
        scratch=[pltpu.VMEM((width, width), LOW)],
    )
    grad_inner, sums_inner, inner_own, *inner_sent = kernel(
        backward_second,
        [shape((count, width)), shape((1, width), WIDE), shape((tokens, width), WIDE)]
        + [shape((tokens, width))] * 3,
        *grads_outer,
        slope,
        w_outer,
        w_inner,
        room=12,
    )
    inner_far = exchanged(inner_sent)

    def near_sum(kept, sent):
        received = partner(sent, "ctx", CORE)
        return kernel(add_near, [shape((2,) + kept.shape[1:])] * 2, kept, received)

    def far_sum(kept, sent, after=()):
        received = partner(sent, "fsdp", 1)
        return kernel(add_far, [shape(kept.shape[1:])] * 2, kept, received, after=after)

    def last_sum(kept, sent, after=()):
        received = partner(sent, "fsdp", 2)
        (total,) = kernel(add_last, [shape(kept.shape)], kept, received, after=after)
        if groups > 1:
            total = lax.psum(total.astype(WIDE), "ctx", axis_index_groups=lines).astype(LOW)
        return total

    inner_kept, *inner_sent = kernel(
        inner_grads,
        [shape((4, half, width))] + [shape((half, width))] * 4,
        normed_low,
        grad_inner,
        scratch=[pltpu.VMEM((width, width), LOW)],
    )
    inner_kept, inner_sent = kernel(
        add_near_parts,
        [shape((2, half, width))] * 2,
        inner_kept,
        *(partner(block, "ctx", CORE) for block in inner_sent),
    )
    outer_kept, outer_sent = near_sum(outer_kept, outer_sent)
    outer_kept, outer_sent, inner_sent = kernel(
        add_far_passing,
        [shape((half, width))] * 2 + [shape((2, half, width))],
        outer_kept,
        partner(outer_sent, "fsdp", 1),
        inner_sent,
    )
    inner_far_sum = far_sum(inner_kept, inner_sent)
    outer_total = last_sum(outer_kept, outer_sent)
    grad_residual, grad_low, sums_two = kernel(
        norm_backward,
        [shape((tokens, width), WIDE), shape((tokens, width)), shape((8, width), WIDE)],
        grad_summed,
        inner_own,
        *inner_far,
        unit_one,
        inverse_one,
        vec,
    )
    grads_low = [grad_low] + chips(grad_low)
    if groups == 1:
        grad_low, grad_queries, grad_kv, *grad_kv_sent = kernel(
            attend_back_all,
            [
                shape((count, width)),
                shape((count, part)),
                shape((count, 2 * part), WIDE),
            ]
            + [shape((tokens, 2 * part))] * CHIPS,
            queries,
            kv_own,
            kv_far,
            *grads_low,
            w_output,
            probs,
            scratch=[
                pltpu.VMEM((2 * count, 2 * part), LOW),
                pltpu.VMEM((count, part), LOW),
                pltpu.VMEM((2 * count, 2 * part), WIDE),
            ],
            room=24,
            after=(outer_kept,),
        )
    else:
        grad_low, grad_context = kernel(
            context_back, [shape((count, width)), shape((count, part))], *grads_low, w_output
        )
        grad_queries, grad_kv = attention_back(queries, kv, grad_context, probs)
        grad_kv = grad_kv.reshape(groups, 2, count, 2 * part).transpose(1, 0, 2, 3)
        grad_kv = lax.psum_scatter(
            grad_kv.reshape(2, groups * count, 2 * part),
            "ctx",
            scatter_dimension=1,
            tiled=True,
            axis_index_groups=lines,
        )
        grad_kv, grad_kv_sent = grad_kv[0], jnp.split(grad_kv[1].astype(LOW), CHIPS)
    grad_kv_far = [joined(block) for block in grad_kv_sent]
    (grad_o,) = kernel(output_grads, [shape((width, part))], context_low, grad_low)
    cut = shape((4, half + 16, width))
    grad_qkv, rest_kept, rest_sent = kernel(
        projection_grads,
        [shape((count, 3 * part)), cut, cut],
        rows_in,
        grad_queries,
        grad_kv,
        *grad_kv_far,
        grad_o,
        sums_one,
        sums_two,
        sums_inner,
        scratch=[pltpu.VMEM((width, width), LOW)],
        after=(outer_total, inner_far_sum[0]),
    )
    rest_near = near_sum(rest_kept, rest_sent)
    input_own, *input_sent = kernel(
        input_grads,
        [shape((tokens, width), WIDE)] + [shape((tokens, width))] * 3,
        grad_qkv,
        w_qkv,
        grad_residual,
        after=tuple(rest_near),
    )
    input_far = exchanged(input_sent)

    rest_far = far_sum(*rest_near)
    (mlp_total,) = kernel(
        add_beside,
        [shape((2 * half, width))],
        outer_total,
        inner_far_sum[0],
        partner(inner_far_sum[1], "fsdp", 2),
        after=(*input_far, rest_far[0]),
    )
    rest_total = last_sum(*rest_far)
    rest_all = lax.all_gather(rest_total, "ctx", axis_index_groups=teams)
    mlp_blocks = kernel(
        stack_halves,
        [shape((CHIPS, half, width))] * 2,
        mlp_total,
        *chips(mlp_total),
        after=(rest_all,),
    )
    grad_input, done_input = kernel(
        add_tokens,
        [shape((1, tokens, width)), shape((8, 128), WIDE)],
        input_own,
        *input_far,
        last=(0,),
        after=(rest_total,),
    )
    g_outer, g_inner, done_mlp = kernel(
        unpack_mlp,
        [
            shape((hidden, width), WIDE),
            shape((part, 4 * hidden), WIDE),
            shape((8, 128), WIDE),
        ],
        *mlp_blocks,
        *map(joined, mlp_blocks),
        last=(0, 1),
        scratch=[pltpu.VMEM((2, CHIPS, half, width), LOW)],
        room=12,
        after=(rest_all,),
    )
    g_query, g_key, g_value, g_output, *vec, g_b_query, g_b_value, g_b_inner = kernel(
        unpack_rest,
        [shape((part, width), WIDE)] * 4
        + [shape((part,), WIDE)] * 8
        + [shape((width,), WIDE)],
        rest_all,
        joined(rest_all),
        last=range(13),
        scratch=[
            pltpu.VMEM((2, CHIPS, half, width), LOW),
            pltpu.VMEM((CHIPS, 16, part), WIDE),
        ],
        room=12,
    )
    return (
        result,
        grad_input,
        g_query,
        g_b_query,
        g_key,
        g_value,
        g_b_value,
        g_output,
        vec[3],
        vec[4],
        vec[5],
        g_inner,
        g_b_inner,
        g_outer,
        vec[0],
        vec[1],
        vec[2],
    )


def solution(mesh):
    rows, cuts, whole = P("fsdp", "ctx", None), P("fsdp", None), P("fsdp")
    params = (cuts, whole, cuts, cuts, whole, cuts, whole, whole, whole)
    params += (cuts, whole, cuts, whole, whole, whole)
    return jax.shard_map(
        per_device,
        mesh=mesh,
        in_specs=(rows, P("fsdp", "ctx")) + params + (rows,),
        out_specs=(rows, rows) + params,
        check_vma=False,
    )
```
